32 devices in a mesh: dp: 8 (over y, x, core), ctx: 4 (over z).
Axes of the slice: x: 2, y: 2, z: 4, core: 2. Of those that a mesh axis runs over, the one named last changes fastest.
Arguments:
- tokens: bfloat16 [8, 1536, 1024], P('dp', 'ctx'), may hold values from -6 to 6
- doc_starts: int32 [8, 4], P('dp'), may hold values from 0 to 1535, as said below
- attn_gain: bfloat16 [1024], P('dp'), may hold values from 0.5 to 1.5
- w_query: bfloat16 [1024, 2048], P('dp'), may hold values from -0.1875 to 0.1875
- w_key: bfloat16 [1024, 1024], P('dp'), may hold values from -0.1875 to 0.1875
- w_value: bfloat16 [1024, 1024], P('dp'), may hold values from -0.1875 to 0.1875
- w_out: bfloat16 [2048, 1024], P('dp'), may hold values from -0.75 to 0.75
- query_gain: bfloat16 [128], replicated, may hold values from 0.796875 to 2
- key_gain: bfloat16 [128], replicated, may hold values from 0.796875 to 2
- mlp_gain: bfloat16 [1024], P('dp'), may hold values from 0.5 to 1.5
- w_gate: bfloat16 [1024, 3072], P('dp'), may hold values from -0.1875 to 0.1875
- w_up: bfloat16 [1024, 3072], P('dp'), may hold values from -0.1875 to 0.1875
- w_down: bfloat16 [3072, 1024], P('dp'), may hold values from -0.109375 to 0.109375
- cotangent: bfloat16 [8, 1536, 1024], P('dp', 'ctx'), may hold values from -6 to 6
Outputs:
- output: bfloat16 [8, 1536, 1024], P('dp', 'ctx')
- input_grad: bfloat16 [8, 1536, 1024], P('dp', 'ctx')
- attn_gain_grad: float32 [1024], P('dp')
- w_query_grad: float32 [1024, 2048], P('dp')
- w_key_grad: float32 [1024, 1024], P('dp')
- w_value_grad: float32 [1024, 1024], P('dp')
- w_out_grad: float32 [2048, 1024], P('dp')
- query_gain_grad: float32 [128], replicated
- key_gain_grad: float32 [128], replicated
- mlp_gain_grad: float32 [1024], P('dp')
- w_gate_grad: float32 [1024, 3072], P('dp')
- w_up_grad: float32 [1024, 3072], P('dp')
- w_down_grad: float32 [3072, 1024], P('dp')
The draws below stay inside these ranges and needn't reach their ends.
Inputs may be any that keep to these rules, and one draw needn't show every extreme that they name: `doc_starts`: row b holds the first stream positions of the 4 documents of pack b: it begins with 0 and rises strictly.
All inputs are finite; a program needn't handle non-finite values.
Results may differ from the reference program's by a relative error of at most 0.02.
Values may be sent and summed in bfloat16 or wider, within the bound.
No kernel may reach another device: no remote copies, remote signals or barrier semaphores. Data moves between devices by JAX's collectives and lax.ppermute only.
A program may use at most 192 MiB of HBM per device.

```python
import math
import jax
import jax.numpy as jnp
from jax import lax

D = 1024
HEADS = 16
KV_HEADS = 8
HEAD_DIM = 128
FF = 3072
STRETCH = 192
BATCH = 8
SEQ = 1536
N_CTX = 4


def draw_doc_starts(key, part):
    key = jax.random.fold_in(key, 17)

    def one_row(row_key):
        first_key, second_key, third_key = jax.random.split(row_key, 3)
        opening = jax.random.randint(first_key, (), 1, STRETCH // 2)
        lowest = (N_CTX + 1) * STRETCH
        longest = SEQ - opening - STRETCH // 2
        spanning = jax.random.randint(second_key, (), lowest, longest)
        remain = SEQ - opening - spanning
        closing = jax.random.randint(third_key, (), 1, remain)
        return jnp.stack([jnp.zeros((), jnp.int32), opening, opening + spanning, opening + spanning + closing]).astype(jnp.int32)
    return jax.vmap(one_row)(jax.random.split(key, BATCH))


def raised(array, stream_key, source, target, parts, factor):
    owner, partner = [(jnp.arange(array.shape[dim]) // (array.shape[dim] // parts)).reshape([-1 if axis == dim else 1 for axis in range(array.ndim)]) for dim in (source, target)]
    chosen = jax.random.permutation(stream_key, parts)[partner]
    strong = (owner == chosen) | (owner == (partner + parts // 2) % parts)
    return jnp.where(strong, factor * array, array)


def level_of(rng, shape, cuts, smallest, high):
    level = 1.0
    for axis_at, parts in cuts:
        draws = jax.random.uniform(jax.random.fold_in(jax.random.fold_in(rng, 6), axis_at), (parts,), jnp.float32, smallest / len(cuts), high / len(cuts))
        level = level * jnp.repeat(jnp.exp(draws), shape[axis_at] // parts).reshape((-1,) + (1,) * (len(shape) - 1 - axis_at))
    return level


def normal_values(rng, extent, deviation, bound, shards=(), held_as=jnp.bfloat16):
    loudness = level_of(rng, extent, shards, -0.22, 0.18) if shards else 1.0
    values = jax.random.normal(rng, extent, jnp.float32) * deviation * loudness
    return jnp.minimum(jnp.maximum(values, -bound), bound).astype(held_as)


def heavy_noise(own_key, dims, spread, bound, cuts, heavy, kind=jnp.bfloat16):
    entries = spread * jax.random.normal(own_key, dims, jnp.float32)
    if cuts:
        entries = entries * level_of(own_key, dims, cuts, -0.22, 0.18)
    return jnp.clip(raised(entries, jax.random.fold_in(own_key, 3), *heavy), -bound, bound).astype(kind)


def setup_inputs(seed: int = 0) -> dict:
    streams_of = jax.random.split(jax.random.key(seed), 15)
    tokens = heavy_noise(streams_of[0], (BATCH, SEQ, D), 1.0, 6.0, ((0, 8), (1, 4)), (0, 2, 8, 2.0))
    doc_starts = draw_doc_starts(jax.random.fold_in(streams_of[14], 71), 0)
    attn_gain = jnp.clip(0.5 + 1.0 * jax.random.uniform(streams_of[2], (D,), jnp.float32) ** level_of(streams_of[2], (D,), ((0, 8),), -0.2, 0.2), 0.5, 1.5).astype(jnp.bfloat16)
    w_query = normal_values(streams_of[3], (D, HEADS * HEAD_DIM), D ** -0.5, 0.1875, ((0, 8),))
    w_key = normal_values(streams_of[4], (D, KV_HEADS * HEAD_DIM), D ** -0.5, 0.1875, ((0, 8),))
    w_value = normal_values(streams_of[5], (D, KV_HEADS * HEAD_DIM), D ** -0.5, 0.1875, ((0, 8),))
    w_out = normal_values(streams_of[6], (HEADS * HEAD_DIM, D), 64 ** -0.5, 0.75, ((0, 8),))
    query_gain = jnp.clip(jax.random.uniform(streams_of[7], (HEAD_DIM,), jnp.float32, 0.796875, 2.0), 0.796875, 2.0).astype(jnp.bfloat16)
    key_gain = jnp.clip(jax.random.uniform(streams_of[8], (HEAD_DIM,), jnp.float32, 0.796875, 2.0), 0.796875, 2.0).astype(jnp.bfloat16)
    mlp_gain = jnp.clip(0.5 + 1.0 * jax.random.uniform(streams_of[9], (D,), jnp.float32) ** level_of(streams_of[9], (D,), ((0, 8),), -0.2, 0.2), 0.5, 1.5).astype(jnp.bfloat16)
    w_gate = normal_values(streams_of[10], (D, FF), D ** -0.5, 0.1875, ((0, 8),))
    w_up = normal_values(streams_of[11], (D, FF), D ** -0.5, 0.1875, ((0, 8),))
    w_down = normal_values(streams_of[12], (FF, D), FF ** -0.5, 0.109375, ((0, 8),))
    cotangent = normal_values(streams_of[13], (BATCH, SEQ, D), 1.0, 6.0, ((0, 8), (1, 4)))
    return dict(tokens=tokens, doc_starts=doc_starts, attn_gain=attn_gain, w_query=w_query, w_key=w_key, w_value=w_value, w_out=w_out, query_gain=query_gain, key_gain=key_gain, mlp_gain=mlp_gain, w_gate=w_gate, w_up=w_up, w_down=w_down, cotangent=cotangent)


EPSILON = 1e-06
ROPE_BASE = 1000000.0
MASKED = -1e+30
HIGHEST = lax.Precision.HIGHEST

@jax.custom_vjp
def low(v):
    return lax.optimization_barrier(v.astype(jnp.bfloat16)).astype(jnp.float32)

@jax.custom_vjp
def low_back(v):
    return v

def low_keep(v):
    return (low(v), None)

def low_pass(kept, grad):
    return (grad,)

def back_keep(v):
    return (v, None)

def back_low(kept, grad):
    return (low(grad),)
low.defvjp(low_keep, low_pass)
low_back.defvjp(back_keep, back_low)

def stream_index(row_ids):
    slab_index = row_ids // (2 * STRETCH)
    within = row_ids % (2 * STRETCH)
    mirrored = (2 * N_CTX - 1 - slab_index) * STRETCH + within - STRETCH
    return jnp.where(within < STRETCH, slab_index * STRETCH + within, mirrored).astype(jnp.int32)

def doc_place(stream, starts):
    started = (starts[None, :] <= stream[:, None]).astype(jnp.int32)
    doc_ids = lax.optimization_barrier(jnp.sum(started, axis=1)).astype(jnp.int32) - 1
    chosen = (doc_ids[:, None] == jnp.arange(starts.shape[0], dtype=jnp.int32)[None, :]).astype(jnp.int32)
    opening = lax.optimization_barrier(jnp.sum(chosen * starts[None, :], axis=1)).astype(jnp.int32)
    return (doc_ids, (stream - opening).astype(jnp.int32))

def rotary(positions):
    half_dim = HEAD_DIM // 2
    inverse = jnp.exp(jnp.arange(half_dim, dtype=jnp.float32) * (-2.0 * math.log(ROPE_BASE) / HEAD_DIM))
    angles = positions.astype(jnp.float32)[:, None] * inverse[None, :]
    angles = jnp.concatenate([angles, angles], axis=1)
    return (jnp.cos(angles), jnp.sin(angles))

def rms_norm(values, gain):
    return values * lax.rsqrt(lax.optimization_barrier(jnp.mean(values * values, axis=-1, keepdims=True)) + EPSILON) * gain

def rotate(values, cos_table, sin_table):
    half_dim = values.shape[-1] // 2
    turned = jnp.concatenate([-values[..., half_dim:], values[..., :half_dim]], axis=-1)
    return values * cos_table + turned * sin_table

def attend_block(queries, query_doc, query_stream, keys_low, values_low, key_doc, key_stream):
    scores = jnp.einsum('tgjd,kgd->gjtk', queries, keys_low, precision=HIGHEST) * HEAD_DIM ** (-0.5)
    scores = low_back(scores)
    allowed = (query_doc[:, None] == key_doc[None, :]) & (key_stream[None, :] <= query_stream[:, None])
    scores = jnp.where(allowed, scores, MASKED)
    weights = low(jax.nn.softmax(scores, axis=-1))
    return jnp.einsum('gjtk,kgd->tgjd', weights, values_low, precision=HIGHEST)

def pack_forward(pack_in, weights, doc_ids, stream, cos_table, sin_table):
    attn_gain, w_query, w_key, w_value, w_out, query_gain, key_gain, mlp_gain, w_gate, w_up, w_down = weights
    pack_rows = pack_in.shape[0]
    groups_per = HEADS // KV_HEADS
    cos_heads = cos_table[:, None, :]
    sin_heads = sin_table[:, None, :]
    normed = low(rms_norm(pack_in, attn_gain))
    query_raw = low_back(jnp.dot(normed, w_query, precision=HIGHEST))
    key_raw = low_back(jnp.dot(normed, w_key, precision=HIGHEST))
    value_raw = low_back(jnp.dot(normed, w_value, precision=HIGHEST))
    queries = low(rotate(rms_norm(query_raw.reshape(pack_rows, HEADS, HEAD_DIM), query_gain), cos_heads, sin_heads))
    keys_low = low(rotate(rms_norm(key_raw.reshape(pack_rows, KV_HEADS, HEAD_DIM), key_gain), cos_heads, sin_heads))
    values_low = low(value_raw).reshape(pack_rows, KV_HEADS, HEAD_DIM)
    block_rows = min(pack_rows, 512)
    num_blocks = pack_rows // block_rows
    attend = jax.checkpoint(attend_block)

    def one_block(element):
        return attend(element[0], element[1], element[2], keys_low, values_low, doc_ids, stream)
    attended = lax.map(one_block, (queries.reshape(num_blocks, block_rows, KV_HEADS, groups_per, HEAD_DIM), doc_ids.reshape(num_blocks, block_rows), stream.reshape(num_blocks, block_rows)))
    mixed_out = low(low_back(attended.reshape(pack_rows, HEADS * HEAD_DIM)))
    branch = low_back(jnp.dot(mixed_out, w_out, precision=HIGHEST))
    middle = pack_in + branch
    normed_mid = low(rms_norm(middle, mlp_gain))
    gate_proj = low_back(jnp.dot(normed_mid, w_gate, precision=HIGHEST))
    up_proj = low_back(jnp.dot(normed_mid, w_up, precision=HIGHEST))
    hidden = low(jax.nn.silu(gate_proj) * up_proj)
    return middle + jnp.dot(hidden, w_down, precision=HIGHEST)

def reference(tokens, doc_starts, attn_gain, w_query, w_key, w_value, w_out, query_gain, key_gain, mlp_gain, w_gate, w_up, w_down, cotangent):
    params = tuple((weight.astype(jnp.float32) for weight in (attn_gain, w_query, w_key, w_value, w_out, query_gain, key_gain, mlp_gain, w_gate, w_up, w_down)))
    stream = stream_index(jnp.arange(SEQ, dtype=jnp.int32))

    def one_pack(running, element):
        pack_in, pack_grad, starts = element
        doc_ids, positions = doc_place(stream, starts)
        cos_table, sin_table = rotary(positions)

        def forward(inputs_f, *weights):
            return pack_forward(inputs_f, weights, doc_ids, stream, cos_table, sin_table)
        result, pullback = jax.vjp(forward, pack_in.astype(jnp.float32), *params)
        gradients = pullback(pack_grad.astype(jnp.float32))
        running = tuple((earlier + update for earlier, update in zip(running, gradients[1:])))
        return (running, (result.astype(jnp.bfloat16), gradients[0].astype(jnp.bfloat16)))
    start_sums = tuple((jnp.zeros(weight.shape, jnp.float32) for weight in params))
    totals, (outputs, input_grads) = lax.scan(one_pack, start_sums, (tokens, cotangent, doc_starts))
    attn_gain_grad, w_query_grad, w_key_grad, w_value_grad, w_out_grad, query_gain_grad, key_gain_grad, mlp_gain_grad, w_gate_grad, w_up_grad, w_down_grad = totals
    return (outputs, input_grads, attn_gain_grad, w_query_grad, w_key_grad, w_value_grad, w_out_grad, query_gain_grad, key_gain_grad, mlp_gain_grad, w_gate_grad, w_up_grad, w_down_grad)
```

```python
import functools
import math

import jax
import jax.numpy as jnp
from jax import lax
from jax.experimental import pallas as pl
from jax.experimental.pallas import tpu as pltpu
from jax.sharding import PartitionSpec as P

HEADS = 16
KV_HEADS = 8
HEAD_DIM = 128
GROUPS = HEADS // KV_HEADS

EPSILON = 1e-06
ROPE_BASE = 1000000.0
MASKED = -1e30
SCALE = HEAD_DIM ** (-0.5)

F32 = jnp.float32
BF16 = jnp.bfloat16
MIB = 1 << 20
VMEM_MIB = 32
LARGE = 1 << 18


ORDER = []


def shape(dims, dtype):
    return jax.ShapeDtypeStruct(dims, dtype)


ANY = pl.BlockSpec(memory_space=pl.ANY)
IN_VMEM = pl.BlockSpec(memory_space=pltpu.VMEM)


def in_hbm(spec, array):
    return spec is not IN_VMEM and spec is not ANY and math.prod(array.shape) * 2 >= LARGE


def call(
    name, body, args, in_specs, out_specs, out_shape, grid=(1,), scratch=(), prefetch=(), aliases=None,
    after=(),
):
    waits = list(ORDER) + list(after)
    taken = len(prefetch) + len(args)
    args = [
        pltpu.with_memory_space_constraint(a, pltpu.HBM) if in_hbm(s, a) else a
        for a, s in zip(args, in_specs)
    ]
    out_shape = [
        pltpu.HBM(o.shape, o.dtype) if in_hbm(s, o) else o for o, s in zip(out_shape, out_specs)
    ]

    def without(*refs):
        body(*refs[:taken], *refs[taken + len(waits) :])

    results = pl.pallas_call(
        without,
        grid_spec=pltpu.PrefetchScalarGridSpec(
            num_scalar_prefetch=len(prefetch),
            grid=grid,
            in_specs=list(in_specs) + [pl.BlockSpec(memory_space=pl.ANY)] * len(waits),
            out_specs=out_specs,
            scratch_shapes=list(scratch),
        ),
        out_shape=out_shape,
        input_output_aliases={len(prefetch) + i: o for i, o in (aliases or {}).items()},
        compiler_params=pltpu.CompilerParams(vmem_limit_bytes=VMEM_MIB * MIB),
        cost_estimate=pl.CostEstimate(flops=0, bytes_accessed=0, transcendentals=0),
        name=name,
    )(*prefetch, *args, *waits)
    ORDER[:] = [min(results, key=lambda r: r.size)]
    return results


def whole(dims):
    return pl.BlockSpec(dims, lambda *_: (0,) * len(dims))


def mm(a, b):
    return lax.dot_general(a, b, (((1,), (0,)), ((), ())), preferred_element_type=F32)


def mm_nt(a, b):
    return lax.dot_general(a, b, (((1,), (1,)), ((), ())), preferred_element_type=F32)


def mm_tn(a, b):
    return lax.dot_general(a, b, (((0,), (0,)), ((), ())), preferred_element_type=F32)


def mean_last(v):
    return jnp.sum(v, axis=-1, keepdims=True) * (1.0 / v.shape[-1])


def factor_of(v):
    return lax.rsqrt(mean_last(v * v) + EPSILON)


def norm_back(v, gain, incoming):
    f = factor_of(v)
    weighted = incoming * gain
    inner = mean_last(weighted * v)
    return f * weighted - v * (f * f * f * inner), incoming * v * f


def stream_index(row_ids, stretch_rows, ctx_size):
    slab_index = row_ids // (2 * stretch_rows)
    within = row_ids % (2 * stretch_rows)
    mirrored = (2 * ctx_size - 1 - slab_index) * stretch_rows + within - stretch_rows
    return jnp.where(within < stretch_rows, slab_index * stretch_rows + within, mirrored)


def opening_of(stream, starts):
    started = starts[None, :] <= stream[:, None]
    return jnp.max(jnp.where(started, starts[None, :], 0), axis=1)


def rotary(positions):
    half_dim = HEAD_DIM // 2
    inverse = jnp.exp(
        jnp.arange(half_dim, dtype=F32) * (-2.0 * math.log(ROPE_BASE) / HEAD_DIM)
    )
    angles = positions.astype(F32)[:, None] * inverse[None, :]
    cos_half, sin_half = jnp.cos(angles), jnp.sin(angles)
    return (
        jnp.concatenate([cos_half, cos_half], axis=1),
        jnp.concatenate([-sin_half, sin_half], axis=1),
    )


def copies(name, sources, plan, out_shape, prefetch=(), after=()):
    count = len(sources)
    first = len(prefetch)

    def body(*refs):
        ins = refs[first : first + count]
        for source, target in plan(refs[:first], ins, refs[first + count :]):
            target[...] = source[...]

    return call(
        name, body, sources, [IN_VMEM] * count, [IN_VMEM] * len(out_shape), out_shape,
        prefetch=prefetch, after=after,
    )


def touch(after):
    def body(out_ref):
        out_ref[...] = jnp.zeros_like(out_ref)

    call("touch", body, [], [], [IN_VMEM], [shape((8, HEAD_DIM), F32)], after=after)


def norm_own(tokens, gain):
    def body(t_ref, g_ref, out_ref):
        x = t_ref[...].astype(F32)
        out_ref[...] = (x * factor_of(x) * g_ref[...]).astype(BF16)

    return call(
        "norm_own", body, [tokens, gain], [IN_VMEM] * 2, [IN_VMEM], [shape(tokens.shape, BF16)]
    )[0]


def norm_pack(own, from_left, from_right, gain, places, ctx_at):
    count = len(from_left) + 1
    rows, width = own.shape
    half = rows // 2

    def body(places_ref, at_ref, gain_ref, *refs):
        blocks, pack_ref = refs[:-1], refs[-1]
        step = pl.program_id(0)
        me = at_ref[0]

        def write(ref):
            x = ref[...].astype(F32)
            low = (x * factor_of(x) * gain_ref[...]).astype(BF16)
            pack_ref[...] = low.reshape(2, 1, half, width)

        @pl.when(step == 0)
        def _():
            write(blocks[0])

        for s in range(1, count):

            @pl.when((step == s) & (me >= s))
            def _():
                write(blocks[s])

            @pl.when((step == s) & (me < s))
            def _():
                write(blocks[count - 1 + count - s])

    blocks = [own] + from_left + from_right
    return call(
        "norm_pack", body, [gain] + blocks,
        [whole((1, width))] + [IN_VMEM] * len(blocks),
        [pl.BlockSpec((2, 1, half, width), lambda k, at, me: (0, at[k], 0, 0))],
        [shape((2, count, half, width), BF16)],
        grid=(count,), prefetch=[places, ctx_at],
    )[0]


def head_norm_rope(raw, gain, cos, sin):
    normed = raw * factor_of(raw) * gain
    return normed * cos + pltpu.roll(normed, HEAD_DIM // 2, 1) * sin


def project_queries(x, weights, gain, cos, sin):
    rows, width = x.shape
    step_cols = 2 * HEAD_DIM
    cols = HEADS * HEAD_DIM

    def body(x_ref, w_ref, g_ref, c_ref, s_ref, raw_ref, rot_ref):
        raw = mm(x_ref[...], w_ref[...])
        raw_ref[...] = raw
        for h in range(2):
            part = raw[:, h * HEAD_DIM : (h + 1) * HEAD_DIM]
            turned = head_norm_rope(part, g_ref[...], c_ref[...], s_ref[...])
            rot_ref[:, h * HEAD_DIM : (h + 1) * HEAD_DIM] = turned.astype(BF16)

    col = pl.BlockSpec((rows, step_cols), lambda j: (0, j))
    return call(
        "project_queries", body, [x, weights, gain, cos, sin],
        [
            whole((rows, width)),
            pl.BlockSpec((width, step_cols), lambda j: (0, j)),
            whole((1, HEAD_DIM)),
            whole((rows, HEAD_DIM)),
            whole((rows, HEAD_DIM)),
        ],
        [col, col],
        [shape((rows, cols), F32), shape((rows, cols), BF16)],
        grid=(cols // step_cols,),
    )


def project_keys_values(x, weights, gain, cos, sin):
    rows, width = x.shape
    step_cols = 2 * HEAD_DIM
    cols = KV_HEADS * HEAD_DIM
    key_at = HEADS * HEAD_DIM // step_cols
    value_at = key_at + cols // step_cols

    def body(x_ref, wk_ref, wv_ref, g_ref, c_ref, s_ref, raw_ref, rot_ref, val_ref):
        raw = mm(x_ref[...], wk_ref[...])
        raw_ref[...] = raw
        for h in range(2):
            part = raw[:, h * HEAD_DIM : (h + 1) * HEAD_DIM]
            turned = head_norm_rope(part, g_ref[...], c_ref[...], s_ref[...])
            rot_ref[:, h * HEAD_DIM : (h + 1) * HEAD_DIM] = turned.astype(BF16)
        val_ref[...] = mm(x_ref[...], wv_ref[...]).astype(BF16)

    col = pl.BlockSpec((rows, step_cols), lambda j: (0, j))
    return call(
        "project_keys_values", body, [x, weights, weights, gain, cos, sin],
        [
            whole((rows, width)),
            pl.BlockSpec((width, step_cols), lambda j: (0, key_at + j)),
            pl.BlockSpec((width, step_cols), lambda j: (0, value_at + j)),
            whole((1, HEAD_DIM)),
            whole((rows, HEAD_DIM)),
            whole((rows, HEAD_DIM)),
        ],
        [col, col, col],
        [shape((rows, cols), F32), shape((rows, cols), BF16), shape((rows, cols), BF16)],
        grid=(cols // step_cols,),
    )


def attend(queries, keys, values, q_low, q_high, k_stream):
    rows = queries.shape[0]
    half = rows // 2
    pack = keys.shape[0]
    pair = GROUPS * HEAD_DIM

    def body(q_ref, k_ref, v_ref, lo_ref, hi_ref, ks_ref, att_ref, mix_ref, lse_ref, bias):
        @pl.when(pl.program_id(0) == 0)
        def _():
            ks = ks_ref[...]
            ok = (ks >= lo_ref[...]) & (ks <= hi_ref[...])
            bias[...] = jnp.where(ok, 0.0, MASKED)

        for part in range(2):
            here = slice(part * half, (part + 1) * half)
            seen = pack // 2 if part == 0 else pack
            q2 = jnp.concatenate(
                [q_ref[here, j * HEAD_DIM : (j + 1) * HEAD_DIM] for j in range(GROUPS)], axis=0
            )
            scores = mm_nt(q2, k_ref[:seen, :]) * SCALE
            scores = (scores.reshape(GROUPS, half, seen) + bias[here, :seen][None]).reshape(
                GROUPS * half, seen
            )
            top = jnp.max(scores, axis=-1, keepdims=True)
            shifted = jnp.exp(scores - top)
            total = jnp.sum(shifted, axis=-1, keepdims=True)
            out = mm(shifted.astype(BF16), v_ref[:seen, :]) * (1.0 / total)
            for j in range(GROUPS):
                piece = out[j * half : (j + 1) * half]
                att_ref[here, j * HEAD_DIM : (j + 1) * HEAD_DIM] = piece
                mix_ref[here, j * HEAD_DIM : (j + 1) * HEAD_DIM] = piece.astype(BF16)
            lse = jnp.broadcast_to(top + jnp.log(total), (GROUPS * half, HEAD_DIM)).T
            lse_ref[0, :, part * GROUPS * half : (part + 1) * GROUPS * half] = lse[:8]

    col = pl.BlockSpec((rows, pair), lambda g: (0, g))
    key = pl.BlockSpec((pack, HEAD_DIM), lambda g: (0, g))
    return call(
        "attend", body, [queries, keys, values, q_low, q_high, k_stream],
        [col, key, key, whole((rows, 1)), whole((rows, 1)), whole((1, pack))],
        [col, col, pl.BlockSpec((1, 8, GROUPS * rows), lambda g: (g, 0, 0))],
        [
            shape((rows, HEADS * HEAD_DIM), F32),
            shape((rows, HEADS * HEAD_DIM), BF16),
            shape((KV_HEADS, 8, GROUPS * rows), F32),
        ],
        grid=(KV_HEADS,),
        scratch=[pltpu.VMEM((rows, pack), F32)],
    )


def project_out(mixed, stack, tokens, gain):
    rows, inner = mixed.shape
    count, _, width = stack.shape
    unit = width // count
    block = 256
    steps = width // block

    def body(m_ref, a_ref, b_ref, t_ref, g_ref, mid_ref, low_ref, acc):
        j = pl.program_id(0)
        w = jnp.concatenate([a_ref[...], b_ref[...]], axis=1).reshape(inner, block)
        acc[j] = t_ref[...].astype(F32) + mm(m_ref[...], w)

        @pl.when(j == steps - 1)
        def _():
            mid = jnp.concatenate([acc[i] for i in range(steps)], axis=1)
            mid_ref[...] = mid
            low_ref[...] = (mid * factor_of(mid) * g_ref[...]).astype(BF16)

    return call(
        "project_out", body, [mixed, stack, stack, tokens, gain],
        [
            whole((rows, inner)),
            pl.BlockSpec((count, unit, block), lambda j: (0, 9, j)),
            pl.BlockSpec((count, unit, block), lambda j: (0, 10, j)),
            pl.BlockSpec((rows, block), lambda j: (0, j)),
            whole((1, width)),
        ],
        [whole((rows, width)), whole((rows, width))],
        [shape((rows, width), F32), shape((rows, width), BF16)],
        grid=(steps,),
        scratch=[pltpu.VMEM((steps, rows, block), F32)],
    )


def gate_up(x, stack):
    rows, width = x.shape
    count = stack.shape[0]
    unit = width // count
    block = 256
    per = width // block
    hidden = 3 * width

    def body(x_ref, g_ref, u_ref, h_ref, dg_ref, du_ref):
        g = mm(x_ref[...], g_ref[...].reshape(width, block))
        u = mm(x_ref[...], u_ref[...].reshape(width, block))
        s = 1.0 / (1.0 + jnp.exp(-g))
        act = g * s
        h_ref[...] = (act * u).astype(BF16)
        dg_ref[...] = (u * s * (1.0 + g * (1.0 - s))).astype(BF16)
        du_ref[...] = act.astype(BF16)

    col = pl.BlockSpec((rows, block), lambda j: (0, j))
    return call(
        "gate_up", body, [x, stack, stack],
        [
            whole((rows, width)),
            pl.BlockSpec((count, unit, block), lambda j: (0, 3 + j // per, j % per)),
            pl.BlockSpec((count, unit, block), lambda j: (0, 6 + j // per, j % per)),
        ],
        [col, col, col],
        [shape((rows, hidden), BF16)] * 3,
        grid=(hidden // block,),
    )


def down_both(hidden, slope_gate, slope_up, grad, stack, middle):
    rows, inner = hidden.shape
    count, _, width = stack.shape
    unit = width // count
    block = 384
    per = block // (3 * unit)
    steps = inner // block

    def body(h_ref, sg_ref, su_ref, dy_ref, w_ref, mid_ref, out_ref, both_ref, acc):
        j = pl.program_id(0)
        w = w_ref[...].reshape(block, width)
        dh = mm_nt(dy_ref[...], w)
        both_ref[0] = (dh * sg_ref[...].astype(F32)).astype(BF16)
        both_ref[1] = (dh * su_ref[...].astype(F32)).astype(BF16)

        @pl.when(j == 0)
        def _():
            acc[...] = mid_ref[...]

        acc[...] += mm(h_ref[...], w)

        @pl.when(j == steps - 1)
        def _():
            out_ref[...] = acc[...].astype(BF16)

    col = pl.BlockSpec((rows, block), lambda j: (0, j))
    return call(
        "down_both", body, [hidden, slope_gate, slope_up, grad, stack, middle],
        [
            col,
            col,
            col,
            whole((rows, width)),
            pl.BlockSpec((per, 3 * unit, width), lambda j: (j, 0, 0)),
            whole((rows, width)),
        ],
        [whole((rows, width)), pl.BlockSpec((2, rows, block), lambda j: (0, 0, j))],
        [shape((rows, width), BF16), shape((2, rows, inner), BF16)],
        grid=(steps,),
        scratch=[pltpu.VMEM((rows, width), F32)],
    )


def mlp_back(d_both, stack, middle, gain, grad):
    _, rows, inner = d_both.shape
    count, _, width = stack.shape
    unit = width // count
    steps = inner // width

    def body(both_ref, g_ref, u_ref, mid_ref, gain_ref, dy_ref, gm_ref, gb_ref, gg_ref, acc):
        j = pl.program_id(0)
        part = mm_nt(both_ref[0], g_ref[...].reshape(width, width))
        part += mm_nt(both_ref[1], u_ref[...].reshape(width, width))

        @pl.when(j == 0)
        def _():
            acc[...] = part

        @pl.when(j > 0)
        def _():
            acc[...] += part

        @pl.when(j == steps - 1)
        def _():
            back, terms = norm_back(mid_ref[...], gain_ref[...], acc[...])
            total = dy_ref[...].astype(F32) + back
            gm_ref[...] = total
            gb_ref[...] = total.astype(BF16)
            gg_ref[...] = jnp.sum(terms, axis=0, keepdims=True)

    return call(
        "mlp_back", body, [d_both, stack, stack, middle, gain, grad],
        [
            pl.BlockSpec((2, rows, width), lambda j: (0, 0, j)),
            pl.BlockSpec((count, unit, width), lambda j: (0, 3 + j, 0)),
            pl.BlockSpec((count, unit, width), lambda j: (0, 6 + j, 0)),
            whole((rows, width)),
            whole((1, width)),
            whole((rows, width)),
        ],
        [whole((rows, width)), whole((rows, width)), whole((1, width))],
        [shape((rows, width), F32), shape((rows, width), BF16), shape((1, width), F32)],
        grid=(steps,),
        scratch=[pltpu.VMEM((rows, width), F32)],
    )


def mixed_back(grad_branch, stack):
    rows, width = grad_branch.shape
    count = stack.shape[0]
    unit = width // count
    block = 256
    per = block // (2 * unit)
    cols = HEADS * HEAD_DIM

    def body(gb_ref, a_ref, b_ref, out_ref):
        w = jnp.concatenate([a_ref[...], b_ref[...]], axis=1).reshape(block, width)
        out_ref[...] = mm_nt(gb_ref[...], w).astype(BF16)

    return call(
        "mixed_back", body, [grad_branch, stack, stack],
        [
            whole((rows, width)),
            pl.BlockSpec((per, unit, width), lambda j: (j, 9, 0)),
            pl.BlockSpec((per, unit, width), lambda j: (j, 10, 0)),
        ],
        [pl.BlockSpec((rows, block), lambda j: (0, j))],
        [shape((rows, cols), BF16)],
        grid=(cols // block,),
    )[0]


def attend_back(
    queries, grad_mixed, attended, keys, values, lse, q_low, q_high, k_stream,
    query_raw, key_raw, query_gain, key_gain, cos_own, sin_own, cos_pack, sin_pack,
    first_head, heads, earlier=(),
):
    rows = queries.shape[0]
    half = rows // 2
    pack = keys.shape[0]
    pair = GROUPS * HEAD_DIM
    wide = GROUPS * rows
    chunk = 256

    def stacked(ref):
        return jnp.concatenate(
            [
                ref[part * half : (part + 1) * half, j * HEAD_DIM : (j + 1) * HEAD_DIM]
                for part in range(2)
                for j in range(GROUPS)
            ],
            axis=0,
        )

    def unrotate(e, cos, sin):
        return e * cos - pltpu.roll(e, HEAD_DIM // 2, 1) * sin

    def body(
        q_ref, do_ref, att_ref, k_ref, v_ref, lse_ref, lo_ref, hi_ref, ks_ref,
        qr_ref, kr_ref, qg_ref, kg_ref, co_ref, so_ref, cp_ref, sp_ref,
        *rest,
    ):
        dq_ref, pair_ref, qgg_ref, kgg_ref, bias, dq_acc = rest[len(earlier) :]

        @pl.when(pl.program_id(0) == 0)
        def _():
            ks = ks_ref[...]
            ok = (ks >= lo_ref[...]) & (ks <= hi_ref[...])
            bias[...] = jnp.where(ok, 0.0, MASKED)
            qgg_ref[...] = jnp.zeros_like(qgg_ref)
            kgg_ref[...] = jnp.zeros_like(kgg_ref)

        q_all = stacked(q_ref)
        do_all = stacked(do_ref)
        delta = jnp.sum((do_all.astype(F32) * stacked(att_ref)).T, axis=0, keepdims=True)
        lse_row = lse_ref[0, 0:1, :]
        k_sum = jnp.zeros((1, HEAD_DIM), F32)
        for at in range(pack // chunk):
            here = slice(at * chunk, (at + 1) * chunk)
            first = 0 if at * chunk < pack // 2 else GROUPS * half
            kk, vv = k_ref[here, :], v_ref[here, :]
            qq, dd = q_all[first:], do_all[first:]
            scores = mm_nt(kk, qq) * SCALE + (bias[here, first:] - lse_row[:, first:])
            probs = jnp.exp(scores)
            d_probs = mm_nt(vv, dd)
            d_scores = (probs * (d_probs - delta[:, first:])).astype(BF16)
            pair_ref[1, here, :] = mm(probs.astype(BF16), dd).astype(BF16)
            dk = mm(d_scores, qq) * SCALE
            dq = mm_tn(d_scores, kk)
            if at == 0:
                dq_acc[...] = dq
            else:
                dq_acc[first:, :] += dq
            dk = unrotate(dk, cp_ref[here, :], sp_ref[here, :])
            dk, terms = norm_back(kr_ref[here, :], kg_ref[...], dk)
            pair_ref[0, here, :] = dk.astype(BF16)
            k_sum += jnp.sum(terms, axis=0, keepdims=True)
        kgg_ref[...] += k_sum
        for j in range(GROUPS):
            cols = slice(j * HEAD_DIM, (j + 1) * HEAD_DIM)
            dq = jnp.concatenate(
                [
                    dq_acc[(part * GROUPS + j) * half : (part * GROUPS + j + 1) * half, :]
                    for part in range(2)
                ],
                axis=0,
            ) * SCALE
            dq = unrotate(dq, co_ref[...], so_ref[...])
            dq, terms = norm_back(qr_ref[:, cols], qg_ref[...], dq)
            dq_ref[:, cols] = dq.astype(BF16)
            qgg_ref[...] += jnp.sum(terms, axis=0, keepdims=True)

    col = pl.BlockSpec((rows, pair), lambda g: (0, first_head + g))
    key = pl.BlockSpec((pack, HEAD_DIM), lambda g: (0, first_head + g))
    gain = whole((1, HEAD_DIM))
    return call(
        "attend_back", body,
        [
            queries, grad_mixed, attended, keys, values, lse, q_low, q_high, k_stream,
            query_raw, key_raw, query_gain, key_gain, cos_own, sin_own, cos_pack, sin_pack,
            *earlier,
        ],
        [
            col, col, col, key, key,
            pl.BlockSpec((1, 8, wide), lambda g: (first_head + g, 0, 0)),
            whole((1, wide)), whole((1, wide)), whole((pack, 1)),
            col, key, gain, gain,
            whole((rows, HEAD_DIM)), whole((rows, HEAD_DIM)),
            whole((pack, HEAD_DIM)), whole((pack, HEAD_DIM)),
        ]
        + [ANY] * len(earlier),
        [col, pl.BlockSpec((2, pack, HEAD_DIM), lambda g: (0, 0, first_head + g)), gain, gain],
        [
            shape((rows, HEADS * HEAD_DIM), BF16),
            shape((2, pack, KV_HEADS * HEAD_DIM), BF16),
            shape((1, HEAD_DIM), F32),
            shape((1, HEAD_DIM), F32),
        ],
        grid=(heads,),
        scratch=[pltpu.VMEM((pack, wide), F32), pltpu.VMEM((wide, HEAD_DIM), F32)],
        aliases={17 + i: i for i in range(len(earlier))},
    )


def normed_back_pack(d_pair, weights, ctx_size):
    _, pack, cols = d_pair.shape
    half = pack // (2 * ctx_size)
    width = weights.shape[0]

    def body(pair_ref, wk_ref, wv_ref, out_ref):
        part = mm_nt(pair_ref[0].reshape(2 * half, cols), wk_ref[...])
        part += mm_nt(pair_ref[1].reshape(2 * half, cols), wv_ref[...])
        out_ref[...] = part.astype(BF16)

    return call(
        "normed_back_pack", body, [d_pair.reshape(2, 2, ctx_size, half, cols), weights, weights],
        [
            pl.BlockSpec((2, 2, 1, half, cols), lambda d: (0, 0, d, 0, 0)),
            pl.BlockSpec((width, cols), lambda d: (0, 2)),
            pl.BlockSpec((width, cols), lambda d: (0, 3)),
        ],
        [pl.BlockSpec((2 * half, width), lambda d: (d, 0))],
        [shape((pack, width), BF16)],
        grid=(ctx_size,),
    )[0]


def normed_back_own(d_queries, weights):
    rows, cols = d_queries.shape
    width = weights.shape[0]
    block = 1024

    def body(dq_ref, w_ref, out_ref):
        part = mm_nt(dq_ref[...], w_ref[...])

        @pl.when(pl.program_id(0) == 0)
        def _():
            out_ref[...] = part

        @pl.when(pl.program_id(0) > 0)
        def _():
            out_ref[...] += part

    return call(
        "normed_back_own", body, [d_queries, weights],
        [
            pl.BlockSpec((rows, block), lambda j: (0, j)),
            pl.BlockSpec((width, block), lambda j: (0, j)),
        ],
        [whole((rows, width))],
        [shape((rows, width), F32)],
        grid=(cols // block,),
    )[0]


def input_back(d_own, d_pack, tokens, gain, grad_middle):
    rows, width = tokens.shape

    def body(a_ref, b_ref, t_ref, gain_ref, gm_ref, out_ref, gg_ref):
        incoming = a_ref[...] + b_ref[...].astype(F32)
        back, terms = norm_back(t_ref[...].astype(F32), gain_ref[...], incoming)
        out_ref[...] = (gm_ref[...] + back).astype(BF16)
        gg_ref[...] = jnp.sum(terms, axis=0, keepdims=True)

    full = whole((rows, width))
    return call(
        "input_back", body, [d_own, d_pack, tokens, gain, grad_middle],
        [full, full, full, whole((1, width)), full],
        [full, whole((1, width))],
        [shape((rows, width), BF16), shape((1, width), F32)],
        grid=(1,),
    )


def weight_grad(left, right, owners=None, cols=None, block=512):
    tokens, rows = left.shape
    count = 1 if owners is None else owners.shape[0]
    unit = rows // count
    deep = right.ndim == 3
    first, each = cols or (0, right.shape[-1])
    width = each * (right.shape[0] if deep else 1)

    def body(*refs):
        if owners is not None:
            own_ref, refs = refs[0], refs[1:]
        l_ref, r_ref, refs = refs[0], refs[1], refs[2:]
        outs, scratch = refs[: -1 if owners is None else -2], refs[-1 if owners is None else -2 :]

        @pl.when(pl.program_id(0) == 0)
        def _():
            scratch[0][...] = l_ref[...].T
            for k in range(count if owners is not None else 0):
                at = pl.multiple_of(own_ref[k] * unit, unit)
                scratch[1][k * unit : (k + 1) * unit, :] = scratch[0][pl.ds(at, unit), :]

        full = mm(scratch[-1][...], r_ref[0] if deep else r_ref[...]).astype(BF16)
        if owners is None:
            outs[0][...] = full
        else:
            full = full.reshape(count, unit, block)
            outs[0][...] = full[: count // 2]
            outs[1][...] = full[count // 2 :]

    per, start = each // block, first // block
    if deep:
        right_spec = pl.BlockSpec((1, tokens, block), lambda j, *_: (j // per, 0, start + j % per))
    else:
        right_spec = pl.BlockSpec((tokens, block), lambda j, *_: (0, start + j))
    if owners is None:
        out = [pl.BlockSpec((rows, block), lambda j: (0, j))]
        out_shape = [shape((rows, width), BF16)]
    else:
        out = [pl.BlockSpec((count // 2, unit, block), lambda j, own: (0, 0, j))] * 2
        out_shape = [shape((count // 2, unit, width), BF16)] * 2
    return call(
        "weight_grad", body, [left, right], [whole((tokens, rows)), right_spec], out, out_shape,
        grid=(width // block,),
        scratch=[pltpu.VMEM((rows, tokens), BF16)] * (1 if owners is None else 2),
        prefetch=() if owners is None else [owners],
    )


def fold(items, steps=1):
    arrays = []

    def slot(term):
        for i, known in enumerate(arrays):
            if known is term:
                return i
        arrays.append(term)
        return len(arrays) - 1

    laid = [([slot(t) for t in terms], rows, bit) for terms, rows, bit in items]
    in_specs = []
    for a in arrays:
        in_specs.append(
            IN_VMEM if steps == 1 else pl.BlockSpec(a.shape[:2] + (a.shape[2] // steps,), lambda j: (0, 0, j))
        )
    out_specs, out_shape = [], []
    for slots, (_, rows), bit in laid:
        many, _, cols = arrays[slots[0]].shape
        dims = (many, rows, cols) if bit is None else (many // 2, rows, cols)
        for _ in range(1 if bit is None else 2):
            out_specs.append(
                IN_VMEM if steps == 1 else pl.BlockSpec(dims[:2] + (cols // steps,), lambda j: (0, 0, j))
            )
            out_shape.append(shape(dims, BF16))

    def body(*refs):
        ins, outs = refs[: len(arrays)], list(refs[len(arrays) :])
        for slots, (first, rows), bit in laid:
            here = slice(first, first + rows)
            many = arrays[slots[0]].shape[0]

            def total(k):
                value = ins[slots[0]][k, here, :].astype(F32)
                for at in slots[1:]:
                    value = value + ins[at][k, here, :].astype(F32)
                return value.astype(BF16)

            if bit is None:
                out = outs.pop(0)
                for k in range(many):
                    out[k] = total(k)
                continue
            sent, kept = outs.pop(0), outs.pop(0)
            places = [0, 0]
            for k in range(many):
                with_bit = (k >> bit) & 1
                (sent if with_bit else kept)[places[with_bit]] = total(k)
                places[with_bit] += 1

    return call("fold", body, arrays, in_specs, out_specs, out_shape, grid=(steps,))


def choose(first, second, dims, odd):
    arrays = [a for a, _ in first + second]
    views = [v for _, v in first + second]

    def body(odd_ref, *refs):
        ins, (sent, kept) = refs[: len(arrays)], refs[len(arrays) :]

        def total(begin, end):
            value = ins[begin][views[begin]].astype(F32)
            for at in range(begin + 1, end):
                value = value + ins[at][views[at]].astype(F32)
            return value.astype(BF16)

        @pl.when(odd_ref[0] == 1)
        def _():
            sent[...] = total(0, len(first))
            kept[...] = total(len(first), len(arrays))

        @pl.when(odd_ref[0] == 0)
        def _():
            kept[...] = total(0, len(first))
            sent[...] = total(len(first), len(arrays))

    return call(
        "choose", body, arrays, [IN_VMEM] * len(arrays), [IN_VMEM] * 2, [shape(dims, BF16)] * 2,
        prefetch=[odd],
    )


def place(sums, odd, out_dims, cuts):
    arrays = [a for pair in sums for a in pair]

    def body(odd_ref, *refs):
        ins, outs = refs[: len(arrays)], refs[len(arrays) :]

        def write(swapped):
            for which, half, source, at, target in cuts:
                outs[at][target] = ins[2 * which + (half ^ swapped)][source].astype(F32)

        @pl.when(odd_ref[0] == 1)
        def _():
            write(1)

        @pl.when(odd_ref[0] == 0)
        def _():
            write(0)

    return call(
        "place", body, arrays, [IN_VMEM] * len(arrays), [whole(d) for d in out_dims],
        [shape(d, F32) for d in out_dims], prefetch=[odd],
    )


def swap(x, axis, bit):
    size = lax.axis_size(axis)
    return lax.ppermute(x, axis, [(i, i ^ bit) for i in range(size)])


def bits_of(size):
    return [1 << b for b in range(size.bit_length() - 1)]


def gather_pieces(own, cut):
    rest = bits_of(lax.axis_size("dp"))[1:]
    spans = [slice(0, cut), slice(cut, own.shape[1])]
    everything = slice(0, own.shape[1])
    held = {0: [(everything, own)]}
    for bit in rest:
        held[bit] = [(everything, swap(own, "dp", bit))]
    first = [held[bit][0][1] for bit in rest]
    for at in range(1 << len(rest)):
        at = 2 * at
        if at in held:
            continue
        held[at] = []
        for span, order in zip(spans, (rest, rest[::-1])):
            last = [bit for bit in order if at & bit][-1]
            before = held[at ^ last]
            source = before[0][1][:, span] if len(before) == 1 else before[spans.index(span)][1]
            held[at].append((span, swap(source, "dp", last)))
    for at in sorted(held):
        held[at | 1] = [(span, swap(piece, "dp", 1)) for span, piece in held[at]]
    return held, first


class Sum:
    def __init__(self, kept, sent, halves, odd):
        self.rest = bits_of(lax.axis_size("dp"))[1:]
        self.order = [list(range(len(self.rest))), list(range(len(self.rest)))[::-1]]
        self.left = [list(range(len(self.rest))), list(range(len(self.rest)))]
        self.odd = odd
        arrived = [swap(s, "dp", 1) for s in sent]
        if len(kept) == 1:
            kept, arrived = kept * 2, arrived * 2
        self.terms = [[k, a] for k, a in zip(kept, arrived)]
        self.rows = halves
        self.stage = 0

    def over_dp(self, steps=1):
        bits = [order[self.stage] for order in self.order]
        items = [
            (terms, rows, left.index(bit))
            for terms, rows, left, bit in zip(self.terms, self.rows, self.left, bits)
        ]
        sent0, kept0, sent1, kept1 = fold(items, steps)
        self.terms = [
            [kept, swap(sent, "dp", self.rest[bit])]
            for kept, sent, bit in zip((kept0, kept1), (sent0, sent1), bits)
        ]
        self.rows = [(0, k.shape[1]) for k in (kept0, kept1)]
        for left, bit in zip(self.left, bits):
            left.remove(bit)
        self.stage += 1

    def to_ctx(self):
        first, second = [[(t, 0) for t in terms] for terms in self.terms]
        self.begin_ctx(first, second, first[0][0].shape[1:])

    def begin_ctx(self, first, second, dims):
        sent, kept = choose(first, second, dims, self.odd)
        self.total, self.next = [kept, swap(sent, "ctx", 1)], bits_of(lax.axis_size("ctx"))[1:]

    def over_ctx(self):
        a, b = [t[None] for t in self.total]
        total = fold([([a, b], (0, a.shape[1]), None)])[0][0]
        if self.next:
            self.total = [total, swap(total, "ctx", self.next.pop(0))]
        else:
            self.total = [total, swap(total, "ctx", 1)]


def sum_everywhere(x):
    for axis in ("dp", "ctx"):
        for bit in bits_of(lax.axis_size(axis)):
            x = x + swap(x, axis, bit)
    return x


def on_device(
    tokens, doc_starts, attn_gain, w_query, w_key, w_value, w_out,
    query_gain, key_gain, mlp_gain, w_gate, w_up, w_down, cotangent,
):
    ORDER.clear()
    rows, width = tokens.shape[1], tokens.shape[2]
    stretch = rows // 2
    ctx_size = lax.axis_size("ctx")
    dp_size = lax.axis_size("dp")
    ctx_at = lax.axis_index("ctx")
    dp_at = lax.axis_index("dp")
    pack_rows = rows * ctx_size
    unit = width // dp_size
    inner = HEADS * HEAD_DIM
    own_tokens = tokens[0]
    grad_out = cotangent[0]
    starts = doc_starts[0]
    odd = (ctx_at % 2).astype(jnp.int32)[None]
    dp_bits = bits_of(dp_size)

    gains = jnp.concatenate(
        [attn_gain[:, None], mlp_gain[:, None], jnp.zeros((unit, HEAD_DIM - 2), BF16)], axis=1
    )

    def packing(_, ins, outs):
        at = 0
        for ref in ins:
            yield ref.at[:, :], outs[0].at[:, pl.ds(at, ref.shape[1])]
            at += ref.shape[1]

    def stacking(_, ins, outs):
        down, gate, up, out = ins
        stack_ref = outs[0]
        yield down.at[:, :], stack_ref.at[pl.ds(0, 3 * unit)]
        for i in range(3):
            cols = pl.ds(i * width, width)
            yield gate.at[:, cols], stack_ref.at[pl.ds((3 + i) * unit, unit)]
            yield up.at[:, cols], stack_ref.at[pl.ds((6 + i) * unit, unit)]
        yield out.at[:, :], stack_ref.at[pl.ds(9 * unit, 2 * unit)]

    attn_cols = inner + 2 * width + HEAD_DIM
    own_attn = copies(
        "pack_attn", [w_query, w_key, w_value, gains], packing, [shape((unit, attn_cols), BF16)]
    )[0]
    pieces, first_pieces = gather_pieces(own_attn, inner)
    from_left, from_right = [], []
    for step in range(1, ctx_size):
        block = from_left[-1] if from_left else own_tokens
        from_left.append(
            lax.ppermute(block, "ctx", [(i, i + 1) for i in range(step - 1, ctx_size - 1)])
        )
        block = from_right[-1] if from_right else own_tokens
        from_right.append(
            lax.ppermute(block, "ctx", [(i + 1, i) for i in range(ctx_size - step)])
        )
    stack_in = copies(
        "pack_stack", [w_down, w_gate, w_up, w_out], stacking, [shape((11 * unit, width), BF16)]
    )[0]
    stack = lax.all_gather(stack_in, "dp", axis=0)
    touch([from_left[0], from_right[0]])
    touch(first_pieces)
    touch([from_left[1], from_right[1]])

    place_at = jnp.arange(pack_rows, dtype=jnp.int32)
    in_half = place_at % (pack_rows // 2)
    part, device, row = place_at // (pack_rows // 2), in_half // stretch, place_at % stretch
    key_stream = stream_index(device * rows + part * stretch + row, stretch, ctx_size)
    query_stream = stream_index(
        ctx_at * rows + jnp.arange(rows, dtype=jnp.int32), stretch, ctx_size
    )
    key_open = opening_of(key_stream, starts)
    query_open = opening_of(query_stream, starts)
    cos_pack, sin_pack = rotary(key_stream - key_open)
    cos_own, sin_own = rotary(query_stream - query_open)

    def doubled(v):
        return jnp.concatenate([v[:stretch]] * GROUPS + [v[stretch:]] * GROUPS)[None, :]

    owners = (dp_at ^ jnp.arange(dp_size, dtype=jnp.int32)).astype(jnp.int32)
    listed = [(k, span, piece) for k in range(dp_size) for span, piece in pieces[k]]

    def assembling(prefetch, ins, outs):
        for (k, span, _), ref in zip(listed, ins):
            at = pl.multiple_of(prefetch[0][k] * unit, unit)
            target = outs[0].at[pl.ds(at, unit), pl.ds(span.start, span.stop - span.start)]
            yield ref.at[:, :], target

    attn_w = copies(
        "assemble_weights", [piece for _, _, piece in listed], assembling,
        [shape((width, attn_cols), BF16)], prefetch=[owners],
    )[0]
    gain_rows = attn_w[:, inner + 2 * width :][:, :2].astype(F32).T
    gain_attn, gain_mlp = gain_rows[0:1], gain_rows[1:2]
    gain_query = query_gain.astype(F32)[None, :]
    gain_key = key_gain.astype(F32)[None, :]

    normed = norm_own(own_tokens, gain_attn)
    query_raw, queries = project_queries(normed, attn_w, gain_query, cos_own, sin_own)
    places = ((ctx_at - jnp.arange(ctx_size, dtype=jnp.int32)) % ctx_size).astype(jnp.int32)
    normed_pack = norm_pack(
        own_tokens, from_left, from_right, gain_attn, places, ctx_at.astype(jnp.int32)[None]
    ).reshape(pack_rows, width)
    key_raw, keys, values = project_keys_values(normed_pack, attn_w, gain_key, cos_pack, sin_pack)
    attended, mixed, lse = attend(
        queries, keys, values, query_open[:, None], query_stream[:, None], key_stream[None, :]
    )
    middle, normed_mid = project_out(mixed, stack, own_tokens, gain_mlp)
    hidden, slope_gate, slope_up = gate_up(normed_mid, stack)

    order = [2 * k for k in range(dp_size // 2)] + [2 * k + 1 for k in range(dp_size // 2)]
    owners = (dp_at ^ jnp.array(order, jnp.int32)).astype(jnp.int32)
    everything = slice(None)
    ctx_steps = len(bits_of(ctx_size))

    def two_rows(total, half):
        cuts = [(0, k, everything, 0, slice(k * half, (k + 1) * half)) for k in range(2)]
        return place([total.total], odd, [(2 * half, width)], cuts)[0]

    def halves_of(pair):
        half = pair[0].shape[1] // 2
        return Sum(pair[:1], pair[1:], [(0, half), (half, half)], odd), half

    later_dp, later_ctx = len(dp_bits) - 2, ctx_steps - 1
    down, down_half = halves_of(weight_grad(hidden, grad_out, owners, block=256))
    output, d_both = down_both(hidden, slope_gate, slope_up, grad_out, stack, middle)
    down.over_dp()
    wide_grad = weight_grad(normed_mid, d_both)[0]
    wide_grad = lax.psum_scatter(wide_grad, "dp", scatter_dimension=0, tiled=True)
    grad_middle, grad_branch, mlp_part = mlp_back(d_both, stack, middle, gain_mlp, grad_out)
    for _ in range(later_dp):
        down.over_dp()
    grad_mixed = mixed_back(grad_branch, stack)
    out, out_half = halves_of(weight_grad(mixed, grad_branch, owners, block=256))
    back_args = (
        queries, grad_mixed, attended, keys, values, lse,
        doubled(query_open), doubled(query_stream), key_stream[:, None],
        query_raw, key_raw, gain_query, gain_key, cos_own, sin_own, cos_pack, sin_pack,
    )
    quarter = KV_HEADS // 4
    gain_parts = []

    def attend_quarter(at, early):
        results = attend_back(*back_args, at * quarter, quarter, early)
        gain_parts.append(results[2:])
        return results[:2]

    def attention_grads(at):
        query = weight_grad(normed, d_query, owners, (at * inner // 2, inner // 2))
        pair = weight_grad(normed_pack, d_pair, owners, (at * width // 2, width // 2))
        return Sum([query[0], pair[0]], [query[1], pair[1]], [(0, unit), (0, unit)], odd)

    early = attend_quarter(0, ())
    down.to_ctx()
    out.over_dp()
    d_query, d_pair = attend_quarter(1, early)
    down.over_ctx()
    for _ in range(later_dp):
        out.over_dp()
    attn_one = attention_grads(0)
    early = attend_quarter(2, (d_query, d_pair))
    for _ in range(later_ctx):
        down.over_ctx()
    out.to_ctx()
    attn_one.over_dp()
    d_query, d_pair = attend_quarter(3, early)
    d_normed = normed_back_pack(d_pair, attn_w, ctx_size)
    d_normed = lax.psum_scatter(d_normed, "ctx", scatter_dimension=0, tiled=True)
    for _ in range(later_dp):
        attn_one.over_dp()
    out.over_ctx()
    attn_two = attention_grads(1)
    down_grad = two_rows(down, down_half)
    wide = Sum([], [], None, odd)
    wide.begin_ctx(
        [(wide_grad, (everything, slice(0, 3 * width)))],
        [(wide_grad, (everything, slice(3 * width, 6 * width)))],
        (unit, 3 * width),
    )
    attn_one.to_ctx()
    attn_two.over_dp()
    d_own = normed_back_own(d_query, attn_w)
    for _ in range(later_ctx):
        out.over_ctx()
    for _ in range(later_dp):
        attn_two.over_dp()
    wide.over_ctx()
    attn_one.over_ctx()
    w_out_grad = two_rows(out, out_half)
    attn_two.to_ctx()
    for _ in range(later_ctx):
        wide.over_ctx()
        attn_one.over_ctx()
    attn_two.over_ctx()
    input_grad, attn_part = input_back(d_own, d_normed, own_tokens, gain_attn, grad_middle)
    gate_grad, up_grad = place(
        [wide.total], odd, [(unit, 3 * width)] * 2, [(0, k, everything, k, everything) for k in range(2)]
    )
    for _ in range(ctx_steps - 1):
        attn_two.over_ctx()
    cuts = []
    for at in range(2):
        near, far = slice(0, width // 2), slice(width // 2, width)
        cuts.append((at, 0, everything, 0, (everything, slice(at * inner // 2, (at + 1) * inner // 2))))
        cuts.append((at, 1, (everything, near), 1, (everything, (near, far)[at])))
        cuts.append((at, 1, (everything, far), 2, (everything, (near, far)[at])))
    query_grad, key_grad, value_grad = place(
        [attn_one.total, attn_two.total], odd, [(unit, inner), (unit, width), (unit, width)], cuts
    )
    query_part, key_part = [sum(parts[1:], parts[0]) for parts in zip(*gain_parts)]

    parts = [attn_part, mlp_part, query_part, key_part]
    small = sum_everywhere(jnp.concatenate(parts, axis=1).reshape(-1, HEAD_DIM)).reshape(-1)
    attn_gain_grad = lax.dynamic_slice(small, (dp_at * unit,), (unit,))
    mlp_gain_grad = lax.dynamic_slice(small, (width + dp_at * unit,), (unit,))
    query_gain_grad = small[2 * width : 2 * width + HEAD_DIM]
    key_gain_grad = small[2 * width + HEAD_DIM :]
    return (
        output[None], input_grad[None], attn_gain_grad, query_grad, key_grad, value_grad, w_out_grad,
        query_gain_grad, key_gain_grad, mlp_gain_grad, gate_grad, up_grad, down_grad,
    )


def solution(mesh):
    in_specs = (
        P("dp", "ctx", None),
        P("dp", None),
        P("dp"),
        P("dp", None),
        P("dp", None),
        P("dp", None),
        P("dp", None),
        P(),
        P(),
        P("dp"),
        P("dp", None),
        P("dp", None),
        P("dp", None),
        P("dp", "ctx", None),
    )
    out_specs = (
        P("dp", "ctx", None),
        P("dp", "ctx", None),
        P("dp"),
        P("dp", None),
        P("dp", None),
        P("dp", None),
        P("dp", None),
        P(),
        P(),
        P("dp"),
        P("dp", None),
        P("dp", None),
        P("dp", None),
    )
    return jax.shard_map(
        on_device, mesh=mesh, in_specs=in_specs, out_specs=out_specs, check_vma=False
    )
```

```python
import functools
import math

import jax
import jax.numpy as jnp
from jax import lax
from jax.experimental import pallas as pl
from jax.experimental.pallas import tpu as pltpu
from jax.sharding import PartitionSpec as P

HEADS = 16
KV_HEADS = 8
HEAD_DIM = 128
GROUPS = HEADS // KV_HEADS

EPSILON = 1e-06
ROPE_BASE = 1000000.0
MASKED = -1e30
SCALE = HEAD_DIM ** (-0.5)

F32 = jnp.float32
BF16 = jnp.bfloat16
MIB = 1 << 20
VMEM_MIB = 20
LARGE = 1 << 18


ORDER = []


def shape(dims, dtype):
    return jax.ShapeDtypeStruct(dims, dtype)


ANY = pl.BlockSpec(memory_space=pl.ANY)
IN_VMEM = pl.BlockSpec(memory_space=pltpu.VMEM)
IN_HBM = pl.BlockSpec(memory_space=pltpu.HBM)


def in_hbm(spec, array):
    return spec not in (IN_VMEM, ANY, IN_HBM) and math.prod(array.shape) * 2 >= LARGE


def call(
    name, body, args, in_specs, out_specs, out_shape, grid=(1,), scratch=(), prefetch=(), aliases=None,
    after=(), vmem=VMEM_MIB,
):
    waits = list(ORDER) + list(after)
    wait_specs = [IN_VMEM] * len(ORDER) + [ANY] * len(after)
    taken = len(prefetch) + len(args)
    token = taken + len(waits) + len(out_shape)
    args = [
        pltpu.with_memory_space_constraint(a, pltpu.HBM) if in_hbm(s, a) else a
        for a, s in zip(args, in_specs)
    ]
    out_shape = [
        pltpu.HBM(o.shape, o.dtype) if in_hbm(s, o) else o for o, s in zip(out_shape, out_specs)
    ]

    def without(*refs):
        refs[token][...] = jnp.zeros_like(refs[token])
        body(*refs[:taken], *refs[taken + len(waits) : token], *refs[token + 1 :])

    results = pl.pallas_call(
        without,
        grid_spec=pltpu.PrefetchScalarGridSpec(
            num_scalar_prefetch=len(prefetch),
            grid=grid,
            in_specs=list(in_specs) + wait_specs,
            out_specs=list(out_specs) + [IN_VMEM],
            scratch_shapes=list(scratch),
        ),
        out_shape=out_shape + [shape((8, HEAD_DIM), F32)],
        input_output_aliases={len(prefetch) + i: o for i, o in (aliases or {}).items()},
        compiler_params=pltpu.CompilerParams(vmem_limit_bytes=vmem * MIB),
        cost_estimate=pl.CostEstimate(flops=0, bytes_accessed=0, transcendentals=0),
        name=name,
    )(*prefetch, *args, *waits)
    ORDER[:] = [results[-1]]
    return results[:-1]


def whole(dims):
    return pl.BlockSpec(dims, lambda *_: (0,) * len(dims))


def mm(a, b):
    return lax.dot_general(a, b, (((1,), (0,)), ((), ())), preferred_element_type=F32)


def mm_nt(a, b):
    return lax.dot_general(a, b, (((1,), (1,)), ((), ())), preferred_element_type=F32)


def mm_tn(a, b):
    return lax.dot_general(a, b, (((0,), (0,)), ((), ())), preferred_element_type=F32)


def mean_last(v):
    return jnp.sum(v, axis=-1, keepdims=True) * (1.0 / v.shape[-1])


def factor_of(v):
    return lax.rsqrt(mean_last(v * v) + EPSILON)


def norm_back(v, gain, incoming):
    f = factor_of(v)
    weighted = incoming * gain
    inner = mean_last(weighted * v)
    return f * weighted - v * (f * f * f * inner), incoming * v * f


def stream_index(row_ids, stretch_rows, ctx_size):
    slab_index = row_ids // (2 * stretch_rows)
    within = row_ids % (2 * stretch_rows)
    mirrored = (2 * ctx_size - 1 - slab_index) * stretch_rows + within - stretch_rows
    return jnp.where(within < stretch_rows, slab_index * stretch_rows + within, mirrored)


def opening_of(stream, starts):
    started = starts[None, :] <= stream[:, None]
    return jnp.max(jnp.where(started, starts[None, :], 0), axis=1)


def rotary(positions):
    half_dim = HEAD_DIM // 2
    inverse = jnp.exp(
        jnp.arange(half_dim, dtype=F32) * (-2.0 * math.log(ROPE_BASE) / HEAD_DIM)
    )
    angles = positions.astype(F32)[:, None] * inverse[None, :]
    cos_half, sin_half = jnp.cos(angles), jnp.sin(angles)
    return (
        jnp.concatenate([cos_half, cos_half], axis=1),
        jnp.concatenate([-sin_half, sin_half], axis=1),
    )


def copies(name, sources, plan, out_shape, prefetch=(), after=(), in_specs=None, out_specs=None):
    count = len(sources)
    first = len(prefetch)

    def body(*refs):
        ins = refs[first : first + count]
        for source, target in plan(refs[:first], ins, refs[first + count :]):
            target[...] = source[...]

    return call(
        name, body, sources, in_specs or [IN_VMEM] * count, out_specs or [IN_VMEM] * len(out_shape), out_shape,
        prefetch=prefetch, after=after,
    )


def touch(after):
    call("touch", lambda *_: None, [], [], [], [], after=after, vmem=4)


def norm_own(tokens, gain):
    def body(t_ref, g_ref, out_ref):
        x = t_ref[...].astype(F32)
        out_ref[...] = (x * factor_of(x) * g_ref[...]).astype(BF16)

    return call(
        "norm_own", body, [tokens, gain], [IN_VMEM] * 2, [IN_VMEM], [shape(tokens.shape, BF16)]
    )[0]


def norm_pack(own, from_left, from_right, gain, places, ctx_at):
    count = len(from_left) + 1
    rows, width = own.shape
    half = rows // 2

    def body(places_ref, at_ref, gain_ref, *refs):
        blocks, pack_ref = refs[:-1], refs[-1]
        step = pl.program_id(0)
        me = at_ref[0]

        def write(ref):
            x = ref[...].astype(F32)
            low = (x * factor_of(x) * gain_ref[...]).astype(BF16)
            pack_ref[...] = low.reshape(2, 1, half, width)

        @pl.when(step == 0)
        def _():
            write(blocks[0])

        for s in range(1, count):

            @pl.when((step == s) & (me >= s))
            def _():
                write(blocks[s])

            @pl.when((step == s) & (me < s))
            def _():
                write(blocks[count - 1 + count - s])

    blocks = [own] + from_left + from_right
    return call(
        "norm_pack", body, [gain] + blocks,
        [whole((1, width))] + [IN_VMEM] * len(blocks),
        [pl.BlockSpec((2, 1, half, width), lambda k, at, me: (0, at[k], 0, 0))],
        [shape((2, count, half, width), BF16)],
        grid=(count,), prefetch=[places, ctx_at],
    )[0]


def lane_sums(v):
    cols = v.shape[-1]
    head = lax.broadcasted_iota(jnp.int32, (cols, cols), 0) // HEAD_DIM
    same = (head == lax.broadcasted_iota(jnp.int32, (cols, cols), 1) // HEAD_DIM).astype(BF16)
    high = v.astype(BF16)
    low = (v - high.astype(F32)).astype(BF16)
    return mm(high, same) + mm(low, same)


def head_factors(raw):
    return lax.rsqrt(lane_sums(raw * raw) * (1.0 / HEAD_DIM) + EPSILON)


def turn(v):
    parts = [
        pltpu.roll(v[:, at : at + HEAD_DIM], HEAD_DIM // 2, 1) for at in range(0, v.shape[1], HEAD_DIM)
    ]
    return parts[0] if len(parts) == 1 else jnp.concatenate(parts, axis=1)


def rotated(v, cos, sin):
    return v * cos + turn(v) * sin


def rope(raw, gain, cos, sin):
    return rotated(raw * head_factors(raw) * gain, cos, sin)


def twice(ref):
    return jnp.concatenate([ref[...]] * 2, axis=1)


def project_queries(x, weights, gain, cos, sin):
    rows, width = x.shape
    cols = HEADS * HEAD_DIM
    block = 2 * HEAD_DIM
    each = 2 * block
    col = pl.BlockSpec((rows, each), lambda j: (0, j))

    def body(x_ref, w_ref, g_ref, c_ref, s_ref, raw_ref, rot_ref, fac_ref):
        g, c, s = twice(g_ref), twice(c_ref), twice(s_ref)
        for j in range(each // block):
            at = slice(j * block, (j + 1) * block)
            raw = mm(x_ref[...], w_ref[:, at])
            raw_ref[:, at] = raw.astype(BF16)
            factors = head_factors(raw)
            rot_ref[:, at] = rotated(raw * factors * g, c, s).astype(BF16)
            for h in range(2):
                fac_ref[2 * j + h] = factors[:, h * HEAD_DIM : (h + 1) * HEAD_DIM].T[:8]

    return call(
        "project_queries", body, [x, weights, gain, cos, sin],
        [IN_VMEM, pl.BlockSpec((width, each), lambda j: (0, j))] + [IN_VMEM] * 3,
        [col, col, pl.BlockSpec((each // HEAD_DIM, 8, rows), lambda j: (j, 0, 0))],
        [shape((rows, cols), BF16), shape((rows, cols), BF16), shape((HEADS, 8, rows), F32)],
        grid=(cols // each,),
    )


def project_keys_values(x, weights, gain, cos, sin):
    rows, width = x.shape
    block = 2 * HEAD_DIM
    cols = KV_HEADS * HEAD_DIM
    inner = HEADS * HEAD_DIM
    part = 256

    def body(x_ref, wk_ref, wv_ref, g_ref, c_ref, s_ref, raw_ref, rot_ref, val_ref):
        wk, wv = wk_ref[...], wv_ref[...]
        g = twice(g_ref)
        for i in range(rows // part):
            here = slice(i * part, (i + 1) * part)
            raw = mm(x_ref[here, :], wk)
            raw_ref[here, :] = raw.astype(BF16)
            val_ref[here, :] = mm(x_ref[here, :], wv).astype(BF16)
            c, s = [jnp.concatenate([r[here, :]] * 2, axis=1) for r in (c_ref, s_ref)]
            rot_ref[here, :] = rope(raw, g, c, s).astype(BF16)

    col = pl.BlockSpec((rows, block), lambda j: (0, j))
    return call(
        "project_keys_values", body, [x, weights, weights, gain, cos, sin],
        [
            IN_VMEM,
            pl.BlockSpec((width, block), lambda j: (0, inner // block + j)),
            pl.BlockSpec((width, block), lambda j: (0, (inner + cols) // block + j)),
        ]
        + [IN_VMEM] * 3,
        [col, col, col], [shape((rows, cols), BF16)] * 3, grid=(cols // block,),
    )


LOG2E = 1.4426950408889634


def attend(queries, keys, values, q_low, q_high, k_stream):
    rows = queries.shape[0]
    half = rows // 2
    pack = keys.shape[0]
    pair = GROUPS * HEAD_DIM

    def body(q_ref, k_ref, v_ref, lo_ref, hi_ref, ks_ref, mix_ref, lse_ref, bias):
        @pl.when(pl.program_id(0) == 0)
        def _():
            ks = ks_ref[...]
            ok = (ks >= lo_ref[...]) & (ks <= hi_ref[...])
            bias[...] = jnp.where(ok, 0.0, MASKED)

        v_ones = jnp.concatenate([v_ref[...], jnp.ones((pack, HEAD_DIM), BF16)], axis=1)
        for part in range(2):
            here = slice(part * half, (part + 1) * half)
            seen = pack // 2 if part == 0 else pack
            for j in range(GROUPS):
                cols = slice(j * HEAD_DIM, (j + 1) * HEAD_DIM)
                scores = mm_nt(q_ref[here, cols], k_ref[:seen, :]) * (SCALE * LOG2E) + bias[here, :seen]
                both = mm(jnp.exp2(scores).astype(BF16), v_ones[:seen])
                total = both[:, HEAD_DIM:]
                mix_ref[here, cols] = (both[:, :HEAD_DIM] * (1.0 / total)).astype(BF16)
                lse_ref[j, :, here] = jnp.log2(total).T[:8]

    col = pl.BlockSpec((rows, pair), lambda g: (0, g))
    key = pl.BlockSpec((pack, HEAD_DIM), lambda g: (0, g))
    return call(
        "attend", body, [queries, keys, values, q_low, q_high, k_stream],
        [col, key, key, whole((rows, 1)), whole((rows, 1)), whole((1, pack))],
        [col, pl.BlockSpec((GROUPS, 8, rows), lambda g: (g, 0, 0))],
        [shape((rows, HEADS * HEAD_DIM), BF16), shape((HEADS, 8, rows), F32)],
        grid=(KV_HEADS,),
        scratch=[pltpu.VMEM((rows, pack), F32)],
    )


def high_low(v):
    high = v.astype(BF16)
    return high, (v - high.astype(F32)).astype(BF16)


def feed_forward(mixed, tokens, grad, gain, stack):
    rows, inner = mixed.shape
    count, _, width = stack.shape
    unit = width // count
    hidden = 3 * width
    block = 256

    def body(
        mixed_hbm, tok_hbm, dy_hbm, gain_ref, stack_ref,
        out_ref, low_ref, h_ref, both_ref, mid_ref,
        w, acc, mixed_ref, tok_ref, dy_ref, sems,
    ):
        def move(first, many, sem):
            here = (slice(None), pl.ds(first * unit, many * unit))
            return pltpu.make_async_copy(stack_ref.at[here], w.at[here], sems.at[sem])

        loads = [
            pltpu.make_async_copy(a, b, sems.at[8 + i])
            for i, (a, b) in enumerate(((mixed_hbm, mixed_ref), (tok_hbm, tok_ref), (dy_hbm, dy_ref)))
        ]
        out_copy = move(9, 2, 0)
        gate_copies = [move(3 + i, 1, 1 + i) for i in range(3)]
        up_copies = [move(6 + i, 1, 4 + i) for i in range(3)]
        down_copy = move(0, 3, 7)
        loads[0].start()
        out_copy.start()
        loads[1].start()
        loads[2].start()
        for a, b in zip(gate_copies, up_copies):
            a.start()
            b.start()
        down_copy.start()

        for load in loads:
            load.wait()
        out_copy.wait()
        for j in range(width // block):
            cols = slice(j * block, (j + 1) * block)
            part = w[:, 9 * unit : 11 * unit, cols].reshape(inner, block)
            mid_ref[:, cols] = tok_ref[:, cols].astype(F32) + mm(mixed_ref[...], part)
        x = mid_ref[...]
        low_ref[...] = (x * factor_of(x) * gain_ref[...]).astype(BF16)

        for i in range(3):
            gate_copies[i].wait()
            up_copies[i].wait()
            for j in range(width // block):
                cols = slice(j * block, (j + 1) * block)
                to = slice(i * width + j * block, i * width + (j + 1) * block)
                g = mm(low_ref[...], w[:, (3 + i) * unit : (4 + i) * unit, cols].reshape(width, block))
                u = mm(low_ref[...], w[:, (6 + i) * unit : (7 + i) * unit, cols].reshape(width, block))
                s = 1.0 / (1.0 + jnp.exp(-g))
                act = g * s
                h_ref[:, to] = (act * u).astype(BF16)
                both_ref[0, :, to] = (u * (s + act * (1.0 - s))).astype(BF16)
                both_ref[1, :, to] = act.astype(BF16)

        down_copy.wait()
        wide = 384
        owners = wide // (3 * unit)
        acc[...] = mid_ref[...]
        for j in range(hidden // wide):
            cols = slice(j * wide, (j + 1) * wide)
            part = w[j * owners : (j + 1) * owners, 0 : 3 * unit, :].reshape(wide, width)
            dh = mm_nt(dy_ref[...], part)
            both_ref[0, :, cols] = (both_ref[0, :, cols].astype(F32) * dh).astype(BF16)
            both_ref[1, :, cols] = (both_ref[1, :, cols].astype(F32) * dh).astype(BF16)
            acc[...] += mm(h_ref[:, cols], part)
        out_ref[...] = acc[...].astype(BF16)

    full = (rows, width)
    return call(
        "feed_forward", body, [mixed, tokens, grad, gain, stack],
        [IN_HBM, IN_HBM, IN_HBM, whole((1, width)), IN_HBM],
        [whole(full), IN_VMEM, IN_VMEM, IN_VMEM, IN_VMEM],
        [
            shape(full, BF16), shape(full, BF16), shape((rows, hidden), BF16),
            shape((2, rows, hidden), BF16), shape(full, F32),
        ],
        scratch=[
            pltpu.VMEM(stack.shape, BF16),
            pltpu.VMEM(full, F32),
            pltpu.VMEM((rows, inner), BF16),
            pltpu.VMEM(full, BF16),
            pltpu.VMEM(full, BF16),
            pltpu.SemaphoreType.DMA((11,)),
        ],
        vmem=40,
    )


def branch_back(both, middle, grad, gain, mixed, lse, factors, stack):
    _, rows, hidden = both.shape
    count, _, width = stack.shape
    unit = width // count
    inner = mixed.shape[1]
    block = 256

    def body(
        both_ref, mid_ref, dy_ref, gain_ref, mixed_ref, lse_ref, fac_ref, stack_ref,
        gm_ref, gb_ref, gg_ref, dm_ref, parcel_ref,
        w, acc, deltas, sems,
    ):
        owners_in = block // unit
        steps = width // block
        copies_in = []
        for b in range(steps):
            here = (pl.ds(b * owners_in, owners_in), pl.ds(3 * unit, 6 * unit))
            to = (pl.ds(b * owners_in, owners_in), pl.ds(0, 6 * unit))
            copies_in.append(pltpu.make_async_copy(stack_ref.at[here], w.at[to], sems.at[b]))
        here, to = (slice(None), pl.ds(9 * unit, 2 * unit)), (slice(None), pl.ds(6 * unit, 2 * unit))
        out_copy = pltpu.make_async_copy(stack_ref.at[here], w.at[to], sems.at[steps])
        for copy in copies_in + [out_copy]:
            copy.start()

        for b in range(steps):
            copies_in[b].wait()
            at = slice(b * owners_in, (b + 1) * owners_in)
            total = None
            for i in range(6):
                part = w[at, i * unit : (i + 1) * unit, :].reshape(block, width)
                term = mm_nt(both_ref[i // 3, :, (i % 3) * width : (i % 3 + 1) * width], part)
                total = term if total is None else total + term
            acc[:, b * block : (b + 1) * block] = total

        back, terms = norm_back(mid_ref[...], gain_ref[...], acc[...])
        grad_mid = dy_ref[...].astype(F32) + back
        gm_ref[...] = grad_mid
        gb_ref[...] = grad_mid.astype(BF16)
        gg_ref[...] = jnp.sum(terms, axis=0, keepdims=True)

        out_copy.wait()
        owners_out = block // (2 * unit)
        for j in range(inner // block):
            cols = slice(j * block, (j + 1) * block)
            at = slice(j * owners_out, (j + 1) * owners_out)
            dm = mm_nt(gb_ref[...], w[at, 6 * unit : 8 * unit, :].reshape(block, width)).astype(BF16)
            dm_ref[:, cols] = dm
            terms = (dm.astype(F32) * mixed_ref[:, cols].astype(F32)).T
            for k in range(block // HEAD_DIM):
                head = j * (block // HEAD_DIM) + k
                deltas[head : head + 1, :] = jnp.sum(
                    terms[k * HEAD_DIM : (k + 1) * HEAD_DIM], axis=0, keepdims=True
                )
        parcel_ref[:rows, :] = gb_ref[...]
        parcel_ref[rows:, :] = jnp.zeros((3 * HEADS, width), BF16)
        for which, values in enumerate((lse_ref[:, 0, :], deltas[...], fac_ref[:, 0, :])):
            at = rows + which * HEADS
            for side, piece in enumerate(high_low(values)):
                parcel_ref[at : at + HEADS, side * rows : (side + 1) * rows] = piece

    full = (rows, width)
    return call(
        "branch_back", body, [both, middle, grad, gain, mixed, lse, factors, stack],
        [
            IN_VMEM, IN_VMEM, whole(full), whole((1, width)), whole((rows, inner)), whole(lse.shape),
            whole(factors.shape), IN_HBM,
        ],
        [whole(full), IN_VMEM, IN_VMEM, whole((rows, inner)), IN_VMEM],
        [
            shape(full, F32), shape(full, BF16), shape((1, width), F32), shape((rows, inner), BF16),
            shape((rows + 3 * HEADS, width), BF16),
        ],
        scratch=[
            pltpu.VMEM((count, 8 * unit, width), BF16),
            pltpu.VMEM(full, F32),
            pltpu.VMEM((HEADS, rows), F32),
            pltpu.SemaphoreType.DMA((width // block + 1,)),
        ],
        vmem=32,
    )


def head_norm_back(v, gain, incoming):
    f = head_factors(v)
    weighted = incoming * gain
    inner = lane_sums(weighted * v) * (1.0 / HEAD_DIM)
    return f * (weighted - v * (f * f * inner)), incoming * v * f


def query_back(
    queries, grad_mixed, mixed, keys, values, lse, q_low, q_high, k_stream, query_raw, gain, cos, sin,
    first, count, earlier=(),
):
    rows = queries.shape[0]
    half = rows // 2
    pack = keys.shape[0]
    pair = GROUPS * HEAD_DIM

    def body(
        q_ref, do_ref, mix_ref, k_ref, v_ref, lse_ref, lo_ref, hi_ref, ks_ref, raw_ref, g_ref, c_ref, s_ref,
        *rest,
    ):
        dq_ref, gg_ref, bias = rest[len(earlier) :]

        @pl.when(pl.program_id(0) == 0)
        def _():
            ks = ks_ref[...]
            ok = (ks >= lo_ref[...]) & (ks <= hi_ref[...])
            bias[...] = jnp.where(ok, 0.0, MASKED)
            gg_ref[...] = jnp.zeros_like(gg_ref)

        deltas = lane_sums(do_ref[...].astype(F32) * mix_ref[...].astype(F32))
        for j in range(GROUPS):
            cols = slice(j * HEAD_DIM, (j + 1) * HEAD_DIM)
            lse_col = jnp.broadcast_to(lse_ref[j, 0:1, :], (HEAD_DIM, rows)).T[:, :1]
            grads = []
            for part in range(2):
                here = slice(part * half, (part + 1) * half)
                seen = pack // 2 if part == 0 else pack
                scores = mm_nt(q_ref[here, cols], k_ref[:seen, :]) * (SCALE * LOG2E) + bias[here, :seen]
                probs = jnp.exp2(scores - lse_col[here])
                d_probs = mm_nt(do_ref[here, cols], v_ref[:seen, :])
                d_scores = (probs * (d_probs - deltas[here, cols][:, :1])).astype(BF16)
                grads.append(mm(d_scores, k_ref[:seen, :]))
            dq = jnp.concatenate(grads, axis=0) * SCALE
            dq = dq * c_ref[...] - turn(dq) * s_ref[...]
            dq, terms = head_norm_back(raw_ref[:, cols].astype(F32), g_ref[...], dq)
            dq_ref[:, cols] = dq.astype(BF16)
            gg_ref[...] += jnp.sum(terms, axis=0, keepdims=True)

    col = pl.BlockSpec((rows, pair), lambda g: (0, first + g))
    key = pl.BlockSpec((pack, HEAD_DIM), lambda g: (0, first + g))
    return call(
        "query_back", body,
        [queries, grad_mixed, mixed, keys, values, lse, q_low, q_high, k_stream, query_raw, gain, cos, sin, *earlier],
        [
            col, col, col, key, key,
            pl.BlockSpec((GROUPS, 8, rows), lambda g: (first + g, 0, 0)),
            whole((rows, 1)), whole((rows, 1)), whole((1, pack)),
            col, whole((1, HEAD_DIM)), whole((rows, HEAD_DIM)), whole((rows, HEAD_DIM)),
        ]
        + [ANY] * len(earlier),
        [col, whole((1, HEAD_DIM))],
        [shape((rows, HEADS * HEAD_DIM), BF16), shape((1, HEAD_DIM), F32)],
        grid=(count,),
        scratch=[pltpu.VMEM((rows, pack), F32)],
        aliases={13: 0} if earlier else None,
    )


def key_back(
    queries, grad_mixed, keys, values, far, q_low, q_high, k_stream, key_raw, gain, cos, sin,
    ctx_at, ctx_size, first, count, earlier=(),
):
    pack = queries.shape[0]
    rows = pack // ctx_size
    half = rows // 2
    pair = GROUPS * HEAD_DIM

    def body(
        at_ref, q_ref, do_ref, k_ref, v_ref, far_ref, lo_ref, hi_ref, ks_ref, raw_ref, g_ref,
        c_ref, s_ref, *rest,
    ):
        out_ref, gg_ref, bias, acc = rest[len(earlier) :]

        @pl.when(pl.program_id(0) == 0)
        def _():
            ks = ks_ref[...]
            ok = (ks >= lo_ref[...]) & (ks <= hi_ref[...])
            bias[...] = jnp.where(ok, 0.0, MASKED)
            gg_ref[...] = jnp.zeros_like(gg_ref)

        k_own = k_ref[...].reshape(rows, HEAD_DIM)
        v_own = v_ref[...].reshape(rows, HEAD_DIM)
        for j in range(GROUPS):
            cols = slice(j * HEAD_DIM, (j + 1) * HEAD_DIM)
            head = GROUPS * (first + pl.program_id(0)) + j
            lse, delta, factors = [far_ref[pl.ds(i * HEADS + head, 1), :] for i in range(3)]
            for late in range(2):
                there = slice(late * pack // 2, (late + 1) * pack // 2)
                here = slice(0, rows if late else half)
                qq, dd = q_ref[there, cols], do_ref[there, cols]
                factor = factors[:, there]
                scores = mm_nt(k_own[here], qq) * (factor * (SCALE * LOG2E)) + bias[here, there]
                probs = jnp.exp2(scores - lse[:, there])
                d_probs = mm_nt(v_own[here], dd)
                d_scores = (probs * factor * (d_probs - delta[:, there])).astype(BF16)
                dv = mm(probs.astype(BF16), dd)
                dk = mm(d_scores, qq)
                if j == 0 and late == 0:
                    acc[...] = jnp.zeros_like(acc)
                acc[0, here, :] += dk
                acc[1, here, :] += dv
        out_ref[1] = acc[1].astype(BF16)
        dk = acc[0] * SCALE
        dk = dk * c_ref[...] - turn(dk) * s_ref[...]
        dk, terms = head_norm_back(raw_ref[...].astype(F32).reshape(rows, HEAD_DIM), g_ref[...], dk)
        out_ref[0] = dk.astype(BF16)
        gg_ref[...] += jnp.sum(terms, axis=0, keepdims=True)

    col = pl.BlockSpec((pack, pair), lambda g, at: (0, first + g))
    key = pl.BlockSpec((2, 1, half, HEAD_DIM), lambda g, at: (0, at[0], 0, first + g))
    laid = (2, ctx_size, half, KV_HEADS * HEAD_DIM)
    return call(
        "key_back", body,
        [
            queries, grad_mixed, keys.reshape(laid), values.reshape(laid), far, q_low, q_high, k_stream, key_raw.reshape(laid), gain, cos, sin, *earlier,
        ],
        [
            col, col, key, key, whole(far.shape), whole((1, pack)), whole((1, pack)), whole((rows, 1)),
            key, whole((1, HEAD_DIM)), whole((rows, HEAD_DIM)), whole((rows, HEAD_DIM)),
        ]
        + [ANY] * len(earlier),
        [pl.BlockSpec((2, rows, HEAD_DIM), lambda g, at: (0, 0, first + g)), whole((1, HEAD_DIM))],
        [shape((2, rows, KV_HEADS * HEAD_DIM), BF16), shape((1, HEAD_DIM), F32)],
        grid=(count,),
        scratch=[pltpu.VMEM((rows, pack), F32), pltpu.VMEM((2, rows, HEAD_DIM), F32)],
        prefetch=[ctx_at], aliases={12: 0} if earlier else None,
    )


def all_queries(x, weights, gain, cos, sin):
    rows, width = x.shape
    cols = HEADS * HEAD_DIM
    block = 2 * HEAD_DIM
    part = 256

    def body(x_ref, w_ref, g_ref, c_ref, s_ref, rot_ref):
        g = twice(g_ref)
        for i in range(rows // part):
            here = slice(i * part, (i + 1) * part)
            raw = mm(x_ref[here, :], w_ref[...])
            c, s = [jnp.concatenate([r[here, :]] * 2, axis=1) for r in (c_ref, s_ref)]
            rot_ref[here, :] = rotated(raw * g, c, s).astype(BF16)

    return call(
        "all_queries", body, [x, weights, gain, cos, sin],
        [IN_VMEM, pl.BlockSpec((width, block), lambda j: (0, j)), IN_VMEM, IN_VMEM, IN_VMEM],
        [pl.BlockSpec((rows, block), lambda j: (0, j))], [shape((rows, cols), BF16)],
        grid=(cols // block,),
    )[0]


def all_grad_mixed(own, parcels, stack, places, ctx_at, rows):
    count = (len(parcels) + 1) // 2
    numbers = parcels[0].shape[0] - rows
    half = rows // 2
    inner = own.shape[1]
    _, _, width = stack.shape
    owners = stack.shape[0]
    unit = width // owners

    def body(places_ref, at_ref, own_ref, a_ref, b_ref, *refs):
        blocks, (out_ref, far_ref, turned) = refs[:-3], refs[-3:]
        step = pl.program_id(0)
        me = at_ref[0]

        def spread(ref):
            both = ref[rows:, :rows].astype(F32) + ref[rows:, rows : 2 * rows].astype(F32)
            far_ref[0, 0] = both[:, :half]
            far_ref[1, 0] = both[:, half:]

        @pl.when(step == 0)
        def _():
            spread(blocks[0])
            out_ref[...] = own_ref[...].reshape(2, 1, half, inner)
            turned[...] = jnp.concatenate([a_ref[...], b_ref[...]], axis=1).reshape(inner, width)

        def write(ref):
            spread(ref)
            for j in range(inner // 512):
                at = slice(j * 512, (j + 1) * 512)
                part = mm_nt(ref[:rows, :], turned[at, :]).astype(BF16)
                out_ref[:, :, :, at] = part.reshape(2, 1, half, 512)

        for s in range(1, count):

            @pl.when((step == s) & (me >= s))
            def _():
                write(blocks[s])

            @pl.when((step == s) & (me < s))
            def _():
                write(blocks[count - 1 + count - s])

    return call(
        "all_grad_mixed", body, [own, stack, stack, *parcels],
        [
            IN_VMEM,
            pl.BlockSpec((owners, unit, width), lambda *_: (0, 9, 0)),
            pl.BlockSpec((owners, unit, width), lambda *_: (0, 10, 0)),
        ]
        + [IN_VMEM] * len(parcels),
        [
            pl.BlockSpec((2, 1, half, inner), lambda k, at, me: (0, at[k], 0, 0)),
            pl.BlockSpec((2, 1, numbers, half), lambda k, at, me: (0, at[k], 0, 0)),
        ],
        [shape((2, count, half, inner), BF16), shape((2, count, numbers, half), F32)],
        grid=(count,), scratch=[pltpu.VMEM((inner, width), BF16)], prefetch=[places, ctx_at], vmem=32,
    )


def normed_back(d_queries, d_pair, weights):
    rows, inner = d_queries.shape
    cols = d_pair.shape[2]
    width = weights.shape[0]

    def body(dq_ref, pair_ref, wq_ref, wk_ref, wv_ref, out_ref):
        part = mm_nt(dq_ref[...], wq_ref[...])
        part += mm_nt(pair_ref[0], wk_ref[...])
        part += mm_nt(pair_ref[1], wv_ref[...])
        out_ref[...] = part

    block = 256
    return call(
        "normed_back", body, [d_queries, d_pair, weights, weights, weights],
        [
            IN_VMEM,
            IN_VMEM,
            pl.BlockSpec((block, inner), lambda j: (j, 0)),
            pl.BlockSpec((block, cols), lambda j: (j, inner // cols)),
            pl.BlockSpec((block, cols), lambda j: (j, inner // cols + 1)),
        ],
        [pl.BlockSpec((rows, block), lambda j: (0, j))],
        [shape((rows, width), F32)],
        grid=(width // block,),
    )[0]


def input_back(d_normed, tokens, gain, grad_middle):
    rows, width = tokens.shape

    def body(a_ref, t_ref, gain_ref, gm_ref, out_ref, gg_ref):
        back, terms = norm_back(t_ref[...].astype(F32), gain_ref[...], a_ref[...])
        out_ref[...] = (gm_ref[...] + back).astype(BF16)
        gg_ref[...] = jnp.sum(terms, axis=0, keepdims=True)

    return call(
        "input_back", body, [d_normed, tokens, gain, grad_middle],
        [IN_VMEM] * 4,
        [whole((rows, width)), IN_VMEM],
        [shape((rows, width), BF16), shape((1, width), F32)],
    )


def weight_grad(left, right, owners=None, cols=None, block=512, apart=False, beside=False):
    tokens, rows = left.shape
    count = 1 if owners is None else owners.shape[0]
    unit = rows // count
    deep = right.ndim == 3
    first, each = cols or (0, right.shape[-1])
    width = each * (right.shape[0] if deep else 1)
    steps = width // block
    split = owners is not None
    results = 2 * (right.shape[0] if apart else 1) if split else 1

    def body(*refs):
        if split:
            own_ref, refs = refs[0], refs[1:]
        l_ref, r_ref, refs = refs[0], refs[1], refs[2:]
        outs, scratch = refs[:results], refs[results:]

        @pl.when(pl.program_id(0) == 0)
        def _():
            scratch[0][...] = l_ref[...].T
            for k in range(count if split else 0):
                at = pl.multiple_of(own_ref[k] * unit, unit)
                scratch[1][k * unit : (k + 1) * unit, :] = scratch[0][pl.ds(at, unit), :]

        def block_at(j):
            if deep:
                per = each // block
                return r_ref[j // per, :, pl.ds(pl.multiple_of(first + (j % per) * block, block), block)]
            return r_ref[:, pl.ds(pl.multiple_of(first + j * block, block), block)]

        if not split:
            outs[0][...] = mm(scratch[0][...], block_at(pl.program_id(0))).astype(BF16)
            return
        per = each // block
        for j in range(steps):
            at = 2 * (j // per) if apart else 0
            to = slice((j % per) * block, (j % per + 1) * block) if apart else slice(j * block, (j + 1) * block)
            for side in range(2):
                here = slice(side * rows // 2, (side + 1) * rows // 2)
                part = mm(scratch[1][here, :], block_at(j)).astype(BF16)
                part = part.reshape(count // 2, unit, block)
                if beside:
                    outs[side][:, :, to] = part[:, : unit // 2]
                    outs[side][:, :, width + j * block : width + (j + 1) * block] = part[:, unit // 2 :]
                else:
                    outs[at + side][:, :, to] = part

    if split:
        out = [IN_VMEM] * results
        dims = (count // 2, unit // 2, 2 * width) if beside else (count // 2, unit, each if apart else width)
        out_shape = [shape(dims, BF16)] * results
    else:
        out = [pl.BlockSpec((rows, block), lambda j: (0, j))]
        out_shape = [shape((rows, width), BF16)]
    return call(
        "weight_grad", body, [left, right], [IN_VMEM] * 2, out, out_shape,
        grid=(1 if split else steps,),
        scratch=[pltpu.VMEM((rows, tokens), BF16)] * (1 + split),
        prefetch=[owners] if split else (),
    )


def fold(items, steps=1):
    arrays = []

    def slot(term):
        for i, known in enumerate(arrays):
            if known is term:
                return i
        arrays.append(term)
        return len(arrays) - 1

    laid = [([slot(t) for t in terms], rows, bit) for terms, rows, bit in items]
    in_specs = []
    for a in arrays:
        in_specs.append(
            IN_VMEM if steps == 1 else pl.BlockSpec(a.shape[:2] + (a.shape[2] // steps,), lambda j: (0, 0, j))
        )
    out_specs, out_shape = [], []
    for slots, (_, rows), bit in laid:
        many, _, cols = arrays[slots[0]].shape
        dims = (many, rows, cols) if bit is None else (many // 2, rows, cols)
        for _ in range(1 if bit is None else 2):
            out_specs.append(
                IN_VMEM if steps == 1 else pl.BlockSpec(dims[:2] + (cols // steps,), lambda j: (0, 0, j))
            )
            out_shape.append(shape(dims, BF16))

    def body(*refs):
        ins, outs = refs[: len(arrays)], list(refs[len(arrays) :])
        for slots, (first, rows), bit in laid:
            here = slice(first, first + rows)
            many = arrays[slots[0]].shape[0]

            def total(k):
                value = ins[slots[0]][k, here, :].astype(F32)
                for at in slots[1:]:
                    value = value + ins[at][k, here, :].astype(F32)
                return value.astype(BF16)

            if bit is None:
                out = outs.pop(0)
                for k in range(many):
                    out[k] = total(k)
                continue
            sent, kept = outs.pop(0), outs.pop(0)
            places = [0, 0]
            for k in range(many):
                with_bit = (k >> bit) & 1
                (sent if with_bit else kept)[places[with_bit]] = total(k)
                places[with_bit] += 1

    return call("fold", body, arrays, in_specs, out_specs, out_shape, grid=(steps,))


def choose(first, second, dims, odd):
    arrays = [a for a, _ in first + second]
    views = [v for _, v in first + second]

    def body(odd_ref, *refs):
        ins, (sent, kept) = refs[: len(arrays)], refs[len(arrays) :]

        def total(begin, end):
            value = ins[begin][views[begin]].astype(F32)
            for at in range(begin + 1, end):
                value = value + ins[at][views[at]].astype(F32)
            return value.astype(BF16)

        @pl.when(odd_ref[0] == 1)
        def _():
            sent[...] = total(0, len(first))
            kept[...] = total(len(first), len(arrays))

        @pl.when(odd_ref[0] == 0)
        def _():
            kept[...] = total(0, len(first))
            sent[...] = total(len(first), len(arrays))

    return call(
        "choose", body, arrays, [IN_VMEM] * len(arrays), [IN_VMEM] * 2, [shape(dims, BF16)] * 2,
        prefetch=[odd],
    )


def place(sums, odd, out_dims, cuts):
    arrays = [a for pair in sums for a in pair]

    def body(odd_ref, *refs):
        ins, outs = refs[: len(arrays)], refs[len(arrays) :]

        def write(swapped):
            for which, half, source, at, target in cuts:
                outs[at][target] = ins[2 * which + (half ^ swapped)][source].astype(F32)

        @pl.when(odd_ref[0] == 1)
        def _():
            write(1)

        @pl.when(odd_ref[0] == 0)
        def _():
            write(0)

    return call(
        "place", body, arrays, [IN_VMEM] * len(arrays), [whole(d) for d in out_dims],
        [shape(d, F32) for d in out_dims], prefetch=[odd],
    )


def swap(x, axis, bit):
    size = lax.axis_size(axis)
    return lax.ppermute(x, axis, [(i, i ^ bit) for i in range(size)])


def bits_of(size):
    return [1 << b for b in range(size.bit_length() - 1)]


def gather_pieces(own, cut):
    rest = bits_of(lax.axis_size("dp"))[1:]
    spans = [slice(0, cut), slice(cut, own.shape[1])]
    everything = slice(0, own.shape[1])
    held = {0: [(everything, own)]}
    for bit in rest:
        held[bit] = [(everything, swap(own, "dp", bit))]
    first = [held[bit][0][1] for bit in rest]
    for at in range(1 << len(rest)):
        at = 2 * at
        if at in held:
            continue
        held[at] = []
        for span, order in zip(spans, (rest, rest[::-1])):
            last = [bit for bit in order if at & bit][-1]
            before = held[at ^ last]
            source = before[0][1][:, span] if len(before) == 1 else before[spans.index(span)][1]
            held[at].append((span, swap(source, "dp", last)))
    for at in sorted(held):
        held[at | 1] = [(span, swap(piece, "dp", 1)) for span, piece in held[at]]
    return held, first


class Sum:
    def __init__(self, kept, sent, halves, odd):
        self.rest = bits_of(lax.axis_size("dp"))[1:]
        self.order = [list(range(len(self.rest))), list(range(len(self.rest)))[::-1]]
        self.left = [list(range(len(self.rest))), list(range(len(self.rest)))]
        self.odd = odd
        arrived = [swap(s, "dp", 1) for s in sent]
        if len(kept) == 1:
            kept, arrived = kept * 2, arrived * 2
        self.terms = [[k, a] for k, a in zip(kept, arrived)]
        self.rows = halves
        self.stage = 0

    def over_dp(self, steps=1):
        bits = [order[self.stage] for order in self.order]
        items = [
            (terms, rows, left.index(bit))
            for terms, rows, left, bit in zip(self.terms, self.rows, self.left, bits)
        ]
        sent0, kept0, sent1, kept1 = fold(items, steps)
        self.terms = [
            [kept, swap(sent, "dp", self.rest[bit])]
            for kept, sent, bit in zip((kept0, kept1), (sent0, sent1), bits)
        ]
        self.rows = [(0, k.shape[1]) for k in (kept0, kept1)]
        for left, bit in zip(self.left, bits):
            left.remove(bit)
        self.stage += 1

    def joined(self):
        dims = [terms[0].shape[1:] for terms in self.terms]
        arrays = [term for terms in self.terms for term in terms]
        many = len(self.terms[0])

        def body(*refs):
            at = 0
            for part, (rows, _) in enumerate(dims):
                value = refs[part * many][0].astype(F32)
                for k in range(1, many):
                    value = value + refs[part * many + k][0].astype(F32)
                refs[-1][at : at + rows, :] = value.astype(BF16)
                at += rows

        total = (sum(rows for rows, _ in dims), dims[0][1])
        return call(
            "joined", body, arrays, [IN_VMEM] * len(arrays), [IN_VMEM], [shape(total, BF16)]
        )[0]

    def to_ctx(self):
        first, second = [[(t, 0) for t in terms] for terms in self.terms]
        self.begin_ctx(first, second, first[0][0].shape[1:])

    def begin_ctx(self, first, second, dims):
        sent, kept = choose(first, second, dims, self.odd)
        self.total, self.next = [kept, swap(sent, "ctx", 1)], bits_of(lax.axis_size("ctx"))[1:]

    def over_ctx(self):
        a, b = [t[None] for t in self.total]
        total = fold([([a, b], (0, a.shape[1]), None)])[0][0]
        if self.next:
            self.total = [total, swap(total, "ctx", self.next.pop(0))]
        else:
            self.total = [total, swap(total, "ctx", 1)]


class Line:
    def __init__(self, total):
        size = lax.axis_size("ctx")
        middle = size // 2
        self.hops = [("add", [(k, k + 1), (size - 1 - k, size - 2 - k)]) for k in range(middle - 1)]
        self.hops.append(("add", [(middle - 1, middle), (middle, middle - 1)]))
        for k in reversed(range(middle - 1)):
            self.hops.append(("take", [(k + 1, k), (size - 2 - k, size - 1 - k)]))
        self.total = total
        self.send()

    def send(self):
        self.kind, pairs = self.hops.pop(0)
        self.takers = [b for _, b in pairs]
        self.came = lax.ppermute(self.total, "ctx", pairs)

    def taking(self):
        at = lax.axis_index("ctx")
        return sum((at == taker).astype(jnp.int32) for taker in self.takers)[None]

    def step(self):
        if self.kind == "add":
            rows = self.total.shape[0]
            self.total = fold([([self.total[None], self.came[None]], (0, rows), None)])[0][0]
        else:
            self.total = jnp.where(self.taking()[0] == 1, self.came, self.total)
        self.send()

    def finish(self):
        while self.hops:
            self.step()

    def place(self, out_dims, cuts):
        cuts = [(0, 0, source, at, target) for source, at, target in cuts]
        if self.kind == "add":
            self.total, self.came = fold([([self.total[None], self.came[None]], (0, self.total.shape[0]), None)])[0][0], self.total
            return place([(self.total, self.came)], jnp.zeros((1,), jnp.int32), out_dims, cuts)
        return place([(self.total, self.came)], self.taking(), out_dims, cuts)


class Relay:
    def __init__(self, block):
        self.size = lax.axis_size("ctx")
        self.from_left, self.from_right = [], []
        self.send(block, block)

    def send(self, right, left):
        step = len(self.from_left)
        self.from_left.append(lax.ppermute(right, "ctx", [(i, i + 1) for i in range(step, self.size - 1)]))
        self.from_right.append(
            lax.ppermute(left, "ctx", [(i + 1, i) for i in range(self.size - 1 - step)])
        )

    def step(self):
        came = [self.from_left[-1], self.from_right[-1]]
        self.send(
            *copies(
                "pass_on", came, lambda _, ins, outs: list(zip(ins, outs)),
                [shape(c.shape, c.dtype) for c in came],
            )
        )

    def finish(self):
        while len(self.from_left) < self.size - 1:
            self.step()


def sum_everywhere(x):
    for axis in ("dp", "ctx"):
        for bit in bits_of(lax.axis_size(axis)):
            x = x + swap(x, axis, bit)
    return x


def on_device(
    tokens, doc_starts, attn_gain, w_query, w_key, w_value, w_out,
    query_gain, key_gain, mlp_gain, w_gate, w_up, w_down, cotangent,
):
    ORDER.clear()
    rows, width = tokens.shape[1], tokens.shape[2]
    stretch = rows // 2
    ctx_size = lax.axis_size("ctx")
    dp_size = lax.axis_size("dp")
    ctx_at = lax.axis_index("ctx")
    dp_at = lax.axis_index("dp")
    pack_rows = rows * ctx_size
    unit = width // dp_size
    inner = HEADS * HEAD_DIM
    own_tokens = tokens[0]
    grad_out = cotangent[0]
    starts = doc_starts[0]
    odd = (ctx_at % 2).astype(jnp.int32)[None]
    dp_bits = bits_of(dp_size)

    gains = jnp.concatenate(
        [attn_gain[:, None], mlp_gain[:, None], jnp.zeros((unit, HEAD_DIM - 2), BF16)], axis=1
    )

    def packing(_, ins, outs):
        at = 0
        for ref in ins:
            yield ref.at[:, :], outs[0].at[:, pl.ds(at, ref.shape[1])]
            at += ref.shape[1]

    def stacking(_, ins, outs):
        down, gate, up, out = ins
        stack_ref = outs[0]
        yield down.at[:, :], stack_ref.at[pl.ds(0, 3 * unit)]
        for i in range(3):
            cols = pl.ds(i * width, width)
            yield gate.at[:, cols], stack_ref.at[pl.ds((3 + i) * unit, unit)]
            yield up.at[:, cols], stack_ref.at[pl.ds((6 + i) * unit, unit)]
        yield out.at[:, :], stack_ref.at[pl.ds(9 * unit, 2 * unit)]

    attn_cols = inner + 2 * width + HEAD_DIM
    own_attn = copies(
        "pack_attn", [w_query, w_key, w_value, gains], packing, [shape((unit, attn_cols), BF16)],
        in_specs=[whole(w.shape) for w in (w_query, w_key, w_value)] + [IN_VMEM],
    )[0]
    pieces, first_pieces = gather_pieces(own_attn, inner)
    gathered = Relay(own_tokens)
    stack_in = copies(
        "pack_stack", [w_down, w_gate, w_up, w_out], stacking, [shape((11 * unit, width), BF16)],
        in_specs=[whole(w.shape) for w in (w_down, w_gate, w_up, w_out)],
        out_specs=[whole((11 * unit, width))],
    )[0]
    stack = lax.all_gather(stack_in, "dp", axis=0)
    gathered.step()
    touch(first_pieces)
    gathered.finish()
    from_left, from_right = gathered.from_left, gathered.from_right

    place_at = jnp.arange(pack_rows, dtype=jnp.int32)
    in_half = place_at % (pack_rows // 2)
    part, device, row = place_at // (pack_rows // 2), in_half // stretch, place_at % stretch
    key_stream = stream_index(device * rows + part * stretch + row, stretch, ctx_size)
    query_stream = stream_index(
        ctx_at * rows + jnp.arange(rows, dtype=jnp.int32), stretch, ctx_size
    )
    key_open = opening_of(key_stream, starts)
    query_open = opening_of(query_stream, starts)
    cos_pack, sin_pack = rotary(key_stream - key_open)
    cos_own, sin_own = rotary(query_stream - query_open)

    owners = (dp_at ^ jnp.arange(dp_size, dtype=jnp.int32)).astype(jnp.int32)
    listed = [(k, span, piece) for k in range(dp_size) for span, piece in pieces[k]]

    def assembling(prefetch, ins, outs):
        for (k, span, _), ref in zip(listed, ins):
            at = pl.multiple_of(prefetch[0][k] * unit, unit)
            cols = pl.ds(span.start, span.stop - span.start)
            yield ref.at[:, :], outs[0].at[pl.ds(at, unit), cols]
            if span.stop == attn_cols:
                last = ref.shape[1] - HEAD_DIM
                yield ref.at[:, pl.ds(last, HEAD_DIM)], outs[1].at[pl.ds(at, unit), :]

    attn_w, gain_cols = copies(
        "assemble_weights", [piece for _, _, piece in listed], assembling,
        [shape((width, attn_cols), BF16), shape((width, HEAD_DIM), BF16)], prefetch=[owners],
        out_specs=[whole((width, attn_cols)), IN_VMEM],
    )
    gain_rows = gain_cols[:, :2].astype(F32).T
    gain_attn, gain_mlp = gain_rows[0:1], gain_rows[1:2]
    gain_query = query_gain.astype(F32)[None, :]
    gain_key = key_gain.astype(F32)[None, :]

    normed = norm_own(own_tokens, gain_attn)
    query_raw, queries, factors = project_queries(normed, attn_w, gain_query, cos_own, sin_own)
    places = ((ctx_at - jnp.arange(ctx_size, dtype=jnp.int32)) % ctx_size).astype(jnp.int32)
    normed_pack = norm_pack(
        own_tokens, from_left, from_right, gain_attn, places, ctx_at.astype(jnp.int32)[None]
    ).reshape(pack_rows, width)
    key_raw, keys, values = project_keys_values(normed_pack, attn_w, gain_key, cos_pack, sin_pack)
    mixed, lse = attend(
        queries, keys, values, query_open[:, None], query_stream[:, None], key_stream[None, :]
    )
    output, normed_mid, hidden, d_both, middle = feed_forward(
        mixed, own_tokens, grad_out, gain_mlp, stack
    )

    order = [2 * k for k in range(dp_size // 2)] + [2 * k + 1 for k in range(dp_size // 2)]
    owners = (dp_at ^ jnp.array(order, jnp.int32)).astype(jnp.int32)
    everything = slice(None)
    ctx_steps = len(bits_of(ctx_size))
    later_dp, later_ctx = len(dp_bits) - 2, ctx_steps - 1

    def two_rows(total, half, widths=(width,)):
        cuts, at = [], 0
        for which, each in enumerate(widths):
            for k in range(2):
                to = (slice(k * half, (k + 1) * half), everything)
                cuts.append((0, k, (everything, slice(at, at + each)), which, to))
            at += each
        return place([total.total], odd, [(2 * half, each) for each in widths], cuts)

    def halves_of(pair):
        half = pair[0].shape[1] // 2
        return Sum(pair[:1], pair[1:], [(0, half), (half, half)], odd), half

    half_heads = KV_HEADS // 2
    down, down_half = halves_of(weight_grad(hidden, grad_out, owners))
    wide_grad = weight_grad(normed_mid, d_both, block=1024)[0]
    wide_grad = lax.psum_scatter(wide_grad, "dp", scatter_dimension=0, tiled=True)
    down.over_dp()
    grad_middle, grad_branch, mlp_part, grad_mixed, parcel = branch_back(
        d_both, middle, grad_out, gain_mlp, mixed, lse, factors, stack
    )
    parcels = Relay(parcel)
    for _ in range(later_dp):
        down.over_dp()
    out_kept, out_sent = weight_grad(mixed, grad_branch, owners, beside=True)
    query_args = (
        queries, grad_mixed, mixed, keys, values, lse, query_open[:, None], query_stream[:, None],
        key_stream[None, :], query_raw, gain_query, cos_own, sin_own,
    )
    d_query, query_part = query_back(*query_args, 0, half_heads)
    parcels.step()
    down = Line(down.joined())
    d_query, query_more = query_back(*query_args, half_heads, half_heads, (d_query,))
    parcels.finish()
    down.step()
    query_kept, query_sent = weight_grad(normed, d_query, owners)
    outer = Sum([out_kept, query_kept], [out_sent, query_sent], [(0, unit), (0, unit)], odd)
    wide_grad = copies(
        "take", [wide_grad], lambda _, ins, outs: [(ins[0], outs[0])], [shape(wide_grad.shape, BF16)]
    )[0]
    wide = Line(wide_grad)
    every_query = all_queries(normed_pack, attn_w, gain_query, cos_pack, sin_pack)
    touch([parcels.from_left[-1], parcels.from_right[-1]])
    down.finish()
    outer.over_dp()
    parcels = [parcel] + parcels.from_left + parcels.from_right
    grad_mixed_pack, far = all_grad_mixed(
        grad_mixed, parcels, stack, places, ctx_at.astype(jnp.int32)[None], rows
    )
    grad_mixed_pack = grad_mixed_pack.reshape(pack_rows, inner)
    far = far.transpose(2, 0, 1, 3).reshape(3 * HEADS, pack_rows)
    key_args = (
        every_query, grad_mixed_pack, keys, values, far,
        key_open[None, :], key_stream[None, :], query_stream[:, None],
        key_raw, gain_key, cos_own, sin_own, ctx_at.astype(jnp.int32)[None], ctx_size,
    )
    wide.step()
    d_pair, key_part = key_back(*key_args, 0, half_heads)
    for _ in range(later_dp):
        outer.over_dp()
    down_grad = down.place([(2 * down_half, width)], [(everything, 0, everything)])[0]
    d_pair, key_more = key_back(*key_args, half_heads, half_heads, (d_pair,))
    query_part, key_part = query_part + query_more, key_part + key_more
    outer = Line(outer.joined())
    key_kept, key_sent, value_kept, value_sent = weight_grad(normed, d_pair, owners, apart=True)
    pair = Sum([key_kept, value_kept], [key_sent, value_sent], [(0, unit), (0, unit)], odd)
    wide.finish()
    d_normed = normed_back(d_query, d_pair, attn_w)
    pair.over_dp()
    input_grad, attn_part = input_back(d_normed, own_tokens, gain_attn, grad_middle)
    for _ in range(later_dp):
        pair.over_dp()
    outer.step()
    gate_grad, up_grad = wide.place(
        [(unit, 3 * width)] * 2,
        [((everything, slice(k * 3 * width, (k + 1) * 3 * width)), k, everything) for k in range(2)],
    )
    pair.to_ctx()
    outer.finish()
    pair.over_ctx()
    near, far_half = slice(0, width), slice(width, 2 * width)
    first, second = slice(0, unit), slice(unit, 2 * unit)
    w_out_grad, query_grad = outer.place(
        [(2 * unit, width), (unit, inner)],
        [
            ((first, near), 0, (first, everything)),
            ((first, far_half), 0, (second, everything)),
            ((second, everything), 1, everything),
        ],
    )
    for _ in range(later_ctx):
        pair.over_ctx()
    key_grad, value_grad = place(
        [pair.total], odd, [(unit, width)] * 2, [(0, k, everything, k, everything) for k in range(2)]
    )

    parts = [attn_part, mlp_part, query_part, key_part]
    small = sum_everywhere(jnp.concatenate(parts, axis=1).reshape(-1, HEAD_DIM)).reshape(-1)
    attn_gain_grad = lax.dynamic_slice(small, (dp_at * unit,), (unit,))
    mlp_gain_grad = lax.dynamic_slice(small, (width + dp_at * unit,), (unit,))
    query_gain_grad = small[2 * width : 2 * width + HEAD_DIM]
    key_gain_grad = small[2 * width + HEAD_DIM :]
    return (
        output[None], input_grad[None], attn_gain_grad, query_grad, key_grad, value_grad, w_out_grad,
        query_gain_grad, key_gain_grad, mlp_gain_grad, gate_grad, up_grad, down_grad,
    )


def solution(mesh):
    in_specs = (
        P("dp", "ctx", None),
        P("dp", None),
        P("dp"),
        P("dp", None),
        P("dp", None),
        P("dp", None),
        P("dp", None),
        P(),
        P(),
        P("dp"),
        P("dp", None),
        P("dp", None),
        P("dp", None),
        P("dp", "ctx", None),
    )
    out_specs = (
        P("dp", "ctx", None),
        P("dp", "ctx", None),
        P("dp"),
        P("dp", None),
        P("dp", None),
        P("dp", None),
        P("dp", None),
        P(),
        P(),
        P("dp"),
        P("dp", None),
        P("dp", None),
        P("dp", None),
    )
    return jax.shard_map(
        on_device, mesh=mesh, in_specs=in_specs, out_specs=out_specs, check_vma=False
    )
```

```python
import functools
import math

import jax
import jax.numpy as jnp
from jax import lax
from jax.experimental import pallas as pl
from jax.experimental.pallas import tpu as pltpu
from jax.sharding import PartitionSpec as P

HEADS = 16
KV_HEADS = 8
HEAD_DIM = 128
GROUPS = HEADS // KV_HEADS

EPSILON = 1e-06
ROPE_BASE = 1000000.0
MASKED = -1e30
SCALE = HEAD_DIM ** (-0.5)

F32 = jnp.float32
BF16 = jnp.bfloat16
MIB = 1 << 20
VMEM_MIB = 20
LARGE = 1 << 18


ORDER = []


def shape(dims, dtype):
    return jax.ShapeDtypeStruct(dims, dtype)


ANY = pl.BlockSpec(memory_space=pl.ANY)
IN_VMEM = pl.BlockSpec(memory_space=pltpu.VMEM)
IN_HBM = pl.BlockSpec(memory_space=pltpu.HBM)


def in_hbm(spec, array):
    return spec not in (IN_VMEM, ANY, IN_HBM) and math.prod(array.shape) * 2 >= LARGE


def call(
    name, body, args, in_specs, out_specs, out_shape, grid=(1,), scratch=(), prefetch=(), aliases=None,
    after=(), vmem=VMEM_MIB,
):
    waits = list(ORDER) + list(after)
    wait_specs = [IN_VMEM] * len(ORDER) + [ANY] * len(after)
    taken = len(prefetch) + len(args)
    token = taken + len(waits) + len(out_shape)
    args = [
        pltpu.with_memory_space_constraint(a, pltpu.HBM) if in_hbm(s, a) else a
        for a, s in zip(args, in_specs)
    ]
    out_shape = [
        pltpu.HBM(o.shape, o.dtype) if in_hbm(s, o) else o for o, s in zip(out_shape, out_specs)
    ]

    def without(*refs):
        refs[token][...] = jnp.zeros_like(refs[token])
        body(*refs[:taken], *refs[taken + len(waits) : token], *refs[token + 1 :])

    results = pl.pallas_call(
        without,
        grid_spec=pltpu.PrefetchScalarGridSpec(
            num_scalar_prefetch=len(prefetch),
            grid=grid,
            in_specs=list(in_specs) + wait_specs,
            out_specs=list(out_specs) + [IN_VMEM],
            scratch_shapes=list(scratch),
        ),
        out_shape=out_shape + [shape((8, HEAD_DIM), F32)],
        input_output_aliases={len(prefetch) + i: o for i, o in (aliases or {}).items()},
        compiler_params=pltpu.CompilerParams(vmem_limit_bytes=vmem * MIB),
        cost_estimate=pl.CostEstimate(flops=0, bytes_accessed=0, transcendentals=0),
        name=name,
    )(*prefetch, *args, *waits)
    ORDER[:] = [results[-1]]
    return results[:-1]


def whole(dims):
    return pl.BlockSpec(dims, lambda *_: (0,) * len(dims))


def mm(a, b):
    return lax.dot_general(a, b, (((1,), (0,)), ((), ())), preferred_element_type=F32)


def mm_nt(a, b):
    return lax.dot_general(a, b, (((1,), (1,)), ((), ())), preferred_element_type=F32)


def mm_tn(a, b):
    return lax.dot_general(a, b, (((0,), (0,)), ((), ())), preferred_element_type=F32)


def mean_last(v):
    return jnp.sum(v, axis=-1, keepdims=True) * (1.0 / v.shape[-1])


def factor_of(v):
    return lax.rsqrt(mean_last(v * v) + EPSILON)


def norm_back(v, gain, incoming):
    f = factor_of(v)
    weighted = incoming * gain
    inner = mean_last(weighted * v)
    return f * weighted - v * (f * f * f * inner), incoming * v * f


def stream_index(row_ids, stretch_rows, ctx_size):
    slab_index = row_ids // (2 * stretch_rows)
    within = row_ids % (2 * stretch_rows)
    mirrored = (2 * ctx_size - 1 - slab_index) * stretch_rows + within - stretch_rows
    return jnp.where(within < stretch_rows, slab_index * stretch_rows + within, mirrored)


def opening_of(stream, starts):
    started = starts[None, :] <= stream[:, None]
    return jnp.max(jnp.where(started, starts[None, :], 0), axis=1)


def rotary(positions):
    half_dim = HEAD_DIM // 2
    inverse = jnp.exp(
        jnp.arange(half_dim, dtype=F32) * (-2.0 * math.log(ROPE_BASE) / HEAD_DIM)
    )
    angles = positions.astype(F32)[:, None] * inverse[None, :]
    cos_half, sin_half = jnp.cos(angles), jnp.sin(angles)
    return (
        jnp.concatenate([cos_half, cos_half], axis=1),
        jnp.concatenate([-sin_half, sin_half], axis=1),
    )


def copies(name, sources, plan, out_shape, prefetch=(), after=(), in_specs=None, out_specs=None):
    count = len(sources)
    first = len(prefetch)

    def body(*refs):
        ins = refs[first : first + count]
        for source, target in plan(refs[:first], ins, refs[first + count :]):
            target[...] = source[...]

    return call(
        name, body, sources, in_specs or [IN_VMEM] * count, out_specs or [IN_VMEM] * len(out_shape), out_shape,
        prefetch=prefetch, after=after,
    )


def touch(after):
    call("touch", lambda *_: None, [], [], [], [], after=after, vmem=4)


def norm_own(tokens, gain):
    def body(t_ref, g_ref, out_ref):
        x = t_ref[...].astype(F32)
        out_ref[...] = (x * factor_of(x) * g_ref[...]).astype(BF16)

    return call(
        "norm_own", body, [tokens, gain], [IN_VMEM] * 2, [IN_VMEM], [shape(tokens.shape, BF16)]
    )[0]


def norm_pack(own, from_left, from_right, gain, places, ctx_at):
    count = len(from_left) + 1
    rows, width = own.shape
    half = rows // 2

    def body(places_ref, at_ref, gain_ref, *refs):
        blocks, pack_ref = refs[:-1], refs[-1]
        step = pl.program_id(0)
        me = at_ref[0]

        def write(ref):
            x = ref[...].astype(F32)
            low = (x * factor_of(x) * gain_ref[...]).astype(BF16)
            pack_ref[...] = low.reshape(2, 1, half, width)

        @pl.when(step == 0)
        def _():
            write(blocks[0])

        for s in range(1, count):

            @pl.when((step == s) & (me >= s))
            def _():
                write(blocks[s])

            @pl.when((step == s) & (me < s))
            def _():
                write(blocks[count - 1 + count - s])

    blocks = [own] + from_left + from_right
    return call(
        "norm_pack", body, [gain] + blocks,
        [whole((1, width))] + [IN_VMEM] * len(blocks),
        [pl.BlockSpec((2, 1, half, width), lambda k, at, me: (0, at[k], 0, 0))],
        [shape((2, count, half, width), BF16)],
        grid=(count,), prefetch=[places, ctx_at],
    )[0]


def lane_sums(v):
    cols = v.shape[-1]
    head = lax.broadcasted_iota(jnp.int32, (cols, cols), 0) // HEAD_DIM
    same = (head == lax.broadcasted_iota(jnp.int32, (cols, cols), 1) // HEAD_DIM).astype(BF16)
    high = v.astype(BF16)
    low = (v - high.astype(F32)).astype(BF16)
    return mm(high, same) + mm(low, same)


def head_factors(raw):
    return lax.rsqrt(lane_sums(raw * raw) * (1.0 / HEAD_DIM) + EPSILON)


def turn(v):
    parts = [
        pltpu.roll(v[:, at : at + HEAD_DIM], HEAD_DIM // 2, 1) for at in range(0, v.shape[1], HEAD_DIM)
    ]
    return parts[0] if len(parts) == 1 else jnp.concatenate(parts, axis=1)


def rotated(v, cos, sin):
    return v * cos + turn(v) * sin


def rope(raw, gain, cos, sin):
    return rotated(raw * head_factors(raw) * gain, cos, sin)


def twice(ref):
    return jnp.concatenate([ref[...]] * 2, axis=1)


def project_queries(x, weights, gain, cos, sin):
    rows, width = x.shape
    cols = HEADS * HEAD_DIM
    block = 2 * HEAD_DIM
    each = 2 * block
    col = pl.BlockSpec((rows, each), lambda j: (0, j))

    def body(x_ref, w_ref, g_ref, c_ref, s_ref, raw_ref, rot_ref, fac_ref):
        g, c, s = twice(g_ref), twice(c_ref), twice(s_ref)
        for j in range(each // block):
            at = slice(j * block, (j + 1) * block)
            raw = mm(x_ref[...], w_ref[:, at])
            raw_ref[:, at] = raw.astype(BF16)
            factors = head_factors(raw)
            rot_ref[:, at] = rotated(raw * factors * g, c, s).astype(BF16)
            for h in range(2):
                fac_ref[2 * j + h] = factors[:, h * HEAD_DIM : (h + 1) * HEAD_DIM].T[:8]

    return call(
        "project_queries", body, [x, weights, gain, cos, sin],
        [IN_VMEM, pl.BlockSpec((width, each), lambda j: (0, j))] + [IN_VMEM] * 3,
        [col, col, pl.BlockSpec((each // HEAD_DIM, 8, rows), lambda j: (j, 0, 0))],
        [shape((rows, cols), BF16), shape((rows, cols), BF16), shape((HEADS, 8, rows), F32)],
        grid=(cols // each,),
    )


def project_keys_values(x, weights, gain, cos, sin):
    rows, width = x.shape
    block = 2 * HEAD_DIM
    cols = KV_HEADS * HEAD_DIM
    inner = HEADS * HEAD_DIM
    part = 256

    def body(x_ref, wk_ref, wv_ref, g_ref, c_ref, s_ref, raw_ref, rot_ref, val_ref):
        wk, wv = wk_ref[...], wv_ref[...]
        g = twice(g_ref)
        for i in range(rows // part):
            here = slice(i * part, (i + 1) * part)
            raw = mm(x_ref[here, :], wk)
            raw_ref[here, :] = raw.astype(BF16)
            val_ref[here, :] = mm(x_ref[here, :], wv).astype(BF16)
            c, s = [jnp.concatenate([r[here, :]] * 2, axis=1) for r in (c_ref, s_ref)]
            rot_ref[here, :] = rope(raw, g, c, s).astype(BF16)

    col = pl.BlockSpec((rows, block), lambda j: (0, j))
    return call(
        "project_keys_values", body, [x, weights, weights, gain, cos, sin],
        [
            IN_VMEM,
            pl.BlockSpec((width, block), lambda j: (0, inner // block + j)),
            pl.BlockSpec((width, block), lambda j: (0, (inner + cols) // block + j)),
        ]
        + [IN_VMEM] * 3,
        [col, col, col], [shape((rows, cols), BF16)] * 3, grid=(cols // block,),
    )


LOG2E = 1.4426950408889634


def attend(queries, keys, values, q_low, q_high, k_stream):
    rows = queries.shape[0]
    half = rows // 2
    pack = keys.shape[0]
    pair = GROUPS * HEAD_DIM

    def body(q_ref, k_ref, v_ref, lo_ref, hi_ref, ks_ref, mix_ref, lse_ref, bias):
        @pl.when(pl.program_id(0) == 0)
        def _():
            ks = ks_ref[...]
            ok = (ks >= lo_ref[...]) & (ks <= hi_ref[...])
            bias[...] = jnp.where(ok, 0.0, MASKED)

        v_ones = jnp.concatenate([v_ref[...], jnp.ones((pack, HEAD_DIM), BF16)], axis=1)
        for part in range(2):
            here = slice(part * half, (part + 1) * half)
            seen = pack // 2 if part == 0 else pack
            for j in range(GROUPS):
                cols = slice(j * HEAD_DIM, (j + 1) * HEAD_DIM)
                scores = mm_nt(q_ref[here, cols], k_ref[:seen, :]) * (SCALE * LOG2E) + bias[here, :seen]
                both = mm(jnp.exp2(scores).astype(BF16), v_ones[:seen])
                total = both[:, HEAD_DIM:]
                mix_ref[here, cols] = (both[:, :HEAD_DIM] * (1.0 / total)).astype(BF16)
                lse_ref[j, :, here] = jnp.log2(total).T[:8]

    col = pl.BlockSpec((rows, pair), lambda g: (0, g))
    key = pl.BlockSpec((pack, HEAD_DIM), lambda g: (0, g))
    return call(
        "attend", body, [queries, keys, values, q_low, q_high, k_stream],
        [col, key, key, whole((rows, 1)), whole((rows, 1)), whole((1, pack))],
        [col, pl.BlockSpec((GROUPS, 8, rows), lambda g: (g, 0, 0))],
        [shape((rows, HEADS * HEAD_DIM), BF16), shape((HEADS, 8, rows), F32)],
        grid=(KV_HEADS,),
        scratch=[pltpu.VMEM((rows, pack), F32)],
    )


def high_low(v):
    high = v.astype(BF16)
    return high, (v - high.astype(F32)).astype(BF16)


def middle_block(mixed, lse, factors, tokens, grad, gain, stack):
    rows, inner = mixed.shape
    count, height, width = stack.shape
    unit = width // count
    hidden = 3 * width
    block = 256
    per_row = block // unit if unit < block else 1

    def body(
        mixed_hbm, lse_ref, fac_ref, tok_hbm, dy_hbm, gain_ref, stack_ref,
        out_ref, low_ref, h_ref, both_ref, gm_ref, gb_ref, gg_ref, dm_ref, parcel_ref,
        w, mid, acc, deltas, mixed_ref, tok_ref, dy_ref, sems,
    ):
        def move(first, many, sem):
            here = (slice(None), pl.ds(first * unit, many * unit))
            return pltpu.make_async_copy(stack_ref.at[here], w.at[here], sems.at[sem])

        loads = [
            pltpu.make_async_copy(a, b, sems.at[8 + i])
            for i, (a, b) in enumerate(((mixed_hbm, mixed_ref), (tok_hbm, tok_ref), (dy_hbm, dy_ref)))
        ]
        loads[0].start()
        out_copy = move(9, 2, 0)
        gate_copies = [move(3 + i, 1, 1 + i) for i in range(3)]
        up_copies = [move(6 + i, 1, 4 + i) for i in range(3)]
        down_copy = move(0, 3, 7)
        out_copy.start()
        loads[1].start()
        loads[2].start()
        for a, b in zip(gate_copies, up_copies):
            a.start()
            b.start()
        down_copy.start()

        for load in loads:
            load.wait()
        out_copy.wait()
        for j in range(width // block):
            cols = slice(j * block, (j + 1) * block)
            part = w[:, 9 * unit : 11 * unit, cols].reshape(inner, block)
            mid[:, cols] = tok_ref[:, cols].astype(F32) + mm(mixed_ref[...], part)
        x = mid[...]
        low_ref[...] = (x * factor_of(x) * gain_ref[...]).astype(BF16)

        for i in range(3):
            gate_copies[i].wait()
            up_copies[i].wait()

            def forward(j, _):
                cols = pl.ds(pl.multiple_of(j * block, block), block)
                to = pl.ds(pl.multiple_of(i * width + j * block, block), block)
                g = mm(low_ref[...], w[:, (3 + i) * unit : (4 + i) * unit, cols].reshape(width, block))
                u = mm(low_ref[...], w[:, (6 + i) * unit : (7 + i) * unit, cols].reshape(width, block))
                s = 1.0 / (1.0 + jnp.exp(-g))
                act = g * s
                h_ref[:, to] = (act * u).astype(BF16)
                both_ref[0, :, to] = (u * (s + act * (1.0 - s))).astype(BF16)
                both_ref[1, :, to] = act.astype(BF16)
                return 0

            lax.fori_loop(0, width // block, forward, 0, unroll=True)

        down_copy.wait()
        acc[...] = mid[...]
        wide = 384
        owners = wide // (3 * unit)

        def down(j, _):
            cols = pl.ds(pl.multiple_of(j * wide, wide), wide)
            part = w[pl.ds(j * owners, owners), 0 : 3 * unit, :].reshape(wide, width)
            dh = mm_nt(dy_ref[...], part)
            both_ref[0, :, cols] = (both_ref[0, :, cols].astype(F32) * dh).astype(BF16)
            both_ref[1, :, cols] = (both_ref[1, :, cols].astype(F32) * dh).astype(BF16)
            acc[...] += mm(h_ref[:, cols], part)
            return 0

        lax.fori_loop(0, hidden // wide, down, 0, unroll=True)
        out_ref[...] = acc[...].astype(BF16)

        owners_in = block // unit
        for b in range(width // block):
            at = slice(b * owners_in, (b + 1) * owners_in)
            total = None
            for i in range(3):
                cols = slice(i * width, (i + 1) * width)
                for side in range(2):
                    first = (3 + 3 * side + i) * unit
                    part = w[at, first : first + unit, :].reshape(block, width)
                    term = mm_nt(both_ref[side, :, cols], part)
                    total = term if total is None else total + term
            acc[:, b * block : (b + 1) * block] = total

        back, terms = norm_back(mid[...], gain_ref[...], acc[...])
        grad_mid = dy_ref[...].astype(F32) + back
        gm_ref[...] = grad_mid
        gb_ref[...] = grad_mid.astype(BF16)
        gg_ref[...] = jnp.sum(terms, axis=0, keepdims=True)

        owners_out = block // (2 * unit)

        def mixed_back(j, _):
            cols = pl.ds(pl.multiple_of(j * block, block), block)
            part = w[pl.ds(j * owners_out, owners_out), 9 * unit : 11 * unit, :].reshape(block, width)
            dm = mm_nt(gb_ref[...], part).astype(BF16)
            dm_ref[:, cols] = dm
            terms = (dm.astype(F32) * mixed_ref[:, cols].astype(F32)).T
            for k in range(block // HEAD_DIM):
                delta = jnp.sum(terms[k * HEAD_DIM : (k + 1) * HEAD_DIM], axis=0, keepdims=True)
                deltas[pl.ds(j * (block // HEAD_DIM) + k, 1), :] = delta
            return 0

        lax.fori_loop(0, inner // block, mixed_back, 0, unroll=True)
        parcel_ref[:rows, :] = gb_ref[...]
        parcel_ref[rows:, :] = jnp.zeros((3 * HEADS, width), BF16)
        extras = (lse_ref[:, 0, :], deltas[...], fac_ref[:, 0, :])
        for which, values in enumerate(extras):
            at = rows + which * HEADS
            for side, piece in enumerate(high_low(values)):
                parcel_ref[at : at + HEADS, side * rows : (side + 1) * rows] = piece

    full = (rows, width)
    return call(
        "middle_block", body, [mixed, lse, factors, tokens, grad, gain, stack],
        [IN_HBM, whole(lse.shape), whole(factors.shape), IN_HBM, IN_HBM, whole((1, width)), IN_HBM],
        [whole(full), IN_VMEM, IN_VMEM, IN_VMEM, whole(full), IN_VMEM, IN_VMEM, whole((rows, inner)), IN_VMEM],
        [
            shape(full, BF16), shape(full, BF16), shape((rows, hidden), BF16),
            shape((2, rows, hidden), BF16), shape(full, F32), shape(full, BF16),
            shape((1, width), F32), shape((rows, inner), BF16), shape((rows + 3 * HEADS, width), BF16),
        ],
        scratch=[
            pltpu.VMEM((count, height, width), BF16),
            pltpu.VMEM(full, F32),
            pltpu.VMEM(full, F32),
            pltpu.VMEM((HEADS, rows), F32),
            pltpu.VMEM((rows, inner), BF16),
            pltpu.VMEM(full, BF16),
            pltpu.VMEM(full, BF16),
            pltpu.SemaphoreType.DMA((11,)),
        ],
        vmem=44,
    )


def head_norm_back(v, gain, incoming):
    f = head_factors(v)
    weighted = incoming * gain
    inner = lane_sums(weighted * v) * (1.0 / HEAD_DIM)
    return f * (weighted - v * (f * f * inner)), incoming * v * f


def query_back(
    queries, grad_mixed, mixed, keys, values, lse, q_low, q_high, k_stream, query_raw, gain, cos, sin,
    first, count, earlier=(),
):
    rows = queries.shape[0]
    half = rows // 2
    pack = keys.shape[0]
    pair = GROUPS * HEAD_DIM

    def body(
        q_ref, do_ref, mix_ref, k_ref, v_ref, lse_ref, lo_ref, hi_ref, ks_ref, raw_ref, g_ref, c_ref, s_ref,
        *rest,
    ):
        dq_ref, gg_ref, bias = rest[len(earlier) :]

        @pl.when(pl.program_id(0) == 0)
        def _():
            ks = ks_ref[...]
            ok = (ks >= lo_ref[...]) & (ks <= hi_ref[...])
            bias[...] = jnp.where(ok, 0.0, MASKED)
            gg_ref[...] = jnp.zeros_like(gg_ref)

        deltas = lane_sums(do_ref[...].astype(F32) * mix_ref[...].astype(F32))
        for j in range(GROUPS):
            cols = slice(j * HEAD_DIM, (j + 1) * HEAD_DIM)
            lse_col = jnp.broadcast_to(lse_ref[j, 0:1, :], (HEAD_DIM, rows)).T[:, :1]
            grads = []
            for part in range(2):
                here = slice(part * half, (part + 1) * half)
                seen = pack // 2 if part == 0 else pack
                scores = mm_nt(q_ref[here, cols], k_ref[:seen, :]) * (SCALE * LOG2E) + bias[here, :seen]
                probs = jnp.exp2(scores - lse_col[here])
                d_probs = mm_nt(do_ref[here, cols], v_ref[:seen, :])
                d_scores = (probs * (d_probs - deltas[here, cols][:, :1])).astype(BF16)
                grads.append(mm(d_scores, k_ref[:seen, :]))
            dq = jnp.concatenate(grads, axis=0) * SCALE
            dq = dq * c_ref[...] - turn(dq) * s_ref[...]
            dq, terms = head_norm_back(raw_ref[:, cols].astype(F32), g_ref[...], dq)
            dq_ref[:, cols] = dq.astype(BF16)
            gg_ref[...] += jnp.sum(terms, axis=0, keepdims=True)

    col = pl.BlockSpec((rows, pair), lambda g: (0, first + g))
    key = pl.BlockSpec((pack, HEAD_DIM), lambda g: (0, first + g))
    return call(
        "query_back", body,
        [queries, grad_mixed, mixed, keys, values, lse, q_low, q_high, k_stream, query_raw, gain, cos, sin, *earlier],
        [
            col, col, col, key, key,
            pl.BlockSpec((GROUPS, 8, rows), lambda g: (first + g, 0, 0)),
            whole((rows, 1)), whole((rows, 1)), whole((1, pack)),
            col, whole((1, HEAD_DIM)), whole((rows, HEAD_DIM)), whole((rows, HEAD_DIM)),
        ]
        + [ANY] * len(earlier),
        [col, whole((1, HEAD_DIM))],
        [shape((rows, HEADS * HEAD_DIM), BF16), shape((1, HEAD_DIM), F32)],
        grid=(count,),
        scratch=[pltpu.VMEM((rows, pack), F32)],
        aliases={13: 0} if earlier else None,
    )


def key_back(
    queries, grad_mixed, keys, values, far, q_low, q_high, k_stream, key_raw, gain, cos, sin,
    ctx_at, ctx_size, first, count, earlier=(),
):
    pack = queries.shape[0]
    rows = pack // ctx_size
    half = rows // 2
    pair = GROUPS * HEAD_DIM

    def body(
        at_ref, q_ref, do_ref, k_ref, v_ref, far_ref, lo_ref, hi_ref, ks_ref, raw_ref, g_ref,
        c_ref, s_ref, *rest,
    ):
        out_ref, gg_ref, bias, acc = rest[len(earlier) :]

        @pl.when(pl.program_id(0) == 0)
        def _():
            ks = ks_ref[...]
            ok = (ks >= lo_ref[...]) & (ks <= hi_ref[...])
            bias[...] = jnp.where(ok, 0.0, MASKED)
            gg_ref[...] = jnp.zeros_like(gg_ref)

        k_own = k_ref[...].reshape(rows, HEAD_DIM)
        v_own = v_ref[...].reshape(rows, HEAD_DIM)
        for j in range(GROUPS):
            cols = slice(j * HEAD_DIM, (j + 1) * HEAD_DIM)
            head = GROUPS * (first + pl.program_id(0)) + j
            lse, delta, factors = [far_ref[pl.ds(i * HEADS + head, 1), :] for i in range(3)]
            for late in range(2):
                there = slice(late * pack // 2, (late + 1) * pack // 2)
                here = slice(0, rows if late else half)
                qq, dd = q_ref[there, cols], do_ref[there, cols]
                factor = factors[:, there]
                scores = mm_nt(k_own[here], qq) * (factor * (SCALE * LOG2E)) + bias[here, there]
                probs = jnp.exp2(scores - lse[:, there])
                d_probs = mm_nt(v_own[here], dd)
                d_scores = (probs * factor * (d_probs - delta[:, there])).astype(BF16)
                dv = mm(probs.astype(BF16), dd)
                dk = mm(d_scores, qq)
                if j == 0 and late == 0:
                    acc[...] = jnp.zeros_like(acc)
                acc[0, here, :] += dk
                acc[1, here, :] += dv
        out_ref[1] = acc[1].astype(BF16)
        dk = acc[0] * SCALE
        dk = dk * c_ref[...] - turn(dk) * s_ref[...]
        dk, terms = head_norm_back(raw_ref[...].astype(F32).reshape(rows, HEAD_DIM), g_ref[...], dk)
        out_ref[0] = dk.astype(BF16)
        gg_ref[...] += jnp.sum(terms, axis=0, keepdims=True)

    col = pl.BlockSpec((pack, pair), lambda g, at: (0, first + g))
    key = pl.BlockSpec((2, 1, half, HEAD_DIM), lambda g, at: (0, at[0], 0, first + g))
    laid = (2, ctx_size, half, KV_HEADS * HEAD_DIM)
    return call(
        "key_back", body,
        [
            queries, grad_mixed, keys.reshape(laid), values.reshape(laid), far, q_low, q_high, k_stream, key_raw.reshape(laid), gain, cos, sin, *earlier,
        ],
        [
            col, col, key, key, whole(far.shape), whole((1, pack)), whole((1, pack)), whole((rows, 1)),
            key, whole((1, HEAD_DIM)), whole((rows, HEAD_DIM)), whole((rows, HEAD_DIM)),
        ]
        + [ANY] * len(earlier),
        [pl.BlockSpec((2, rows, HEAD_DIM), lambda g, at: (0, 0, first + g)), whole((1, HEAD_DIM))],
        [shape((2, rows, KV_HEADS * HEAD_DIM), BF16), shape((1, HEAD_DIM), F32)],
        grid=(count,),
        scratch=[pltpu.VMEM((rows, pack), F32), pltpu.VMEM((2, rows, HEAD_DIM), F32)],
        prefetch=[ctx_at], aliases={12: 0} if earlier else None,
    )


def all_queries(x, weights, gain, cos, sin):
    rows, width = x.shape
    cols = HEADS * HEAD_DIM
    block = 2 * HEAD_DIM
    part = 256

    def body(x_ref, w_ref, g_ref, c_ref, s_ref, rot_ref):
        g = twice(g_ref)
        for i in range(rows // part):
            here = slice(i * part, (i + 1) * part)
            raw = mm(x_ref[here, :], w_ref[...])
            c, s = [jnp.concatenate([r[here, :]] * 2, axis=1) for r in (c_ref, s_ref)]
            rot_ref[here, :] = rotated(raw * g, c, s).astype(BF16)

    return call(
        "all_queries", body, [x, weights, gain, cos, sin],
        [IN_VMEM, pl.BlockSpec((width, block), lambda j: (0, j)), IN_VMEM, IN_VMEM, IN_VMEM],
        [pl.BlockSpec((rows, block), lambda j: (0, j))], [shape((rows, cols), BF16)],
        grid=(cols // block,),
    )[0]


def all_grad_mixed(own, parcels, stack, places, ctx_at, rows):
    count = (len(parcels) + 1) // 2
    numbers = parcels[0].shape[0] - rows
    half = rows // 2
    inner = own.shape[1]
    _, _, width = stack.shape
    owners = stack.shape[0]
    unit = width // owners

    def body(places_ref, at_ref, own_ref, a_ref, b_ref, *refs):
        blocks, (out_ref, far_ref, turned) = refs[:-3], refs[-3:]
        step = pl.program_id(0)
        me = at_ref[0]

        def spread(ref):
            both = ref[rows:, :rows].astype(F32) + ref[rows:, rows : 2 * rows].astype(F32)
            far_ref[0, 0] = both[:, :half]
            far_ref[1, 0] = both[:, half:]

        @pl.when(step == 0)
        def _():
            spread(blocks[0])
            out_ref[...] = own_ref[...].reshape(2, 1, half, inner)
            turned[...] = jnp.concatenate([a_ref[...], b_ref[...]], axis=1).reshape(inner, width)

        def write(ref):
            spread(ref)
            for j in range(inner // 512):
                at = slice(j * 512, (j + 1) * 512)
                part = mm_nt(ref[:rows, :], turned[at, :]).astype(BF16)
                out_ref[:, :, :, at] = part.reshape(2, 1, half, 512)

        for s in range(1, count):

            @pl.when((step == s) & (me >= s))
            def _():
                write(blocks[s])

            @pl.when((step == s) & (me < s))
            def _():
                write(blocks[count - 1 + count - s])

    return call(
        "all_grad_mixed", body, [own, stack, stack, *parcels],
        [
            IN_VMEM,
            pl.BlockSpec((owners, unit, width), lambda *_: (0, 9, 0)),
            pl.BlockSpec((owners, unit, width), lambda *_: (0, 10, 0)),
        ]
        + [whole(parcel.shape) for parcel in parcels],
        [
            pl.BlockSpec((2, 1, half, inner), lambda k, at, me: (0, at[k], 0, 0)),
            pl.BlockSpec((2, 1, numbers, half), lambda k, at, me: (0, at[k], 0, 0)),
        ],
        [shape((2, count, half, inner), BF16), shape((2, count, numbers, half), F32)],
        grid=(count,), scratch=[pltpu.VMEM((inner, width), BF16)], prefetch=[places, ctx_at], vmem=32,
    )


def normed_back(d_queries, d_pair, weights):
    rows, inner = d_queries.shape
    cols = d_pair.shape[2]
    width = weights.shape[0]

    def body(dq_ref, pair_ref, wq_ref, wk_ref, wv_ref, out_ref):
        part = mm_nt(dq_ref[...], wq_ref[...])
        part += mm_nt(pair_ref[0], wk_ref[...])
        part += mm_nt(pair_ref[1], wv_ref[...])
        out_ref[...] = part

    block = 256
    return call(
        "normed_back", body, [d_queries, d_pair, weights, weights, weights],
        [
            IN_VMEM,
            IN_VMEM,
            pl.BlockSpec((block, inner), lambda j: (j, 0)),
            pl.BlockSpec((block, cols), lambda j: (j, inner // cols)),
            pl.BlockSpec((block, cols), lambda j: (j, inner // cols + 1)),
        ],
        [pl.BlockSpec((rows, block), lambda j: (0, j))],
        [shape((rows, width), F32)],
        grid=(width // block,),
    )[0]


def input_back(d_normed, tokens, gain, grad_middle):
    rows, width = tokens.shape

    def body(a_ref, t_ref, gain_ref, gm_ref, out_ref, gg_ref):
        back, terms = norm_back(t_ref[...].astype(F32), gain_ref[...], a_ref[...])
        out_ref[...] = (gm_ref[...] + back).astype(BF16)
        gg_ref[...] = jnp.sum(terms, axis=0, keepdims=True)

    return call(
        "input_back", body, [d_normed, tokens, gain, grad_middle],
        [IN_VMEM] * 4,
        [whole((rows, width)), IN_VMEM],
        [shape((rows, width), BF16), shape((1, width), F32)],
    )


def weight_grad(left, right, owners=None, cols=None, block=512, apart=False, beside=False):
    tokens, rows = left.shape
    count = 1 if owners is None else owners.shape[0]
    unit = rows // count
    deep = right.ndim == 3
    first, each = cols or (0, right.shape[-1])
    width = each * (right.shape[0] if deep else 1)
    steps = width // block
    split = owners is not None
    results = 2 * (right.shape[0] if apart else 1) if split else 1

    def body(*refs):
        if split:
            own_ref, refs = refs[0], refs[1:]
        l_ref, r_ref, refs = refs[0], refs[1], refs[2:]
        outs, scratch = refs[:results], refs[results:]

        @pl.when(pl.program_id(0) == 0)
        def _():
            scratch[0][...] = l_ref[...].T
            for k in range(count if split else 0):
                at = pl.multiple_of(own_ref[k] * unit, unit)
                scratch[1][k * unit : (k + 1) * unit, :] = scratch[0][pl.ds(at, unit), :]

        def block_at(j):
            if deep:
                per = each // block
                return r_ref[j // per, :, pl.ds(pl.multiple_of(first + (j % per) * block, block), block)]
            return r_ref[:, pl.ds(pl.multiple_of(first + j * block, block), block)]

        if not split:
            outs[0][...] = mm(scratch[0][...], block_at(pl.program_id(0))).astype(BF16)
            return
        per = each // block
        for j in range(steps):
            at = 2 * (j // per) if apart else 0
            to = slice((j % per) * block, (j % per + 1) * block) if apart else slice(j * block, (j + 1) * block)
            for side in range(2):
                here = slice(side * rows // 2, (side + 1) * rows // 2)
                part = mm(scratch[1][here, :], block_at(j)).astype(BF16)
                part = part.reshape(count // 2, unit, block)
                if beside:
                    outs[side][:, :, to] = part[:, : unit // 2]
                    outs[side][:, :, width + j * block : width + (j + 1) * block] = part[:, unit // 2 :]
                else:
                    outs[at + side][:, :, to] = part

    if split:
        out = [IN_VMEM] * results
        dims = (count // 2, unit // 2, 2 * width) if beside else (count // 2, unit, each if apart else width)
        out_shape = [shape(dims, BF16)] * results
    else:
        out = [pl.BlockSpec((rows, block), lambda j: (0, j))]
        out_shape = [shape((rows, width), BF16)]
    return call(
        "weight_grad", body, [left, right], [IN_VMEM] * 2, out, out_shape,
        grid=(1 if split else steps,),
        scratch=[pltpu.VMEM((rows, tokens), BF16)] * (1 + split),
        prefetch=[owners] if split else (),
    )


def fold(items, steps=1):
    arrays = []

    def slot(term):
        for i, known in enumerate(arrays):
            if known is term:
                return i
        arrays.append(term)
        return len(arrays) - 1

    laid = [([slot(t) for t in terms], rows, bit) for terms, rows, bit in items]
    in_specs = []
    for a in arrays:
        in_specs.append(
            IN_VMEM if steps == 1 else pl.BlockSpec(a.shape[:2] + (a.shape[2] // steps,), lambda j: (0, 0, j))
        )
    out_specs, out_shape = [], []
    for slots, (_, rows), bit in laid:
        many, _, cols = arrays[slots[0]].shape
        dims = (many, rows, cols) if bit is None else (many // 2, rows, cols)
        for _ in range(1 if bit is None else 2):
            out_specs.append(
                IN_VMEM if steps == 1 else pl.BlockSpec(dims[:2] + (cols // steps,), lambda j: (0, 0, j))
            )
            out_shape.append(shape(dims, BF16))

    def body(*refs):
        ins, outs = refs[: len(arrays)], list(refs[len(arrays) :])
        for slots, (first, rows), bit in laid:
            here = slice(first, first + rows)
            many = arrays[slots[0]].shape[0]

            def total(k):
                value = ins[slots[0]][k, here, :].astype(F32)
                for at in slots[1:]:
                    value = value + ins[at][k, here, :].astype(F32)
                return value.astype(BF16)

            if bit is None:
                out = outs.pop(0)
                for k in range(many):
                    out[k] = total(k)
                continue
            sent, kept = outs.pop(0), outs.pop(0)
            places = [0, 0]
            for k in range(many):
                with_bit = (k >> bit) & 1
                (sent if with_bit else kept)[places[with_bit]] = total(k)
                places[with_bit] += 1

    return call("fold", body, arrays, in_specs, out_specs, out_shape, grid=(steps,))


def choose(first, second, dims, odd):
    arrays = [a for a, _ in first + second]
    views = [v for _, v in first + second]

    def body(odd_ref, *refs):
        ins, (sent, kept) = refs[: len(arrays)], refs[len(arrays) :]

        def total(begin, end):
            value = ins[begin][views[begin]].astype(F32)
            for at in range(begin + 1, end):
                value = value + ins[at][views[at]].astype(F32)
            return value.astype(BF16)

        @pl.when(odd_ref[0] == 1)
        def _():
            sent[...] = total(0, len(first))
            kept[...] = total(len(first), len(arrays))

        @pl.when(odd_ref[0] == 0)
        def _():
            kept[...] = total(0, len(first))
            sent[...] = total(len(first), len(arrays))

    return call(
        "choose", body, arrays, [IN_VMEM] * len(arrays), [IN_VMEM] * 2, [shape(dims, BF16)] * 2,
        prefetch=[odd],
    )


def place(sums, odd, out_dims, cuts):
    arrays = [a for pair in sums for a in pair]

    def body(odd_ref, *refs):
        ins, outs = refs[: len(arrays)], refs[len(arrays) :]

        def write(swapped):
            for which, half, source, at, target in cuts:
                outs[at][target] = ins[2 * which + (half ^ swapped)][source].astype(F32)

        @pl.when(odd_ref[0] == 1)
        def _():
            write(1)

        @pl.when(odd_ref[0] == 0)
        def _():
            write(0)

    return call(
        "place", body, arrays, [IN_VMEM] * len(arrays), [whole(d) for d in out_dims],
        [shape(d, F32) for d in out_dims], prefetch=[odd],
    )


def swap(x, axis, bit):
    size = lax.axis_size(axis)
    return lax.ppermute(x, axis, [(i, i ^ bit) for i in range(size)])


def bits_of(size):
    return [1 << b for b in range(size.bit_length() - 1)]


def gather_pieces(own, cut):
    rest = bits_of(lax.axis_size("dp"))[1:]
    spans = [slice(0, cut), slice(cut, own.shape[1])]
    everything = slice(0, own.shape[1])
    held = {0: [(everything, own)]}
    for bit in rest:
        held[bit] = [(everything, swap(own, "dp", bit))]
    first = [held[bit][0][1] for bit in rest]
    for at in range(1 << len(rest)):
        at = 2 * at
        if at in held:
            continue
        held[at] = []
        for span, order in zip(spans, (rest, rest[::-1])):
            last = [bit for bit in order if at & bit][-1]
            before = held[at ^ last]
            source = before[0][1][:, span] if len(before) == 1 else before[spans.index(span)][1]
            held[at].append((span, swap(source, "dp", last)))
    for at in sorted(held):
        held[at | 1] = [(span, swap(piece, "dp", 1)) for span, piece in held[at]]
    return held, first


class Sum:
    def __init__(self, kept, sent, halves, odd):
        self.rest = bits_of(lax.axis_size("dp"))[1:]
        self.order = [list(range(len(self.rest))), list(range(len(self.rest)))[::-1]]
        self.left = [list(range(len(self.rest))), list(range(len(self.rest)))]
        self.odd = odd
        arrived = [swap(s, "dp", 1) for s in sent]
        if len(kept) == 1:
            kept, arrived = kept * 2, arrived * 2
        self.terms = [[k, a] for k, a in zip(kept, arrived)]
        self.rows = halves
        self.stage = 0

    def over_dp(self, steps=1):
        bits = [order[self.stage] for order in self.order]
        items = [
            (terms, rows, left.index(bit))
            for terms, rows, left, bit in zip(self.terms, self.rows, self.left, bits)
        ]
        sent0, kept0, sent1, kept1 = fold(items, steps)
        self.terms = [
            [kept, swap(sent, "dp", self.rest[bit])]
            for kept, sent, bit in zip((kept0, kept1), (sent0, sent1), bits)
        ]
        self.rows = [(0, k.shape[1]) for k in (kept0, kept1)]
        for left, bit in zip(self.left, bits):
            left.remove(bit)
        self.stage += 1

    def joined(self):
        dims = [terms[0].shape[1:] for terms in self.terms]
        arrays = [term for terms in self.terms for term in terms]
        many = len(self.terms[0])

        def body(*refs):
            at = 0
            for part, (rows, _) in enumerate(dims):
                value = refs[part * many][0].astype(F32)
                for k in range(1, many):
                    value = value + refs[part * many + k][0].astype(F32)
                refs[-1][at : at + rows, :] = value.astype(BF16)
                at += rows

        total = (sum(rows for rows, _ in dims), dims[0][1])
        return call(
            "joined", body, arrays, [IN_VMEM] * len(arrays), [IN_VMEM], [shape(total, BF16)]
        )[0]

    def to_ctx(self):
        first, second = [[(t, 0) for t in terms] for terms in self.terms]
        self.begin_ctx(first, second, first[0][0].shape[1:])

    def begin_ctx(self, first, second, dims):
        sent, kept = choose(first, second, dims, self.odd)
        self.total, self.next = [kept, swap(sent, "ctx", 1)], bits_of(lax.axis_size("ctx"))[1:]

    def over_ctx(self):
        a, b = [t[None] for t in self.total]
        total = fold([([a, b], (0, a.shape[1]), None)])[0][0]
        if self.next:
            self.total = [total, swap(total, "ctx", self.next.pop(0))]
        else:
            self.total = [total, swap(total, "ctx", 1)]


class Line:
    def __init__(self, total):
        size = lax.axis_size("ctx")
        middle = size // 2
        self.hops = [("add", [(k, k + 1), (size - 1 - k, size - 2 - k)]) for k in range(middle - 1)]
        self.hops.append(("add", [(middle - 1, middle), (middle, middle - 1)]))
        for k in reversed(range(middle - 1)):
            self.hops.append(("take", [(k + 1, k), (size - 2 - k, size - 1 - k)]))
        self.total = total
        self.send()

    def send(self):
        self.kind, pairs = self.hops.pop(0)
        self.takers = [b for _, b in pairs]
        self.came = lax.ppermute(self.total, "ctx", pairs)

    def taking(self):
        at = lax.axis_index("ctx")
        return sum((at == taker).astype(jnp.int32) for taker in self.takers)[None]

    def step(self):
        if self.kind == "add":
            rows = self.total.shape[0]
            self.total = fold([([self.total[None], self.came[None]], (0, rows), None)])[0][0]
        else:
            self.total = jnp.where(self.taking()[0] == 1, self.came, self.total)
        self.send()

    def finish(self):
        while self.hops:
            self.step()

    def place(self, out_dims, cuts):
        cuts = [(0, 0, source, at, target) for source, at, target in cuts]
        if self.kind == "add":
            self.total, self.came = fold([([self.total[None], self.came[None]], (0, self.total.shape[0]), None)])[0][0], self.total
            return place([(self.total, self.came)], jnp.zeros((1,), jnp.int32), out_dims, cuts)
        return place([(self.total, self.came)], self.taking(), out_dims, cuts)


class Relay:
    def __init__(self, block):
        self.size = lax.axis_size("ctx")
        self.from_left, self.from_right = [], []
        self.send(block, block)

    def send(self, right, left):
        step = len(self.from_left)
        self.from_left.append(lax.ppermute(right, "ctx", [(i, i + 1) for i in range(step, self.size - 1)]))
        self.from_right.append(
            lax.ppermute(left, "ctx", [(i + 1, i) for i in range(self.size - 1 - step)])
        )

    def step(self):
        came = [self.from_left[-1], self.from_right[-1]]
        self.send(
            *copies(
                "pass_on", came, lambda _, ins, outs: list(zip(ins, outs)),
                [shape(c.shape, c.dtype) for c in came],
                in_specs=[whole(c.shape) for c in came], out_specs=[whole(c.shape) for c in came],
            )
        )

    def finish(self):
        while len(self.from_left) < self.size - 1:
            self.step()


class Everywhere:
    def __init__(self, x):
        self.left = [("dp", bit) for bit in bits_of(lax.axis_size("dp"))]
        self.left += [("ctx", bit) for bit in bits_of(lax.axis_size("ctx"))]
        self.total = x
        self.came = swap(x, *self.left.pop(0))

    def step(self):
        def body(a_ref, b_ref, out_ref):
            out_ref[...] = a_ref[...] + b_ref[...]

        self.total = call(
            "add_small", body, [self.total, self.came], [IN_VMEM] * 2, [IN_VMEM],
            [shape(self.total.shape, F32)],
        )[0]
        if self.left:
            self.came = swap(self.total, *self.left.pop(0))
            return True
        return False

    def finish(self):
        while self.step():
            pass
        return self.total


def on_device(
    tokens, doc_starts, attn_gain, w_query, w_key, w_value, w_out,
    query_gain, key_gain, mlp_gain, w_gate, w_up, w_down, cotangent,
):
    ORDER.clear()
    rows, width = tokens.shape[1], tokens.shape[2]
    stretch = rows // 2
    ctx_size = lax.axis_size("ctx")
    dp_size = lax.axis_size("dp")
    ctx_at = lax.axis_index("ctx")
    dp_at = lax.axis_index("dp")
    pack_rows = rows * ctx_size
    unit = width // dp_size
    inner = HEADS * HEAD_DIM
    own_tokens = tokens[0]
    grad_out = cotangent[0]
    starts = doc_starts[0]
    odd = (ctx_at % 2).astype(jnp.int32)[None]
    dp_bits = bits_of(dp_size)

    gains = jnp.concatenate(
        [attn_gain[:, None], mlp_gain[:, None], jnp.zeros((unit, HEAD_DIM - 2), BF16)], axis=1
    )

    def packing(_, ins, outs):
        at = 0
        for ref in ins:
            yield ref.at[:, :], outs[0].at[:, pl.ds(at, ref.shape[1])]
            at += ref.shape[1]

    def stacking(_, ins, outs):
        down, gate, up, out = ins
        stack_ref = outs[0]
        yield down.at[:, :], stack_ref.at[pl.ds(0, 3 * unit)]
        for i in range(3):
            cols = pl.ds(i * width, width)
            yield gate.at[:, cols], stack_ref.at[pl.ds((3 + i) * unit, unit)]
            yield up.at[:, cols], stack_ref.at[pl.ds((6 + i) * unit, unit)]
        yield out.at[:, :], stack_ref.at[pl.ds(9 * unit, 2 * unit)]

    attn_cols = inner + 2 * width + HEAD_DIM
    own_attn = copies(
        "pack_attn", [w_query, w_key, w_value, gains], packing, [shape((unit, attn_cols), BF16)],
        in_specs=[whole(w.shape) for w in (w_query, w_key, w_value)] + [IN_VMEM],
    )[0]
    pieces, first_pieces = gather_pieces(own_attn, inner)
    gathered = Relay(own_tokens)
    stack_in = copies(
        "pack_stack", [w_down, w_gate, w_up, w_out], stacking, [shape((11 * unit, width), BF16)],
        in_specs=[whole(w.shape) for w in (w_down, w_gate, w_up, w_out)],
        out_specs=[whole((11 * unit, width))],
    )[0]
    stack = lax.all_gather(stack_in, "dp", axis=0)
    gathered.step()
    touch(first_pieces)
    gathered.finish()
    from_left, from_right = gathered.from_left, gathered.from_right

    place_at = jnp.arange(pack_rows, dtype=jnp.int32)
    in_half = place_at % (pack_rows // 2)
    part, device, row = place_at // (pack_rows // 2), in_half // stretch, place_at % stretch
    key_stream = stream_index(device * rows + part * stretch + row, stretch, ctx_size)
    query_stream = stream_index(
        ctx_at * rows + jnp.arange(rows, dtype=jnp.int32), stretch, ctx_size
    )
    key_open = opening_of(key_stream, starts)
    query_open = opening_of(query_stream, starts)
    cos_pack, sin_pack = rotary(key_stream - key_open)
    cos_own, sin_own = rotary(query_stream - query_open)

    owners = (dp_at ^ jnp.arange(dp_size, dtype=jnp.int32)).astype(jnp.int32)
    listed = [(k, span, piece) for k in range(dp_size) for span, piece in pieces[k]]

    def assembling(prefetch, ins, outs):
        for (k, span, _), ref in zip(listed, ins):
            at = pl.multiple_of(prefetch[0][k] * unit, unit)
            cols = pl.ds(span.start, span.stop - span.start)
            yield ref.at[:, :], outs[0].at[pl.ds(at, unit), cols]
            if span.stop == attn_cols:
                last = ref.shape[1] - HEAD_DIM
                yield ref.at[:, pl.ds(last, HEAD_DIM)], outs[1].at[pl.ds(at, unit), :]

    attn_w, gain_cols = copies(
        "assemble_weights", [piece for _, _, piece in listed], assembling,
        [shape((width, attn_cols), BF16), shape((width, HEAD_DIM), BF16)], prefetch=[owners],
        out_specs=[whole((width, attn_cols)), IN_VMEM],
    )
    gain_rows = gain_cols[:, :2].astype(F32).T
    gain_attn, gain_mlp = gain_rows[0:1], gain_rows[1:2]
    gain_query = query_gain.astype(F32)[None, :]
    gain_key = key_gain.astype(F32)[None, :]

    normed = norm_own(own_tokens, gain_attn)
    query_raw, queries, factors = project_queries(normed, attn_w, gain_query, cos_own, sin_own)
    places = ((ctx_at - jnp.arange(ctx_size, dtype=jnp.int32)) % ctx_size).astype(jnp.int32)
    normed_pack = norm_pack(
        own_tokens, from_left, from_right, gain_attn, places, ctx_at.astype(jnp.int32)[None]
    ).reshape(pack_rows, width)
    key_raw, keys, values = project_keys_values(normed_pack, attn_w, gain_key, cos_pack, sin_pack)
    mixed, lse = attend(
        queries, keys, values, query_open[:, None], query_stream[:, None], key_stream[None, :]
    )
    (
        output, normed_mid, hidden, d_both, grad_middle, grad_branch, mlp_part, grad_mixed, parcel,
    ) = middle_block(mixed, lse, factors, own_tokens, grad_out, gain_mlp, stack)

    order = [2 * k for k in range(dp_size // 2)] + [2 * k + 1 for k in range(dp_size // 2)]
    owners = (dp_at ^ jnp.array(order, jnp.int32)).astype(jnp.int32)
    everything = slice(None)
    ctx_steps = len(bits_of(ctx_size))
    later_dp, later_ctx = len(dp_bits) - 2, ctx_steps - 1

    def two_rows(total, half, widths=(width,)):
        cuts, at = [], 0
        for which, each in enumerate(widths):
            for k in range(2):
                to = (slice(k * half, (k + 1) * half), everything)
                cuts.append((0, k, (everything, slice(at, at + each)), which, to))
            at += each
        return place([total.total], odd, [(2 * half, each) for each in widths], cuts)

    def halves_of(pair):
        half = pair[0].shape[1] // 2
        return Sum(pair[:1], pair[1:], [(0, half), (half, half)], odd), half

    half_heads = KV_HEADS // 2
    parcels = Relay(parcel)
    wide_grad = weight_grad(normed_mid, d_both, block=1024)[0]
    wide_grad = lax.psum_scatter(wide_grad, "dp", scatter_dimension=0, tiled=True)
    query_args = (
        queries, grad_mixed, mixed, keys, values, lse, query_open[:, None], query_stream[:, None],
        key_stream[None, :], query_raw, gain_query, cos_own, sin_own,
    )
    d_query, query_part = query_back(*query_args, 0, half_heads)
    out_kept, out_sent = weight_grad(mixed, grad_branch, owners, beside=True)

    parcels.step()

    d_query, query_more = query_back(*query_args, half_heads, half_heads, (d_query,))

    parcels.finish()
    query_kept, query_sent = weight_grad(normed, d_query, owners)
    outer = Sum([out_kept, query_kept], [out_sent, query_sent], [(0, unit), (0, unit)], odd)

    every_query = all_queries(normed_pack, attn_w, gain_query, cos_pack, sin_pack)

    touch([parcels.from_left[-1], parcels.from_right[-1]])
    down_grad = weight_grad(hidden, grad_out, block=256)[0]
    down_grad = lax.psum_scatter(down_grad, "dp", scatter_dimension=0, tiled=True)
    outer.over_dp()
    wide_grad = copies(
        "take", [wide_grad], lambda _, ins, outs: [(ins[0], outs[0])], [shape(wide_grad.shape, BF16)]
    )[0]
    wide = Line(wide_grad)

    parcels = [parcel] + parcels.from_left + parcels.from_right
    grad_mixed_pack, far = all_grad_mixed(
        grad_mixed, parcels, stack, places, ctx_at.astype(jnp.int32)[None], rows
    )
    grad_mixed_pack = grad_mixed_pack.reshape(pack_rows, inner)
    far = far.transpose(2, 0, 1, 3).reshape(3 * HEADS, pack_rows)
    key_args = (
        every_query, grad_mixed_pack, keys, values, far,
        key_open[None, :], key_stream[None, :], query_stream[:, None],
        key_raw, gain_key, cos_own, sin_own, ctx_at.astype(jnp.int32)[None], ctx_size,
    )
    d_pair, key_part = key_back(*key_args, 0, half_heads)

    for _ in range(later_dp):
        outer.over_dp()
    wide.step()

    d_pair, key_more = key_back(*key_args, half_heads, half_heads, (d_pair,))
    query_part, key_part = query_part + query_more, key_part + key_more

    outer = Line(outer.joined())
    key_kept, key_sent, value_kept, value_sent = weight_grad(normed, d_pair, owners, apart=True)
    pair = Sum([key_kept, value_kept], [key_sent, value_sent], [(0, unit), (0, unit)], odd)

    d_normed = normed_back(d_query, d_pair, attn_w)
    input_grad, attn_part = input_back(d_normed, own_tokens, gain_attn, grad_middle)

    wide.finish()
    pair.over_dp()
    down_grad = copies(
        "take", [down_grad], lambda _, ins, outs: [(ins[0], outs[0])], [shape(down_grad.shape, BF16)]
    )[0]
    down = Line(down_grad)
    small = Everywhere(
        jnp.concatenate([attn_part, mlp_part, query_part, key_part], axis=1).reshape(-1, HEAD_DIM)
    )

    for _ in range(later_dp):
        pair.over_dp()
    small.step()
    outer.step()

    pair.to_ctx()
    small.step()
    down.step()
    gate_grad, up_grad = wide.place(
        [(unit, 3 * width)] * 2,
        [((everything, slice(k * 3 * width, (k + 1) * 3 * width)), k, everything) for k in range(2)],
    )

    pair.over_ctx()
    small.step()
    outer.finish()

    for _ in range(later_ctx):
        pair.over_ctx()
        small.step()
    down.finish()
    small = small.finish().reshape(-1)
    near, far_half = slice(0, width), slice(width, 2 * width)
    first, second = slice(0, unit), slice(unit, 2 * unit)
    w_out_grad, query_grad = outer.place(
        [(2 * unit, width), (unit, inner)],
        [
            ((first, near), 0, (first, everything)),
            ((first, far_half), 0, (second, everything)),
            ((second, everything), 1, everything),
        ],
    )
    down_grad = down.place([down_grad.shape], [(everything, 0, everything)])[0]
    key_grad, value_grad = place(
        [pair.total], odd, [(unit, width)] * 2, [(0, k, everything, k, everything) for k in range(2)]
    )

    attn_gain_grad = lax.dynamic_slice(small, (dp_at * unit,), (unit,))
    mlp_gain_grad = lax.dynamic_slice(small, (width + dp_at * unit,), (unit,))
    query_gain_grad = small[2 * width : 2 * width + HEAD_DIM]
    key_gain_grad = small[2 * width + HEAD_DIM :]
    return (
        output[None], input_grad[None], attn_gain_grad, query_grad, key_grad, value_grad, w_out_grad,
        query_gain_grad, key_gain_grad, mlp_gain_grad, gate_grad, up_grad, down_grad,
    )


def solution(mesh):
    in_specs = (
        P("dp", "ctx", None),
        P("dp", None),
        P("dp"),
        P("dp", None),
        P("dp", None),
        P("dp", None),
        P("dp", None),
        P(),
        P(),
        P("dp"),
        P("dp", None),
        P("dp", None),
        P("dp", None),
        P("dp", "ctx", None),
    )
    out_specs = (
        P("dp", "ctx", None),
        P("dp", "ctx", None),
        P("dp"),
        P("dp", None),
        P("dp", None),
        P("dp", None),
        P("dp", None),
        P(),
        P(),
        P("dp"),
        P("dp", None),
        P("dp", None),
        P("dp", None),
    )
    return jax.shard_map(
        on_device, mesh=mesh, in_specs=in_specs, out_specs=out_specs, check_vma=False
    )
```

```python
import functools
import math

import jax
import jax.numpy as jnp
from jax import lax
from jax.experimental import pallas as pl
from jax.experimental.pallas import tpu as pltpu
from jax.sharding import PartitionSpec as P

HEADS = 16
KV_HEADS = 8
HEAD_DIM = 128
GROUPS = HEADS // KV_HEADS

EPSILON = 1e-06
ROPE_BASE = 1000000.0
MASKED = -1e30
SCALE = HEAD_DIM ** (-0.5)

F32 = jnp.float32
BF16 = jnp.bfloat16
MIB = 1 << 20
VMEM_MIB = 16
LARGE = 1 << 18


ORDER = []


def room(pack):
    return VMEM_MIB * max(1, pack // 1536)


def shape(dims, dtype):
    return jax.ShapeDtypeStruct(dims, dtype)


ANY = pl.BlockSpec(memory_space=pl.ANY)
IN_VMEM = pl.BlockSpec(memory_space=pltpu.VMEM)
IN_HBM = pl.BlockSpec(memory_space=pltpu.HBM)


def in_hbm(spec, array):
    return spec not in (IN_VMEM, ANY, IN_HBM) and math.prod(array.shape) * 2 >= LARGE


def call(
    name, body, args, in_specs, out_specs, out_shape, grid=(1,), scratch=(), prefetch=(), aliases=None,
    after=(), vmem=VMEM_MIB,
):
    waits = list(ORDER) + list(after)
    wait_specs = [IN_VMEM] * len(ORDER) + [ANY] * len(after)
    taken = len(prefetch) + len(args)
    token = taken + len(waits) + len(out_shape)
    args = [
        pltpu.with_memory_space_constraint(a, pltpu.HBM) if in_hbm(s, a) else a
        for a, s in zip(args, in_specs)
    ]
    out_shape = [
        pltpu.HBM(o.shape, o.dtype) if in_hbm(s, o) else o for o, s in zip(out_shape, out_specs)
    ]

    def without(*refs):
        refs[token][...] = jnp.zeros_like(refs[token])
        body(*refs[:taken], *refs[taken + len(waits) : token], *refs[token + 1 :])

    results = pl.pallas_call(
        without,
        grid_spec=pltpu.PrefetchScalarGridSpec(
            num_scalar_prefetch=len(prefetch),
            grid=grid,
            in_specs=list(in_specs) + wait_specs,
            out_specs=list(out_specs) + [IN_VMEM],
            scratch_shapes=list(scratch),
        ),
        out_shape=out_shape + [shape((8, HEAD_DIM), F32)],
        input_output_aliases={len(prefetch) + i: o for i, o in (aliases or {}).items()},
        compiler_params=pltpu.CompilerParams(vmem_limit_bytes=vmem * MIB),
        cost_estimate=pl.CostEstimate(flops=0, bytes_accessed=0, transcendentals=0),
        name=name,
    )(*prefetch, *args, *waits)
    ORDER[:] = [results[-1]]
    return results[:-1]


def whole(dims):
    return pl.BlockSpec(dims, lambda *_: (0,) * len(dims))


def mm(a, b):
    return lax.dot_general(a, b, (((1,), (0,)), ((), ())), preferred_element_type=F32)


def mm_nt(a, b):
    return lax.dot_general(a, b, (((1,), (1,)), ((), ())), preferred_element_type=F32)


def mm_tn(a, b):
    return lax.dot_general(a, b, (((0,), (0,)), ((), ())), preferred_element_type=F32)


def mean_last(v):
    return jnp.sum(v, axis=-1, keepdims=True) * (1.0 / v.shape[-1])


def factor_of(v):
    return lax.rsqrt(mean_last(v * v) + EPSILON)


def norm_back(v, gain, incoming):
    f = factor_of(v)
    weighted = incoming * gain
    inner = mean_last(weighted * v)
    return f * weighted - v * (f * f * f * inner), incoming * v * f


def stream_index(row_ids, stretch_rows, ctx_size):
    slab_index = row_ids // (2 * stretch_rows)
    within = row_ids % (2 * stretch_rows)
    mirrored = (2 * ctx_size - 1 - slab_index) * stretch_rows + within - stretch_rows
    return jnp.where(within < stretch_rows, slab_index * stretch_rows + within, mirrored)


def opening_of(stream, starts):
    started = starts[None, :] <= stream[:, None]
    return jnp.max(jnp.where(started, starts[None, :], 0), axis=1)


def rotary(positions):
    half_dim = HEAD_DIM // 2
    inverse = jnp.exp(
        jnp.arange(half_dim, dtype=F32) * (-2.0 * math.log(ROPE_BASE) / HEAD_DIM)
    )
    angles = positions.astype(F32)[:, None] * inverse[None, :]
    cos_half, sin_half = jnp.cos(angles), jnp.sin(angles)
    return (
        jnp.concatenate([cos_half, cos_half], axis=1),
        jnp.concatenate([-sin_half, sin_half], axis=1),
    )


def copies(name, sources, plan, out_shape, prefetch=(), after=(), in_specs=None, out_specs=None):
    count = len(sources)
    first = len(prefetch)

    def body(*refs):
        ins = refs[first : first + count]
        for source, target in plan(refs[:first], ins, refs[first + count :]):
            target[...] = source[...]

    return call(
        name, body, sources, in_specs or [IN_VMEM] * count, out_specs or [IN_VMEM] * len(out_shape), out_shape,
        prefetch=prefetch, after=after, vmem=24,
    )


def touch(after):
    call("touch", lambda *_: None, [], [], [], [], after=after, vmem=4)


def norm_own(tokens, gain):
    def body(t_ref, g_ref, out_ref):
        x = t_ref[...].astype(F32)
        out_ref[...] = (x * factor_of(x) * g_ref[...]).astype(BF16)

    return call(
        "norm_own", body, [tokens, gain], [IN_VMEM] * 2, [IN_VMEM], [shape(tokens.shape, BF16)]
    )[0]


def norm_pack(own, from_left, from_right, gain, places, ctx_at):
    count = len(from_left) + 1
    rows, width = own.shape
    half = rows // 2

    def body(places_ref, at_ref, gain_ref, *refs):
        blocks, pack_ref = refs[:-1], refs[-1]
        step = pl.program_id(0)
        me = at_ref[0]

        def write(ref):
            x = ref[...].astype(F32)
            low = (x * factor_of(x) * gain_ref[...]).astype(BF16)
            pack_ref[...] = low.reshape(2, 1, half, width)

        @pl.when(step == 0)
        def _():
            write(blocks[0])

        for s in range(1, count):

            @pl.when((step == s) & (me >= s))
            def _():
                write(blocks[s])

            @pl.when((step == s) & (me < s))
            def _():
                write(blocks[count - 1 + count - s])

    blocks = [own] + from_left + from_right
    return call(
        "norm_pack", body, [gain] + blocks,
        [whole((1, width))] + [IN_VMEM] * len(blocks),
        [pl.BlockSpec((2, 1, half, width), lambda k, at, me: (0, at[k], 0, 0))],
        [shape((2, count, half, width), BF16)],
        grid=(count,), prefetch=[places, ctx_at],
    )[0]


def lane_sums(v):
    cols = v.shape[-1]
    head = lax.broadcasted_iota(jnp.int32, (cols, cols), 0) // HEAD_DIM
    same = (head == lax.broadcasted_iota(jnp.int32, (cols, cols), 1) // HEAD_DIM).astype(BF16)
    high = v.astype(BF16)
    low = (v - high.astype(F32)).astype(BF16)
    return mm(high, same) + mm(low, same)


def head_factors(raw):
    return lax.rsqrt(lane_sums(raw * raw) * (1.0 / HEAD_DIM) + EPSILON)


def turn(v):
    parts = [
        pltpu.roll(v[:, at : at + HEAD_DIM], HEAD_DIM // 2, 1) for at in range(0, v.shape[1], HEAD_DIM)
    ]
    return parts[0] if len(parts) == 1 else jnp.concatenate(parts, axis=1)


def rotated(v, cos, sin):
    return v * cos + turn(v) * sin


def rope(raw, gain, cos, sin):
    return rotated(raw * head_factors(raw) * gain, cos, sin)


def twice(ref):
    return jnp.concatenate([ref[...]] * 2, axis=1)


def project_queries(x, weights, gain, cos, sin):
    rows, width = x.shape
    cols = HEADS * HEAD_DIM
    block = 2 * HEAD_DIM
    each = 2 * block
    col = pl.BlockSpec((rows, each), lambda j: (0, j))

    def body(x_ref, w_ref, g_ref, c_ref, s_ref, raw_ref, rot_ref, fac_ref):
        g, c, s = twice(g_ref), twice(c_ref), twice(s_ref)
        for j in range(each // block):
            at = slice(j * block, (j + 1) * block)
            raw = mm(x_ref[...], w_ref[:, at])
            raw_ref[:, at] = raw.astype(BF16)
            factors = head_factors(raw)
            rot_ref[:, at] = rotated(raw * factors * g, c, s).astype(BF16)
            for h in range(2):
                fac_ref[2 * j + h] = factors[:, h * HEAD_DIM : (h + 1) * HEAD_DIM].T[:8]

    return call(
        "project_queries", body, [x, weights, gain, cos, sin],
        [IN_VMEM, pl.BlockSpec((width, each), lambda j: (0, j))] + [IN_VMEM] * 3,
        [col, col, pl.BlockSpec((each // HEAD_DIM, 8, rows), lambda j: (j, 0, 0))],
        [shape((rows, cols), BF16), shape((rows, cols), BF16), shape((HEADS, 8, rows), F32)],
        grid=(cols // each,),
    )


def project_keys_values(x, weights, gain, cos, sin):
    rows, width = x.shape
    block = 2 * HEAD_DIM
    cols = KV_HEADS * HEAD_DIM
    inner = HEADS * HEAD_DIM
    part = 256

    def body(x_ref, wk_ref, wv_ref, g_ref, c_ref, s_ref, raw_ref, rot_ref, val_ref):
        wk, wv = wk_ref[...], wv_ref[...]
        g = twice(g_ref)
        for i in range(rows // part):
            here = slice(i * part, (i + 1) * part)
            raw = mm(x_ref[here, :], wk)
            raw_ref[here, :] = raw.astype(BF16)
            val_ref[here, :] = mm(x_ref[here, :], wv).astype(BF16)
            c, s = [jnp.concatenate([r[here, :]] * 2, axis=1) for r in (c_ref, s_ref)]
            rot_ref[here, :] = rope(raw, g, c, s).astype(BF16)

    col = pl.BlockSpec((rows, block), lambda j: (0, j))
    return call(
        "project_keys_values", body, [x, weights, weights, gain, cos, sin],
        [
            IN_VMEM,
            pl.BlockSpec((width, block), lambda j: (0, inner // block + j)),
            pl.BlockSpec((width, block), lambda j: (0, (inner + cols) // block + j)),
        ]
        + [IN_VMEM] * 3,
        [col, col, col], [shape((rows, cols), BF16)] * 3, grid=(cols // block,), vmem=room(rows),
    )


LOG2E = 1.4426950408889634


def attend(queries, keys, values, q_low, q_high, k_stream):
    rows = queries.shape[0]
    half = rows // 2
    pack = keys.shape[0]
    pair = GROUPS * HEAD_DIM

    def body(q_ref, k_ref, v_ref, lo_ref, hi_ref, ks_ref, mix_ref, lse_ref, bias):
        @pl.when(pl.program_id(0) == 0)
        def _():
            ks = ks_ref[...]
            ok = (ks >= lo_ref[...]) & (ks <= hi_ref[...])
            bias[...] = jnp.where(ok, 0.0, MASKED)

        v_ones = jnp.concatenate([v_ref[...], jnp.ones((pack, HEAD_DIM), BF16)], axis=1)
        for part in range(2):
            here = slice(part * half, (part + 1) * half)
            seen = pack // 2 if part == 0 else pack
            for j in range(GROUPS):
                cols = slice(j * HEAD_DIM, (j + 1) * HEAD_DIM)
                scores = mm_nt(q_ref[here, cols], k_ref[:seen, :]) * (SCALE * LOG2E) + bias[here, :seen]
                both = mm(jnp.exp2(scores).astype(BF16), v_ones[:seen])
                total = both[:, HEAD_DIM:]
                mix_ref[here, cols] = (both[:, :HEAD_DIM] * (1.0 / total)).astype(BF16)
                lse_ref[j, :, here] = jnp.log2(total).T[:8]

    col = pl.BlockSpec((rows, pair), lambda g: (0, g))
    key = pl.BlockSpec((pack, HEAD_DIM), lambda g: (0, g))
    return call(
        "attend", body, [queries, keys, values, q_low, q_high, k_stream],
        [col, key, key, whole((rows, 1)), whole((rows, 1)), whole((1, pack))],
        [col, pl.BlockSpec((GROUPS, 8, rows), lambda g: (g, 0, 0))],
        [shape((rows, HEADS * HEAD_DIM), BF16), shape((HEADS, 8, rows), F32)],
        grid=(KV_HEADS,), vmem=room(pack),
        scratch=[pltpu.VMEM((rows, pack), F32)],
    )


def high_low(v):
    high = v.astype(BF16)
    return high, (v - high.astype(F32)).astype(BF16)


def middle_block(mixed, lse, factors, tokens, grad, gain, stack):
    rows, inner = mixed.shape
    count, height, width = stack.shape
    unit = width // count
    hidden = 3 * width
    block = 256
    per_row = block // unit if unit < block else 1

    def body(
        mixed_hbm, lse_ref, fac_ref, tok_hbm, dy_hbm, gain_ref, stack_ref,
        out_ref, low_ref, h_ref, both_ref, gm_ref, gb_ref, gg_ref, dm_ref, parcel_ref,
        w, mid, acc, deltas, mixed_ref, tok_ref, dy_ref, sems,
    ):
        def move(first, many, sem):
            here = (slice(None), pl.ds(first * unit, many * unit))
            return pltpu.make_async_copy(stack_ref.at[here], w.at[here], sems.at[sem])

        loads = [
            pltpu.make_async_copy(a, b, sems.at[8 + i])
            for i, (a, b) in enumerate(((mixed_hbm, mixed_ref), (tok_hbm, tok_ref), (dy_hbm, dy_ref)))
        ]
        loads[0].start()
        out_copy = move(9, 2, 0)
        gate_copies = [move(3 + i, 1, 1 + i) for i in range(3)]
        up_copies = [move(6 + i, 1, 4 + i) for i in range(3)]
        down_copy = move(0, 3, 7)
        for copy in (out_copy, loads[1], loads[2]):
            copy.start()
        for copy in [out_copy] + loads:
            copy.wait()
        for a, b in zip(gate_copies, up_copies):
            a.start()
            b.start()
        down_copy.start()

        for j in range(width // block):
            cols = slice(j * block, (j + 1) * block)
            part = w[:, 9 * unit : 11 * unit, cols].reshape(inner, block)
            mid[:, cols] = tok_ref[:, cols].astype(F32) + mm(mixed_ref[...], part)
        x = mid[...]
        low_ref[...] = (x * factor_of(x) * gain_ref[...]).astype(BF16)

        for i in range(3):
            gate_copies[i].wait()
            up_copies[i].wait()

            def forward(j, _):
                cols = pl.ds(pl.multiple_of(j * block, block), block)
                to = pl.ds(pl.multiple_of(i * width + j * block, block), block)
                g = mm(low_ref[...], w[:, (3 + i) * unit : (4 + i) * unit, cols].reshape(width, block))
                u = mm(low_ref[...], w[:, (6 + i) * unit : (7 + i) * unit, cols].reshape(width, block))
                s = 1.0 / (1.0 + jnp.exp(-g))
                act = g * s
                h_ref[:, to] = (act * u).astype(BF16)
                both_ref[0, :, to] = (u * (s + act * (1.0 - s))).astype(BF16)
                both_ref[1, :, to] = act.astype(BF16)
                return 0

            lax.fori_loop(0, width // block, forward, 0, unroll=True)

        down_copy.wait()
        acc[...] = mid[...]
        wide = 384
        owners = wide // (3 * unit)

        def down(j, _):
            cols = pl.ds(pl.multiple_of(j * wide, wide), wide)
            part = w[pl.ds(j * owners, owners), 0 : 3 * unit, :].reshape(wide, width)
            dh = mm_nt(dy_ref[...], part)
            both_ref[0, :, cols] = (both_ref[0, :, cols].astype(F32) * dh).astype(BF16)
            both_ref[1, :, cols] = (both_ref[1, :, cols].astype(F32) * dh).astype(BF16)
            acc[...] += mm(h_ref[:, cols], part)
            return 0

        lax.fori_loop(0, hidden // wide, down, 0, unroll=True)
        out_ref[...] = acc[...].astype(BF16)

        owners_in = block // unit
        for b in range(width // block):
            at = slice(b * owners_in, (b + 1) * owners_in)
            total = None
            for i in range(3):
                cols = slice(i * width, (i + 1) * width)
                for side in range(2):
                    first = (3 + 3 * side + i) * unit
                    part = w[at, first : first + unit, :].reshape(block, width)
                    term = mm_nt(both_ref[side, :, cols], part)
                    total = term if total is None else total + term
            acc[:, b * block : (b + 1) * block] = total

        back, terms = norm_back(mid[...], gain_ref[...], acc[...])
        grad_mid = dy_ref[...].astype(F32) + back
        gm_ref[...] = grad_mid
        gb_ref[...] = grad_mid.astype(BF16)
        gg_ref[...] = jnp.sum(terms, axis=0, keepdims=True)

        owners_out = block // (2 * unit)

        def mixed_back(j, _):
            cols = pl.ds(pl.multiple_of(j * block, block), block)
            part = w[pl.ds(j * owners_out, owners_out), 9 * unit : 11 * unit, :].reshape(block, width)
            dm = mm_nt(gb_ref[...], part).astype(BF16)
            dm_ref[:, cols] = dm
            terms = (dm.astype(F32) * mixed_ref[:, cols].astype(F32)).T
            for k in range(block // HEAD_DIM):
                delta = jnp.sum(terms[k * HEAD_DIM : (k + 1) * HEAD_DIM], axis=0, keepdims=True)
                deltas[pl.ds(j * (block // HEAD_DIM) + k, 1), :] = delta
            return 0

        lax.fori_loop(0, inner // block, mixed_back, 0, unroll=True)
        parcel_ref[:rows, :] = gb_ref[...]
        parcel_ref[rows:, :] = jnp.zeros((3 * HEADS, width), BF16)
        extras = (lse_ref[:, 0, :], deltas[...], fac_ref[:, 0, :])
        for which, values in enumerate(extras):
            at = rows + which * HEADS
            for side, piece in enumerate(high_low(values)):
                parcel_ref[at : at + HEADS, side * rows : (side + 1) * rows] = piece

    full = (rows, width)
    return call(
        "middle_block", body, [mixed, lse, factors, tokens, grad, gain, stack],
        [IN_HBM, whole(lse.shape), whole(factors.shape), IN_HBM, IN_HBM, whole((1, width)), IN_HBM],
        [whole(full), IN_VMEM, IN_VMEM, IN_VMEM, whole(full), IN_VMEM, IN_VMEM, whole((rows, inner)), IN_VMEM],
        [
            shape(full, BF16), shape(full, BF16), shape((rows, hidden), BF16),
            shape((2, rows, hidden), BF16), shape(full, F32), shape(full, BF16),
            shape((1, width), F32), shape((rows, inner), BF16), shape((rows + 3 * HEADS, width), BF16),
        ],
        scratch=[
            pltpu.VMEM((count, height, width), BF16),
            pltpu.VMEM(full, F32),
            pltpu.VMEM(full, F32),
            pltpu.VMEM((HEADS, rows), F32),
            pltpu.VMEM((rows, inner), BF16),
            pltpu.VMEM(full, BF16),
            pltpu.VMEM(full, BF16),
            pltpu.SemaphoreType.DMA((11,)),
        ],
        vmem=44,
    )


def head_norm_back(v, gain, incoming):
    f = head_factors(v)
    weighted = incoming * gain
    inner = lane_sums(weighted * v) * (1.0 / HEAD_DIM)
    return f * (weighted - v * (f * f * inner)), incoming * v * f


def query_back(
    queries, grad_mixed, mixed, keys, values, lse, q_low, q_high, k_stream, query_raw, gain, cos, sin,
    first, count, earlier=(),
):
    rows = queries.shape[0]
    half = rows // 2
    pack = keys.shape[0]
    pair = GROUPS * HEAD_DIM

    def body(
        q_ref, do_ref, mix_ref, k_ref, v_ref, lse_ref, lo_ref, hi_ref, ks_ref, raw_ref, g_ref, c_ref, s_ref,
        *rest,
    ):
        dq_ref, gg_ref, bias = rest[len(earlier) :]

        @pl.when(pl.program_id(0) == 0)
        def _():
            ks = ks_ref[...]
            ok = (ks >= lo_ref[...]) & (ks <= hi_ref[...])
            bias[...] = jnp.where(ok, 0.0, MASKED)
            gg_ref[...] = jnp.zeros_like(gg_ref)

        deltas = lane_sums(do_ref[...].astype(F32) * mix_ref[...].astype(F32))
        for j in range(GROUPS):
            cols = slice(j * HEAD_DIM, (j + 1) * HEAD_DIM)
            lse_col = jnp.broadcast_to(lse_ref[j, 0:1, :], (HEAD_DIM, rows)).T[:, :1]
            grads = []
            for part in range(2):
                here = slice(part * half, (part + 1) * half)
                seen = pack // 2 if part == 0 else pack
                scores = mm_nt(q_ref[here, cols], k_ref[:seen, :]) * (SCALE * LOG2E) + bias[here, :seen]
                probs = jnp.exp2(scores - lse_col[here])
                d_probs = mm_nt(do_ref[here, cols], v_ref[:seen, :])
                d_scores = (probs * (d_probs - deltas[here, cols][:, :1])).astype(BF16)
                grads.append(mm(d_scores, k_ref[:seen, :]))
            dq = jnp.concatenate(grads, axis=0) * SCALE
            dq = dq * c_ref[...] - turn(dq) * s_ref[...]
            dq, terms = head_norm_back(raw_ref[:, cols].astype(F32), g_ref[...], dq)
            dq_ref[:, cols] = dq.astype(BF16)
            gg_ref[...] += jnp.sum(terms, axis=0, keepdims=True)

    col = pl.BlockSpec((rows, pair), lambda g: (0, first + g))
    key = pl.BlockSpec((pack, HEAD_DIM), lambda g: (0, first + g))
    return call(
        "query_back", body,
        [queries, grad_mixed, mixed, keys, values, lse, q_low, q_high, k_stream, query_raw, gain, cos, sin, *earlier],
        [
            col, col, col, key, key,
            pl.BlockSpec((GROUPS, 8, rows), lambda g: (first + g, 0, 0)),
            whole((rows, 1)), whole((rows, 1)), whole((1, pack)),
            col, whole((1, HEAD_DIM)), whole((rows, HEAD_DIM)), whole((rows, HEAD_DIM)),
        ]
        + [ANY] * len(earlier),
        [col, whole((1, HEAD_DIM))],
        [shape((rows, HEADS * HEAD_DIM), BF16), shape((1, HEAD_DIM), F32)],
        grid=(count,), vmem=room(pack),
        scratch=[pltpu.VMEM((rows, pack), F32)],
        aliases={13: 0} if earlier else None,
    )


def key_back(
    queries, grad_mixed, keys, values, far, q_low, q_high, k_stream, key_raw, gain, cos, sin,
    ctx_at, ctx_size, first, count, earlier=(),
):
    pack = queries.shape[0]
    rows = pack // ctx_size
    half = rows // 2
    pair = GROUPS * HEAD_DIM

    def body(
        at_ref, q_ref, do_ref, k_ref, v_ref, far_ref, lo_ref, hi_ref, ks_ref, raw_ref, g_ref,
        c_ref, s_ref, *rest,
    ):
        out_ref, gg_ref, bias, acc = rest[len(earlier) :]

        @pl.when(pl.program_id(0) == 0)
        def _():
            ks = ks_ref[...]
            ok = (ks >= lo_ref[...]) & (ks <= hi_ref[...])
            bias[...] = jnp.where(ok, 0.0, MASKED)
            gg_ref[...] = jnp.zeros_like(gg_ref)

        k_own = k_ref[...].reshape(rows, HEAD_DIM)
        v_own = v_ref[...].reshape(rows, HEAD_DIM)
        for j in range(GROUPS):
            cols = slice(j * HEAD_DIM, (j + 1) * HEAD_DIM)
            head = GROUPS * (first + pl.program_id(0)) + j
            lse, delta, factors = [far_ref[pl.ds(i * HEADS + head, 1), :] for i in range(3)]
            for late in range(2):
                there = slice(late * pack // 2, (late + 1) * pack // 2)
                here = slice(0, rows if late else half)
                qq, dd = q_ref[there, cols], do_ref[there, cols]
                factor = factors[:, there]
                scores = mm_nt(k_own[here], qq) * (factor * (SCALE * LOG2E)) + bias[here, there]
                probs = jnp.exp2(scores - lse[:, there])
                d_probs = mm_nt(v_own[here], dd)
                d_scores = (probs * factor * (d_probs - delta[:, there])).astype(BF16)
                dv = mm(probs.astype(BF16), dd)
                dk = mm(d_scores, qq)
                if j == 0 and late == 0:
                    acc[...] = jnp.zeros_like(acc)
                acc[0, here, :] += dk
                acc[1, here, :] += dv
        out_ref[1] = acc[1].astype(BF16)
        dk = acc[0] * SCALE
        dk = dk * c_ref[...] - turn(dk) * s_ref[...]
        dk, terms = head_norm_back(raw_ref[...].astype(F32).reshape(rows, HEAD_DIM), g_ref[...], dk)
        out_ref[0] = dk.astype(BF16)
        gg_ref[...] += jnp.sum(terms, axis=0, keepdims=True)

    col = pl.BlockSpec((pack, pair), lambda g, at: (0, first + g))
    key = pl.BlockSpec((2, 1, half, HEAD_DIM), lambda g, at: (0, at[0], 0, first + g))
    laid = (2, ctx_size, half, KV_HEADS * HEAD_DIM)
    return call(
        "key_back", body,
        [
            queries, grad_mixed, keys.reshape(laid), values.reshape(laid), far, q_low, q_high, k_stream, key_raw.reshape(laid), gain, cos, sin, *earlier,
        ],
        [
            col, col, key, key, whole(far.shape), whole((1, pack)), whole((1, pack)), whole((rows, 1)),
            key, whole((1, HEAD_DIM)), whole((rows, HEAD_DIM)), whole((rows, HEAD_DIM)),
        ]
        + [ANY] * len(earlier),
        [pl.BlockSpec((2, rows, HEAD_DIM), lambda g, at: (0, 0, first + g)), whole((1, HEAD_DIM))],
        [shape((2, rows, KV_HEADS * HEAD_DIM), BF16), shape((1, HEAD_DIM), F32)],
        grid=(count,), vmem=room(pack),
        scratch=[pltpu.VMEM((rows, pack), F32), pltpu.VMEM((2, rows, HEAD_DIM), F32)],
        prefetch=[ctx_at], aliases={12: 0} if earlier else None,
    )


def all_queries(x, weights, gain, cos, sin):
    rows, width = x.shape
    cols = HEADS * HEAD_DIM
    block = 2 * HEAD_DIM
    part = 256

    def body(x_ref, w_ref, g_ref, c_ref, s_ref, rot_ref):
        g = twice(g_ref)
        for i in range(rows // part):
            here = slice(i * part, (i + 1) * part)
            raw = mm(x_ref[here, :], w_ref[...])
            c, s = [jnp.concatenate([r[here, :]] * 2, axis=1) for r in (c_ref, s_ref)]
            rot_ref[here, :] = rotated(raw * g, c, s).astype(BF16)

    return call(
        "all_queries", body, [x, weights, gain, cos, sin],
        [IN_VMEM, pl.BlockSpec((width, block), lambda j: (0, j)), IN_VMEM, IN_VMEM, IN_VMEM],
        [pl.BlockSpec((rows, block), lambda j: (0, j))], [shape((rows, cols), BF16)],
        grid=(cols // block,), vmem=room(rows),
    )[0]


def all_grad_mixed(own, parcels, stack, places, ctx_at, rows):
    count = (len(parcels) + 1) // 2
    numbers = parcels[0].shape[0] - rows
    half = rows // 2
    inner = own.shape[1]
    _, _, width = stack.shape
    owners = stack.shape[0]
    unit = width // owners

    def body(places_ref, at_ref, own_ref, a_ref, b_ref, *refs):
        blocks, (out_ref, far_ref, turned) = refs[:-3], refs[-3:]
        step = pl.program_id(0)
        me = at_ref[0]

        def spread(ref):
            both = ref[rows:, :rows].astype(F32) + ref[rows:, rows : 2 * rows].astype(F32)
            far_ref[0, 0] = both[:, :half]
            far_ref[1, 0] = both[:, half:]

        @pl.when(step == 0)
        def _():
            spread(blocks[0])
            out_ref[...] = own_ref[...].reshape(2, 1, half, inner)
            turned[...] = jnp.concatenate([a_ref[...], b_ref[...]], axis=1).reshape(inner, width)

        def write(ref):
            spread(ref)
            for j in range(inner // 512):
                at = slice(j * 512, (j + 1) * 512)
                part = mm_nt(ref[:rows, :], turned[at, :]).astype(BF16)
                out_ref[:, :, :, at] = part.reshape(2, 1, half, 512)

        for s in range(1, count):

            @pl.when((step == s) & (me >= s))
            def _():
                write(blocks[s])

            @pl.when((step == s) & (me < s))
            def _():
                write(blocks[count - 1 + count - s])

    return call(
        "all_grad_mixed", body, [own, stack, stack, *parcels],
        [
            IN_VMEM,
            pl.BlockSpec((owners, unit, width), lambda *_: (0, 9, 0)),
            pl.BlockSpec((owners, unit, width), lambda *_: (0, 10, 0)),
        ]
        + [whole(parcel.shape) for parcel in parcels],
        [
            pl.BlockSpec((2, 1, half, inner), lambda k, at, me: (0, at[k], 0, 0)),
            pl.BlockSpec((2, 1, numbers, half), lambda k, at, me: (0, at[k], 0, 0)),
        ],
        [shape((2, count, half, inner), BF16), shape((2, count, numbers, half), F32)],
        grid=(count,), scratch=[pltpu.VMEM((inner, width), BF16)], prefetch=[places, ctx_at], vmem=32,
    )


def normed_back(d_queries, d_pair, weights):
    rows, inner = d_queries.shape
    cols = d_pair.shape[2]
    width = weights.shape[0]

    def body(dq_ref, pair_ref, wq_ref, wk_ref, wv_ref, out_ref):
        part = mm_nt(dq_ref[...], wq_ref[...])
        part += mm_nt(pair_ref[0], wk_ref[...])
        part += mm_nt(pair_ref[1], wv_ref[...])
        out_ref[...] = part

    block = 256
    return call(
        "normed_back", body, [d_queries, d_pair, weights, weights, weights],
        [
            IN_VMEM,
            IN_VMEM,
            pl.BlockSpec((block, inner), lambda j: (j, 0)),
            pl.BlockSpec((block, cols), lambda j: (j, inner // cols)),
            pl.BlockSpec((block, cols), lambda j: (j, inner // cols + 1)),
        ],
        [pl.BlockSpec((rows, block), lambda j: (0, j))],
        [shape((rows, width), F32)],
        grid=(width // block,),
    )[0]


def input_back(d_normed, tokens, gain, grad_middle):
    rows, width = tokens.shape

    def body(a_ref, t_ref, gain_ref, gm_ref, out_ref, gg_ref):
        back, terms = norm_back(t_ref[...].astype(F32), gain_ref[...], a_ref[...])
        out_ref[...] = (gm_ref[...] + back).astype(BF16)
        gg_ref[...] = jnp.sum(terms, axis=0, keepdims=True)

    return call(
        "input_back", body, [d_normed, tokens, gain, grad_middle],
        [IN_VMEM] * 4,
        [whole((rows, width)), IN_VMEM],
        [shape((rows, width), BF16), shape((1, width), F32)],
    )


def weight_grad(left, right, owners=None, cols=None, block=512, apart=False, beside=False):
    tokens, rows = left.shape
    count = 1 if owners is None else owners.shape[0]
    unit = rows // count
    deep = right.ndim == 3
    first, each = cols or (0, right.shape[-1])
    width = each * (right.shape[0] if deep else 1)
    steps = width // block
    split = owners is not None
    results = 2 * (right.shape[0] if apart else 1) if split else 1

    def body(*refs):
        if split:
            own_ref, refs = refs[0], refs[1:]
        l_ref, r_ref, refs = refs[0], refs[1], refs[2:]
        outs, scratch = refs[:results], refs[results:]

        @pl.when(pl.program_id(0) == 0)
        def _():
            scratch[0][...] = l_ref[...].T
            for k in range(count if split else 0):
                at = pl.multiple_of(own_ref[k] * unit, unit)
                scratch[1][k * unit : (k + 1) * unit, :] = scratch[0][pl.ds(at, unit), :]

        def block_at(j):
            if deep:
                per = each // block
                return r_ref[j // per, :, pl.ds(pl.multiple_of(first + (j % per) * block, block), block)]
            return r_ref[:, pl.ds(pl.multiple_of(first + j * block, block), block)]

        if not split:
            outs[0][...] = mm(scratch[0][...], block_at(pl.program_id(0))).astype(BF16)
            return
        per = each // block
        for j in range(steps):
            at = 2 * (j // per) if apart else 0
            to = slice((j % per) * block, (j % per + 1) * block) if apart else slice(j * block, (j + 1) * block)
            for side in range(2):
                here = slice(side * rows // 2, (side + 1) * rows // 2)
                part = mm(scratch[1][here, :], block_at(j)).astype(BF16)
                part = part.reshape(count // 2, unit, block)
                if beside:
                    outs[side][:, :, to] = part[:, : unit // 2]
                    outs[side][:, :, width + j * block : width + (j + 1) * block] = part[:, unit // 2 :]
                else:
                    outs[at + side][:, :, to] = part

    if split:
        out = [IN_VMEM] * results
        dims = (count // 2, unit // 2, 2 * width) if beside else (count // 2, unit, each if apart else width)
        out_shape = [shape(dims, BF16)] * results
    else:
        out = [pl.BlockSpec((rows, block), lambda j: (0, j))]
        out_shape = [shape((rows, width), BF16)]
    return call(
        "weight_grad", body, [left, right], [IN_VMEM] * 2, out, out_shape,
        grid=(1 if split else steps,),
        scratch=[pltpu.VMEM((rows, tokens), BF16)] * (1 + split),
        prefetch=[owners] if split else (),
    )


def fold(items, steps=1):
    arrays = []

    def slot(term):
        for i, known in enumerate(arrays):
            if known is term:
                return i
        arrays.append(term)
        return len(arrays) - 1

    laid = [([slot(t) for t in terms], rows, bit) for terms, rows, bit in items]
    in_specs = []
    for a in arrays:
        in_specs.append(
            IN_VMEM if steps == 1 else pl.BlockSpec(a.shape[:2] + (a.shape[2] // steps,), lambda j: (0, 0, j))
        )
    out_specs, out_shape = [], []
    for slots, (_, rows), bit in laid:
        many, _, cols = arrays[slots[0]].shape
        dims = (many, rows, cols) if bit is None else (many // 2, rows, cols)
        for _ in range(1 if bit is None else 2):
            out_specs.append(
                IN_VMEM if steps == 1 else pl.BlockSpec(dims[:2] + (cols // steps,), lambda j: (0, 0, j))
            )
            out_shape.append(shape(dims, BF16))

    def body(*refs):
        ins, outs = refs[: len(arrays)], list(refs[len(arrays) :])
        for slots, (first, rows), bit in laid:
            here = slice(first, first + rows)
            many = arrays[slots[0]].shape[0]

            def total(k):
                value = ins[slots[0]][k, here, :].astype(F32)
                for at in slots[1:]:
                    value = value + ins[at][k, here, :].astype(F32)
                return value.astype(BF16)

            if bit is None:
                out = outs.pop(0)
                for k in range(many):
                    out[k] = total(k)
                continue
            sent, kept = outs.pop(0), outs.pop(0)
            places = [0, 0]
            for k in range(many):
                with_bit = (k >> bit) & 1
                (sent if with_bit else kept)[places[with_bit]] = total(k)
                places[with_bit] += 1

    return call("fold", body, arrays, in_specs, out_specs, out_shape, grid=(steps,))


def choose(first, second, dims, odd):
    arrays = [a for a, _ in first + second]
    views = [v for _, v in first + second]

    def body(odd_ref, *refs):
        ins, (sent, kept) = refs[: len(arrays)], refs[len(arrays) :]

        def total(begin, end):
            value = ins[begin][views[begin]].astype(F32)
            for at in range(begin + 1, end):
                value = value + ins[at][views[at]].astype(F32)
            return value.astype(BF16)

        @pl.when(odd_ref[0] == 1)
        def _():
            sent[...] = total(0, len(first))
            kept[...] = total(len(first), len(arrays))

        @pl.when(odd_ref[0] == 0)
        def _():
            kept[...] = total(0, len(first))
            sent[...] = total(len(first), len(arrays))

    return call(
        "choose", body, arrays, [IN_VMEM] * len(arrays), [IN_VMEM] * 2, [shape(dims, BF16)] * 2,
        prefetch=[odd],
    )


def place(sums, odd, out_dims, cuts):
    arrays = [a for pair in sums for a in pair]

    def body(odd_ref, *refs):
        ins, outs = refs[: len(arrays)], refs[len(arrays) :]

        def write(swapped):
            for which, half, source, at, target in cuts:
                outs[at][target] = ins[2 * which + (half ^ swapped)][source].astype(F32)

        @pl.when(odd_ref[0] == 1)
        def _():
            write(1)

        @pl.when(odd_ref[0] == 0)
        def _():
            write(0)

    return call(
        "place", body, arrays, [IN_VMEM] * len(arrays), [whole(d) for d in out_dims],
        [shape(d, F32) for d in out_dims], prefetch=[odd],
    )


def swap(x, axis, bit):
    size = lax.axis_size(axis)
    return lax.ppermute(x, axis, [(i, i ^ bit) for i in range(size)])


def bits_of(size):
    return [1 << b for b in range(size.bit_length() - 1)]


def gather_pieces(own, cut):
    rest = bits_of(lax.axis_size("dp"))[1:]
    spans = [slice(0, cut), slice(cut, own.shape[1])]
    everything = slice(0, own.shape[1])
    held = {0: [(everything, own)]}
    for bit in rest:
        held[bit] = [(everything, swap(own, "dp", bit))]
    first = [held[bit][0][1] for bit in rest]
    for at in range(1 << len(rest)):
        at = 2 * at
        if at in held:
            continue
        held[at] = []
        for span, order in zip(spans, (rest, rest[::-1])):
            last = [bit for bit in order if at & bit][-1]
            before = held[at ^ last]
            source = before[0][1][:, span] if len(before) == 1 else before[spans.index(span)][1]
            held[at].append((span, swap(source, "dp", last)))
    for at in sorted(held):
        held[at | 1] = [(span, swap(piece, "dp", 1)) for span, piece in held[at]]
    return held, first


class Sum:
    def __init__(self, kept, sent, halves, odd):
        self.rest = bits_of(lax.axis_size("dp"))[1:]
        self.order = [list(range(len(self.rest))), list(range(len(self.rest)))[::-1]]
        self.left = [list(range(len(self.rest))), list(range(len(self.rest)))]
        self.odd = odd
        arrived = [swap(s, "dp", 1) for s in sent]
        if len(kept) == 1:
            kept, arrived = kept * 2, arrived * 2
        self.terms = [[k, a] for k, a in zip(kept, arrived)]
        self.rows = halves
        self.stage = 0

    def over_dp(self, steps=1):
        bits = [order[self.stage] for order in self.order]
        items = [
            (terms, rows, left.index(bit))
            for terms, rows, left, bit in zip(self.terms, self.rows, self.left, bits)
        ]
        sent0, kept0, sent1, kept1 = fold(items, steps)
        self.terms = [
            [kept, swap(sent, "dp", self.rest[bit])]
            for kept, sent, bit in zip((kept0, kept1), (sent0, sent1), bits)
        ]
        self.rows = [(0, k.shape[1]) for k in (kept0, kept1)]
        for left, bit in zip(self.left, bits):
            left.remove(bit)
        self.stage += 1

    def joined(self):
        dims = [terms[0].shape[1:] for terms in self.terms]
        arrays = [term for terms in self.terms for term in terms]
        many = len(self.terms[0])

        def body(*refs):
            at = 0
            for part, (rows, _) in enumerate(dims):
                value = refs[part * many][0].astype(F32)
                for k in range(1, many):
                    value = value + refs[part * many + k][0].astype(F32)
                refs[-1][at : at + rows, :] = value.astype(BF16)
                at += rows

        total = (sum(rows for rows, _ in dims), dims[0][1])
        return call(
            "joined", body, arrays, [IN_VMEM] * len(arrays), [IN_VMEM], [shape(total, BF16)]
        )[0]

    def to_ctx(self):
        first, second = [[(t, 0) for t in terms] for terms in self.terms]
        self.begin_ctx(first, second, first[0][0].shape[1:])

    def begin_ctx(self, first, second, dims):
        sent, kept = choose(first, second, dims, self.odd)
        self.total, self.next = [kept, swap(sent, "ctx", 1)], bits_of(lax.axis_size("ctx"))[1:]

    def over_ctx(self):
        a, b = [t[None] for t in self.total]
        total = fold([([a, b], (0, a.shape[1]), None)])[0][0]
        if self.next:
            self.total = [total, swap(total, "ctx", self.next.pop(0))]
        else:
            self.total = [total, swap(total, "ctx", 1)]


class Line:
    def __init__(self, total):
        size = lax.axis_size("ctx")
        middle = size // 2
        self.hops = [("add", [(k, k + 1), (size - 1 - k, size - 2 - k)]) for k in range(middle - 1)]
        self.hops.append(("add", [(middle - 1, middle), (middle, middle - 1)]))
        for k in reversed(range(middle - 1)):
            self.hops.append(("take", [(k + 1, k), (size - 2 - k, size - 1 - k)]))
        self.total = total
        self.send()

    def send(self):
        self.kind, pairs = self.hops.pop(0)
        self.takers = [b for _, b in pairs]
        self.came = lax.ppermute(self.total, "ctx", pairs)

    def taking(self):
        at = lax.axis_index("ctx")
        return sum((at == taker).astype(jnp.int32) for taker in self.takers)[None]

    def step(self):
        if self.kind == "add":
            rows = self.total.shape[0]
            self.total = fold([([self.total[None], self.came[None]], (0, rows), None)])[0][0]
        else:
            self.total = jnp.where(self.taking()[0] == 1, self.came, self.total)
        self.send()

    def finish(self):
        while self.hops:
            self.step()

    def place(self, out_dims, cuts):
        cuts = [(0, 0, source, at, target) for source, at, target in cuts]
        if self.kind == "add":
            self.total, self.came = fold([([self.total[None], self.came[None]], (0, self.total.shape[0]), None)])[0][0], self.total
            return place([(self.total, self.came)], jnp.zeros((1,), jnp.int32), out_dims, cuts)
        return place([(self.total, self.came)], self.taking(), out_dims, cuts)


class Relay:
    def __init__(self, block):
        self.size = lax.axis_size("ctx")
        self.from_left, self.from_right = [], []
        self.send(block, block)

    def send(self, right, left):
        step = len(self.from_left)
        self.from_left.append(lax.ppermute(right, "ctx", [(i, i + 1) for i in range(step, self.size - 1)]))
        self.from_right.append(
            lax.ppermute(left, "ctx", [(i + 1, i) for i in range(self.size - 1 - step)])
        )

    def step(self):
        came = [self.from_left[-1], self.from_right[-1]]
        self.send(
            *copies(
                "pass_on", came, lambda _, ins, outs: list(zip(ins, outs)),
                [shape(c.shape, c.dtype) for c in came],
                in_specs=[whole(c.shape) for c in came], out_specs=[whole(c.shape) for c in came],
            )
        )

    def finish(self):
        while len(self.from_left) < self.size - 1:
            self.step()


class Everywhere:
    def __init__(self, x):
        self.left = [("dp", bit) for bit in bits_of(lax.axis_size("dp"))]
        self.left += [("ctx", bit) for bit in bits_of(lax.axis_size("ctx"))]
        self.total = x
        self.came = swap(x, *self.left.pop(0))

    def step(self):
        def body(a_ref, b_ref, out_ref):
            out_ref[...] = a_ref[...] + b_ref[...]

        self.total = call(
            "add_small", body, [self.total, self.came], [IN_VMEM] * 2, [IN_VMEM],
            [shape(self.total.shape, F32)],
        )[0]
        if self.left:
            self.came = swap(self.total, *self.left.pop(0))
            return True
        return False

    def finish(self):
        while self.step():
            pass
        return self.total


def on_device(
    tokens, doc_starts, attn_gain, w_query, w_key, w_value, w_out,
    query_gain, key_gain, mlp_gain, w_gate, w_up, w_down, cotangent,
):
    ORDER.clear()
    rows, width = tokens.shape[1], tokens.shape[2]
    stretch = rows // 2
    ctx_size = lax.axis_size("ctx")
    dp_size = lax.axis_size("dp")
    ctx_at = lax.axis_index("ctx")
    dp_at = lax.axis_index("dp")
    pack_rows = rows * ctx_size
    unit = width // dp_size
    inner = HEADS * HEAD_DIM
    own_tokens = tokens[0]
    grad_out = cotangent[0]
    starts = doc_starts[0]
    odd = (ctx_at % 2).astype(jnp.int32)[None]
    dp_bits = bits_of(dp_size)

    gains = jnp.concatenate(
        [attn_gain[:, None], mlp_gain[:, None], jnp.zeros((unit, HEAD_DIM - 2), BF16)], axis=1
    )

    def packing(_, ins, outs):
        at = 0
        for ref in ins:
            yield ref.at[:, :], outs[0].at[:, pl.ds(at, ref.shape[1])]
            at += ref.shape[1]

    def stacking(_, ins, outs):
        down, gate, up, out = ins
        stack_ref = outs[0]
        yield down.at[:, :], stack_ref.at[pl.ds(0, 3 * unit)]
        for i in range(3):
            cols = pl.ds(i * width, width)
            yield gate.at[:, cols], stack_ref.at[pl.ds((3 + i) * unit, unit)]
            yield up.at[:, cols], stack_ref.at[pl.ds((6 + i) * unit, unit)]
        yield out.at[:, :], stack_ref.at[pl.ds(9 * unit, 2 * unit)]

    attn_cols = inner + 2 * width + HEAD_DIM
    own_attn = copies(
        "pack_attn", [w_query, w_key, w_value, gains], packing, [shape((unit, attn_cols), BF16)],
        in_specs=[whole(w.shape) for w in (w_query, w_key, w_value)] + [IN_VMEM],
    )[0]
    pieces, first_pieces = gather_pieces(own_attn, inner)
    gathered = Relay(own_tokens)
    stack_in = copies(
        "pack_stack", [w_down, w_gate, w_up, w_out], stacking, [shape((11 * unit, width), BF16)],
        in_specs=[whole(w.shape) for w in (w_down, w_gate, w_up, w_out)],
        out_specs=[whole((11 * unit, width))],
    )[0]
    stack = lax.all_gather(stack_in, "dp", axis=0)
    gathered.step()
    touch(first_pieces)
    gathered.finish()
    from_left, from_right = gathered.from_left, gathered.from_right

    place_at = jnp.arange(pack_rows, dtype=jnp.int32)
    in_half = place_at % (pack_rows // 2)
    part, device, row = place_at // (pack_rows // 2), in_half // stretch, place_at % stretch
    key_stream = stream_index(device * rows + part * stretch + row, stretch, ctx_size)
    query_stream = stream_index(
        ctx_at * rows + jnp.arange(rows, dtype=jnp.int32), stretch, ctx_size
    )
    key_open = opening_of(key_stream, starts)
    query_open = opening_of(query_stream, starts)
    cos_pack, sin_pack = rotary(key_stream - key_open)
    cos_own, sin_own = rotary(query_stream - query_open)

    owners = (dp_at ^ jnp.arange(dp_size, dtype=jnp.int32)).astype(jnp.int32)
    listed = [(k, span, piece) for k in range(dp_size) for span, piece in pieces[k]]

    def assembling(prefetch, ins, outs):
        for (k, span, _), ref in zip(listed, ins):
            at = pl.multiple_of(prefetch[0][k] * unit, unit)
            cols = pl.ds(span.start, span.stop - span.start)
            yield ref.at[:, :], outs[0].at[pl.ds(at, unit), cols]
            if span.stop == attn_cols:
                last = ref.shape[1] - HEAD_DIM
                yield ref.at[:, pl.ds(last, HEAD_DIM)], outs[1].at[pl.ds(at, unit), :]

    attn_w, gain_cols = copies(
        "assemble_weights", [piece for _, _, piece in listed], assembling,
        [shape((width, attn_cols), BF16), shape((width, HEAD_DIM), BF16)], prefetch=[owners],
        out_specs=[whole((width, attn_cols)), IN_VMEM],
    )
    gain_rows = gain_cols[:, :2].astype(F32).T
    gain_attn, gain_mlp = gain_rows[0:1], gain_rows[1:2]
    gain_query = query_gain.astype(F32)[None, :]
    gain_key = key_gain.astype(F32)[None, :]

    normed = norm_own(own_tokens, gain_attn)
    query_raw, queries, factors = project_queries(normed, attn_w, gain_query, cos_own, sin_own)
    places = ((ctx_at - jnp.arange(ctx_size, dtype=jnp.int32)) % ctx_size).astype(jnp.int32)
    normed_pack = norm_pack(
        own_tokens, from_left, from_right, gain_attn, places, ctx_at.astype(jnp.int32)[None]
    ).reshape(pack_rows, width)
    key_raw, keys, values = project_keys_values(normed_pack, attn_w, gain_key, cos_pack, sin_pack)
    mixed, lse = attend(
        queries, keys, values, query_open[:, None], query_stream[:, None], key_stream[None, :]
    )
    (
        output, normed_mid, hidden, d_both, grad_middle, grad_branch, mlp_part, grad_mixed, parcel,
    ) = middle_block(mixed, lse, factors, own_tokens, grad_out, gain_mlp, stack)

    order = [2 * k for k in range(dp_size // 2)] + [2 * k + 1 for k in range(dp_size // 2)]
    owners = (dp_at ^ jnp.array(order, jnp.int32)).astype(jnp.int32)
    everything = slice(None)
    ctx_steps = len(bits_of(ctx_size))
    later_dp, later_ctx = len(dp_bits) - 2, ctx_steps - 1

    def two_rows(total, half, widths=(width,)):
        cuts, at = [], 0
        for which, each in enumerate(widths):
            for k in range(2):
                to = (slice(k * half, (k + 1) * half), everything)
                cuts.append((0, k, (everything, slice(at, at + each)), which, to))
            at += each
        return place([total.total], odd, [(2 * half, each) for each in widths], cuts)

    def halves_of(pair):
        half = pair[0].shape[1] // 2
        return Sum(pair[:1], pair[1:], [(0, half), (half, half)], odd), half

    half_heads = KV_HEADS // 2
    parcels = Relay(parcel)
    wide_grad = weight_grad(normed_mid, d_both, block=1024)[0]
    wide_grad = lax.psum_scatter(wide_grad, "dp", scatter_dimension=0, tiled=True)
    query_args = (
        queries, grad_mixed, mixed, keys, values, lse, query_open[:, None], query_stream[:, None],
        key_stream[None, :], query_raw, gain_query, cos_own, sin_own,
    )
    d_query, query_part = query_back(*query_args, 0, half_heads)
    out_kept, out_sent = weight_grad(mixed, grad_branch, owners, beside=True)

    parcels.step()

    d_query, query_more = query_back(*query_args, half_heads, half_heads, (d_query,))

    parcels.finish()
    query_kept, query_sent = weight_grad(normed, d_query, owners)
    outer = Sum([out_kept, query_kept], [out_sent, query_sent], [(0, unit), (0, unit)], odd)

    every_query = all_queries(normed_pack, attn_w, gain_query, cos_pack, sin_pack)

    touch([parcels.from_left[-1], parcels.from_right[-1]])
    outer.over_dp()
    wide_grad = copies(
        "take", [wide_grad], lambda _, ins, outs: [(ins[0], outs[0])], [shape(wide_grad.shape, BF16)]
    )[0]
    wide = Line(wide_grad)

    parcels = [parcel] + parcels.from_left + parcels.from_right
    grad_mixed_pack, far = all_grad_mixed(
        grad_mixed, parcels, stack, places, ctx_at.astype(jnp.int32)[None], rows
    )
    grad_mixed_pack = grad_mixed_pack.reshape(pack_rows, inner)
    far = far.transpose(2, 0, 1, 3).reshape(3 * HEADS, pack_rows)
    key_args = (
        every_query, grad_mixed_pack, keys, values, far,
        key_open[None, :], key_stream[None, :], query_stream[:, None],
        key_raw, gain_key, cos_own, sin_own, ctx_at.astype(jnp.int32)[None], ctx_size,
    )
    d_pair, key_part = key_back(*key_args, 0, half_heads)

    for _ in range(later_dp):
        outer.over_dp()
    wide.step()
    down_grad = weight_grad(hidden, grad_out, block=256)[0]
    down_grad = lax.psum_scatter(down_grad, "dp", scatter_dimension=0, tiled=True)

    d_pair, key_more = key_back(*key_args, half_heads, half_heads, (d_pair,))
    query_part, key_part = query_part + query_more, key_part + key_more

    outer = Line(outer.joined())
    key_kept, key_sent, value_kept, value_sent = weight_grad(normed, d_pair, owners, apart=True)
    pair = Sum([key_kept, value_kept], [key_sent, value_sent], [(0, unit), (0, unit)], odd)

    d_normed = normed_back(d_query, d_pair, attn_w)
    input_grad, attn_part = input_back(d_normed, own_tokens, gain_attn, grad_middle)

    wide.finish()
    pair.over_dp()
    small = Everywhere(
        jnp.concatenate([attn_part, mlp_part, query_part, key_part], axis=1).reshape(-1, HEAD_DIM)
    )
    small.step()

    for _ in range(later_dp):
        pair.over_dp()
    outer.step()
    small.step()
    down_grad = copies(
        "take", [down_grad], lambda _, ins, outs: [(ins[0], outs[0])], [shape(down_grad.shape, BF16)],
        in_specs=[whole(down_grad.shape)], out_specs=[whole(down_grad.shape)],
    )[0]
    down_sum = lax.psum(down_grad, "ctx")

    pair.to_ctx()
    small.step()
    gate_grad, up_grad = wide.place(
        [(unit, 3 * width)] * 2,
        [((everything, slice(k * 3 * width, (k + 1) * 3 * width)), k, everything) for k in range(2)],
    )

    pair.over_ctx()
    small.step()
    outer.finish()
    touch([down_sum])

    for _ in range(later_ctx):
        pair.over_ctx()
    small = small.finish().reshape(-1)
    near, far_half = slice(0, width), slice(width, 2 * width)
    first, second = slice(0, unit), slice(unit, 2 * unit)
    w_out_grad, query_grad = outer.place(
        [(2 * unit, width), (unit, inner)],
        [
            ((first, near), 0, (first, everything)),
            ((first, far_half), 0, (second, everything)),
            ((second, everything), 1, everything),
        ],
    )
    down_grad = down_sum.astype(F32)
    key_grad, value_grad = place(
        [pair.total], odd, [(unit, width)] * 2, [(0, k, everything, k, everything) for k in range(2)]
    )

    attn_gain_grad = lax.dynamic_slice(small, (dp_at * unit,), (unit,))
    mlp_gain_grad = lax.dynamic_slice(small, (width + dp_at * unit,), (unit,))
    query_gain_grad = small[2 * width : 2 * width + HEAD_DIM]
    key_gain_grad = small[2 * width + HEAD_DIM :]
    return (
        output[None], input_grad[None], attn_gain_grad, query_grad, key_grad, value_grad, w_out_grad,
        query_gain_grad, key_gain_grad, mlp_gain_grad, gate_grad, up_grad, down_grad,
    )


def solution(mesh):
    in_specs = (
        P("dp", "ctx", None),
        P("dp", None),
        P("dp"),
        P("dp", None),
        P("dp", None),
        P("dp", None),
        P("dp", None),
        P(),
        P(),
        P("dp"),
        P("dp", None),
        P("dp", None),
        P("dp", None),
        P("dp", "ctx", None),
    )
    out_specs = (
        P("dp", "ctx", None),
        P("dp", "ctx", None),
        P("dp"),
        P("dp", None),
        P("dp", None),
        P("dp", None),
        P("dp", None),
        P(),
        P(),
        P("dp"),
        P("dp", None),
        P("dp", None),
        P("dp", None),
    )
    return jax.shard_map(
        on_device, mesh=mesh, in_specs=in_specs, out_specs=out_specs, check_vma=False
    )
```

```python
import functools
import math

import jax
import jax.numpy as jnp
from jax import lax
from jax.experimental import pallas as pl
from jax.experimental.pallas import tpu as pltpu
from jax.sharding import PartitionSpec as P

HEADS = 16
KV_HEADS = 8
HEAD_DIM = 128
GROUPS = HEADS // KV_HEADS

EPSILON = 1e-06
ROPE_BASE = 1000000.0
MASKED = -1e30
SCALE = HEAD_DIM ** (-0.5)

F32 = jnp.float32
BF16 = jnp.bfloat16
MIB = 1 << 20
VMEM_MIB = 16
LARGE = 1 << 18


ORDER = []


def room(pack):
    return VMEM_MIB * max(1, pack // 1536)


def shape(dims, dtype):
    return jax.ShapeDtypeStruct(dims, dtype)


ANY = pl.BlockSpec(memory_space=pl.ANY)
IN_VMEM = pl.BlockSpec(memory_space=pltpu.VMEM)
IN_HBM = pl.BlockSpec(memory_space=pltpu.HBM)


def in_hbm(spec, array):
    return spec not in (IN_VMEM, ANY, IN_HBM) and math.prod(array.shape) * 2 >= LARGE


def call(
    name, body, args, in_specs, out_specs, out_shape, grid=(1,), scratch=(), prefetch=(), aliases=None,
    after=(), vmem=VMEM_MIB,
):
    waits = list(ORDER) + list(after)
    wait_specs = [IN_VMEM] * len(ORDER) + [ANY] * len(after)
    taken = len(prefetch) + len(args)
    token = taken + len(waits) + len(out_shape)
    args = [
        pltpu.with_memory_space_constraint(a, pltpu.HBM) if in_hbm(s, a) else a
        for a, s in zip(args, in_specs)
    ]
    out_shape = [
        pltpu.HBM(o.shape, o.dtype) if in_hbm(s, o) else o for o, s in zip(out_shape, out_specs)
    ]

    def without(*refs):
        refs[token][...] = jnp.zeros_like(refs[token])
        body(*refs[:taken], *refs[taken + len(waits) : token], *refs[token + 1 :])

    results = pl.pallas_call(
        without,
        grid_spec=pltpu.PrefetchScalarGridSpec(
            num_scalar_prefetch=len(prefetch),
            grid=grid,
            in_specs=list(in_specs) + wait_specs,
            out_specs=list(out_specs) + [IN_VMEM],
            scratch_shapes=list(scratch),
        ),
        out_shape=out_shape + [shape((8, HEAD_DIM), F32)],
        input_output_aliases={len(prefetch) + i: o for i, o in (aliases or {}).items()},
        compiler_params=pltpu.CompilerParams(vmem_limit_bytes=vmem * MIB),
        cost_estimate=pl.CostEstimate(flops=0, bytes_accessed=0, transcendentals=0),
        name=name,
    )(*prefetch, *args, *waits)
    ORDER[:] = [results[-1]]
    return results[:-1]


def whole(dims):
    return pl.BlockSpec(dims, lambda *_: (0,) * len(dims))


def mm(a, b):
    return lax.dot_general(a, b, (((1,), (0,)), ((), ())), preferred_element_type=F32)


def mm_nt(a, b):
    return lax.dot_general(a, b, (((1,), (1,)), ((), ())), preferred_element_type=F32)


def mm_tn(a, b):
    return lax.dot_general(a, b, (((0,), (0,)), ((), ())), preferred_element_type=F32)


def mean_last(v):
    return jnp.sum(v, axis=-1, keepdims=True) * (1.0 / v.shape[-1])


def factor_of(v):
    return lax.rsqrt(mean_last(v * v) + EPSILON)


def norm_back(v, gain, incoming):
    f = factor_of(v)
    weighted = incoming * gain
    inner = mean_last(weighted * v)
    return f * weighted - v * (f * f * f * inner), incoming * v * f


def stream_index(row_ids, stretch_rows, ctx_size):
    slab_index = row_ids // (2 * stretch_rows)
    within = row_ids % (2 * stretch_rows)
    mirrored = (2 * ctx_size - 1 - slab_index) * stretch_rows + within - stretch_rows
    return jnp.where(within < stretch_rows, slab_index * stretch_rows + within, mirrored)


def opening_of(stream, starts):
    started = starts[None, :] <= stream[:, None]
    return jnp.max(jnp.where(started, starts[None, :], 0), axis=1)


def rotary(positions):
    half_dim = HEAD_DIM // 2
    inverse = jnp.exp(
        jnp.arange(half_dim, dtype=F32) * (-2.0 * math.log(ROPE_BASE) / HEAD_DIM)
    )
    angles = positions.astype(F32)[:, None] * inverse[None, :]
    cos_half, sin_half = jnp.cos(angles), jnp.sin(angles)
    return (
        jnp.concatenate([cos_half, cos_half], axis=1),
        jnp.concatenate([-sin_half, sin_half], axis=1),
    )


def copies(name, sources, plan, out_shape, prefetch=(), after=(), in_specs=None, out_specs=None):
    count = len(sources)
    first = len(prefetch)

    def body(*refs):
        ins = refs[first : first + count]
        for source, target in plan(refs[:first], ins, refs[first + count :]):
            target[...] = source[...]

    return call(
        name, body, sources, in_specs or [IN_VMEM] * count, out_specs or [IN_VMEM] * len(out_shape), out_shape,
        prefetch=prefetch, after=after, vmem=24,
    )


def touch(after):
    call("touch", lambda *_: None, [], [], [], [], after=after, vmem=4)


def norm_own(tokens, gain):
    def body(t_ref, g_ref, out_ref):
        x = t_ref[...].astype(F32)
        out_ref[...] = (x * factor_of(x) * g_ref[...]).astype(BF16)

    return call(
        "norm_own", body, [tokens, gain], [IN_VMEM] * 2, [IN_VMEM], [shape(tokens.shape, BF16)]
    )[0]


def norm_pack(own, from_left, from_right, gain, places, ctx_at):
    count = len(from_left) + 1
    rows, width = own.shape
    half = rows // 2

    def body(places_ref, at_ref, gain_ref, *refs):
        blocks, pack_ref = refs[:-1], refs[-1]
        step = pl.program_id(0)
        me = at_ref[0]

        def write(ref):
            x = ref[...].astype(F32)
            low = (x * factor_of(x) * gain_ref[...]).astype(BF16)
            pack_ref[...] = low.reshape(2, 1, half, width)

        @pl.when(step == 0)
        def _():
            write(blocks[0])

        for s in range(1, count):

            @pl.when((step == s) & (me >= s))
            def _():
                write(blocks[s])

            @pl.when((step == s) & (me < s))
            def _():
                write(blocks[count - 1 + count - s])

    blocks = [own] + from_left + from_right
    return call(
        "norm_pack", body, [gain] + blocks,
        [whole((1, width))] + [IN_VMEM] * len(blocks),
        [pl.BlockSpec((2, 1, half, width), lambda k, at, me: (0, at[k], 0, 0))],
        [shape((2, count, half, width), BF16)],
        grid=(count,), prefetch=[places, ctx_at],
    )[0]


def lane_sums(v):
    cols = v.shape[-1]
    head = lax.broadcasted_iota(jnp.int32, (cols, cols), 0) // HEAD_DIM
    same = (head == lax.broadcasted_iota(jnp.int32, (cols, cols), 1) // HEAD_DIM).astype(BF16)
    high = v.astype(BF16)
    low = (v - high.astype(F32)).astype(BF16)
    return mm(high, same) + mm(low, same)


def head_factors(raw):
    return lax.rsqrt(lane_sums(raw * raw) * (1.0 / HEAD_DIM) + EPSILON)


def turn(v):
    parts = [
        pltpu.roll(v[:, at : at + HEAD_DIM], HEAD_DIM // 2, 1) for at in range(0, v.shape[1], HEAD_DIM)
    ]
    return parts[0] if len(parts) == 1 else jnp.concatenate(parts, axis=1)


def rotated(v, cos, sin):
    return v * cos + turn(v) * sin


def rope(raw, gain, cos, sin):
    return rotated(raw * head_factors(raw) * gain, cos, sin)


def twice(ref):
    return jnp.concatenate([ref[...]] * 2, axis=1)


def project_queries(x, weights, gain, cos, sin):
    rows, width = x.shape
    cols = HEADS * HEAD_DIM
    block = 2 * HEAD_DIM
    each = 2 * block
    col = pl.BlockSpec((rows, each), lambda j: (0, j))

    def body(x_ref, w_ref, g_ref, c_ref, s_ref, raw_ref, rot_ref, fac_ref):
        g, c, s = twice(g_ref), twice(c_ref), twice(s_ref)
        for j in range(each // block):
            at = slice(j * block, (j + 1) * block)
            raw = mm(x_ref[...], w_ref[:, at])
            raw_ref[:, at] = raw.astype(BF16)
            factors = head_factors(raw)
            rot_ref[:, at] = rotated(raw * factors * g, c, s).astype(BF16)
            for h in range(2):
                fac_ref[2 * j + h] = factors[:, h * HEAD_DIM : (h + 1) * HEAD_DIM].T[:8]

    return call(
        "project_queries", body, [x, weights, gain, cos, sin],
        [IN_VMEM, pl.BlockSpec((width, each), lambda j: (0, j))] + [IN_VMEM] * 3,
        [col, col, pl.BlockSpec((each // HEAD_DIM, 8, rows), lambda j: (j, 0, 0))],
        [shape((rows, cols), BF16), shape((rows, cols), BF16), shape((HEADS, 8, rows), F32)],
        grid=(cols // each,),
    )


def project_keys_values(x, weights, gain, cos, sin):
    rows, width = x.shape
    block = 2 * HEAD_DIM
    cols = KV_HEADS * HEAD_DIM
    inner = HEADS * HEAD_DIM
    part = 256

    def body(x_ref, wk_ref, wv_ref, g_ref, c_ref, s_ref, raw_ref, rot_ref, val_ref):
        wk, wv = wk_ref[...], wv_ref[...]
        g = twice(g_ref)
        for i in range(rows // part):
            here = slice(i * part, (i + 1) * part)
            raw = mm(x_ref[here, :], wk)
            raw_ref[here, :] = raw.astype(BF16)
            val_ref[here, :] = mm(x_ref[here, :], wv).astype(BF16)
            c, s = [jnp.concatenate([r[here, :]] * 2, axis=1) for r in (c_ref, s_ref)]
            rot_ref[here, :] = rope(raw, g, c, s).astype(BF16)

    col = pl.BlockSpec((rows, block), lambda j: (0, j))
    return call(
        "project_keys_values", body, [x, weights, weights, gain, cos, sin],
        [
            IN_VMEM,
            pl.BlockSpec((width, block), lambda j: (0, inner // block + j)),
            pl.BlockSpec((width, block), lambda j: (0, (inner + cols) // block + j)),
        ]
        + [IN_VMEM] * 3,
        [col, col, col], [shape((rows, cols), BF16)] * 3, grid=(cols // block,), vmem=room(rows),
    )


LOG2E = 1.4426950408889634


def attend(queries, keys, values, q_low, q_high, k_stream):
    rows = queries.shape[0]
    half = rows // 2
    pack = keys.shape[0]
    pair = GROUPS * HEAD_DIM

    def body(q_ref, k_ref, v_ref, lo_ref, hi_ref, ks_ref, mix_ref, lse_ref, bias):
        @pl.when(pl.program_id(0) == 0)
        def _():
            ks = ks_ref[...]
            ok = (ks >= lo_ref[...]) & (ks <= hi_ref[...])
            bias[...] = jnp.where(ok, 0.0, MASKED)

        v_ones = jnp.concatenate([v_ref[...], jnp.ones((pack, HEAD_DIM), BF16)], axis=1)
        for part in range(2):
            here = slice(part * half, (part + 1) * half)
            seen = pack // 2 if part == 0 else pack
            for j in range(GROUPS):
                cols = slice(j * HEAD_DIM, (j + 1) * HEAD_DIM)
                scores = mm_nt(q_ref[here, cols], k_ref[:seen, :]) * (SCALE * LOG2E) + bias[here, :seen]
                both = mm(jnp.exp2(scores).astype(BF16), v_ones[:seen])
                total = both[:, HEAD_DIM:]
                mix_ref[here, cols] = (both[:, :HEAD_DIM] * (1.0 / total)).astype(BF16)
                lse_ref[j, :, here] = jnp.log2(total).T[:8]

    col = pl.BlockSpec((rows, pair), lambda g: (0, g))
    key = pl.BlockSpec((pack, HEAD_DIM), lambda g: (0, g))
    return call(
        "attend", body, [queries, keys, values, q_low, q_high, k_stream],
        [col, key, key, whole((rows, 1)), whole((rows, 1)), whole((1, pack))],
        [col, pl.BlockSpec((GROUPS, 8, rows), lambda g: (g, 0, 0))],
        [shape((rows, HEADS * HEAD_DIM), BF16), shape((HEADS, 8, rows), F32)],
        grid=(KV_HEADS,), vmem=room(pack),
        scratch=[pltpu.VMEM((rows, pack), F32)],
    )


def high_low(v):
    high = v.astype(BF16)
    return high, (v - high.astype(F32)).astype(BF16)


def middle_block(mixed, lse, factors, tokens, grad, gain, stack):
    rows, inner = mixed.shape
    count, height, width = stack.shape
    unit = width // count
    hidden = 3 * width
    block = 256
    per_row = block // unit if unit < block else 1

    def body(
        mixed_hbm, lse_ref, fac_ref, tok_hbm, dy_hbm, gain_ref, stack_ref,
        out_ref, low_ref, h_ref, both_ref, gm_ref, gb_ref, gg_ref, dm_ref, parcel_ref,
        w, mid, acc, deltas, mixed_ref, tok_ref, dy_ref, sems,
    ):
        def move(first, many, sem):
            here = (slice(None), pl.ds(first * unit, many * unit))
            return pltpu.make_async_copy(stack_ref.at[here], w.at[here], sems.at[sem])

        loads = [
            pltpu.make_async_copy(a, b, sems.at[8 + i])
            for i, (a, b) in enumerate(((mixed_hbm, mixed_ref), (tok_hbm, tok_ref), (dy_hbm, dy_ref)))
        ]
        loads[0].start()
        out_copy = move(9, 2, 0)
        gate_copies = [move(3 + i, 1, 1 + i) for i in range(3)]
        up_copies = [move(6 + i, 1, 4 + i) for i in range(3)]
        down_copy = move(0, 3, 7)
        for copy in (out_copy, loads[1], loads[2]):
            copy.start()
        for copy in [out_copy] + loads:
            copy.wait()
        for a, b in zip(gate_copies, up_copies):
            a.start()
            b.start()
        down_copy.start()

        for j in range(width // block):
            cols = slice(j * block, (j + 1) * block)
            part = w[:, 9 * unit : 11 * unit, cols].reshape(inner, block)
            mid[:, cols] = tok_ref[:, cols].astype(F32) + mm(mixed_ref[...], part)
        x = mid[...]
        low_ref[...] = (x * factor_of(x) * gain_ref[...]).astype(BF16)

        for i in range(3):
            gate_copies[i].wait()
            up_copies[i].wait()

            def forward(j, _):
                cols = pl.ds(pl.multiple_of(j * block, block), block)
                to = pl.ds(pl.multiple_of(i * width + j * block, block), block)
                g = mm(low_ref[...], w[:, (3 + i) * unit : (4 + i) * unit, cols].reshape(width, block))
                u = mm(low_ref[...], w[:, (6 + i) * unit : (7 + i) * unit, cols].reshape(width, block))
                s = 1.0 / (1.0 + jnp.exp(-g))
                act = g * s
                h_ref[:, to] = (act * u).astype(BF16)
                both_ref[0, :, to] = (u * (s + act * (1.0 - s))).astype(BF16)
                both_ref[1, :, to] = act.astype(BF16)
                return 0

            lax.fori_loop(0, width // block, forward, 0, unroll=True)

        down_copy.wait()
        acc[...] = mid[...]
        wide = 384
        owners = wide // (3 * unit)

        def down(j, _):
            cols = pl.ds(pl.multiple_of(j * wide, wide), wide)
            part = w[pl.ds(j * owners, owners), 0 : 3 * unit, :].reshape(wide, width)
            dh = mm_nt(dy_ref[...], part)
            both_ref[0, :, cols] = (both_ref[0, :, cols].astype(F32) * dh).astype(BF16)
            both_ref[1, :, cols] = (both_ref[1, :, cols].astype(F32) * dh).astype(BF16)
            acc[...] += mm(h_ref[:, cols], part)
            return 0

        lax.fori_loop(0, hidden // wide, down, 0, unroll=True)
        out_ref[...] = acc[...].astype(BF16)

        owners_in = block // unit
        for b in range(width // block):
            at = slice(b * owners_in, (b + 1) * owners_in)
            total = None
            for i in range(3):
                cols = slice(i * width, (i + 1) * width)
                for side in range(2):
                    first = (3 + 3 * side + i) * unit
                    part = w[at, first : first + unit, :].reshape(block, width)
                    term = mm_nt(both_ref[side, :, cols], part)
                    total = term if total is None else total + term
            acc[:, b * block : (b + 1) * block] = total

        back, terms = norm_back(mid[...], gain_ref[...], acc[...])
        grad_mid = dy_ref[...].astype(F32) + back
        gm_ref[...] = grad_mid
        gb_ref[...] = grad_mid.astype(BF16)
        gg_ref[...] = jnp.sum(terms, axis=0, keepdims=True)

        owners_out = block // (2 * unit)

        def mixed_back(j, _):
            cols = pl.ds(pl.multiple_of(j * block, block), block)
            part = w[pl.ds(j * owners_out, owners_out), 9 * unit : 11 * unit, :].reshape(block, width)
            dm = mm_nt(gb_ref[...], part).astype(BF16)
            dm_ref[:, cols] = dm
            terms = (dm.astype(F32) * mixed_ref[:, cols].astype(F32)).T
            for k in range(block // HEAD_DIM):
                delta = jnp.sum(terms[k * HEAD_DIM : (k + 1) * HEAD_DIM], axis=0, keepdims=True)
                deltas[pl.ds(j * (block // HEAD_DIM) + k, 1), :] = delta
            return 0

        lax.fori_loop(0, inner // block, mixed_back, 0, unroll=True)
        parcel_ref[:rows, :] = gb_ref[...]
        parcel_ref[rows:, :] = jnp.zeros((3 * HEADS, width), BF16)
        extras = (lse_ref[:, 0, :], deltas[...], fac_ref[:, 0, :])
        for which, values in enumerate(extras):
            at = rows + which * HEADS
            for side, piece in enumerate(high_low(values)):
                parcel_ref[at : at + HEADS, side * rows : (side + 1) * rows] = piece

    full = (rows, width)
    return call(
        "middle_block", body, [mixed, lse, factors, tokens, grad, gain, stack],
        [IN_HBM, whole(lse.shape), whole(factors.shape), IN_HBM, IN_HBM, whole((1, width)), IN_HBM],
        [whole(full), IN_VMEM, IN_VMEM, IN_VMEM, whole(full), IN_VMEM, IN_VMEM, whole((rows, inner)), IN_VMEM],
        [
            shape(full, BF16), shape(full, BF16), shape((rows, hidden), BF16),
            shape((2, rows, hidden), BF16), shape(full, F32), shape(full, BF16),
            shape((1, width), F32), shape((rows, inner), BF16), shape((rows + 3 * HEADS, width), BF16),
        ],
        scratch=[
            pltpu.VMEM((count, height, width), BF16),
            pltpu.VMEM(full, F32),
            pltpu.VMEM(full, F32),
            pltpu.VMEM((HEADS, rows), F32),
            pltpu.VMEM((rows, inner), BF16),
            pltpu.VMEM(full, BF16),
            pltpu.VMEM(full, BF16),
            pltpu.SemaphoreType.DMA((11,)),
        ],
        vmem=44,
    )


def head_norm_back(v, gain, incoming):
    f = head_factors(v)
    weighted = incoming * gain
    inner = lane_sums(weighted * v) * (1.0 / HEAD_DIM)
    return f * (weighted - v * (f * f * inner)), incoming * v * f


def query_back(
    queries, grad_mixed, mixed, keys, values, lse, q_low, q_high, k_stream, query_raw, gain, cos, sin,
    first, count, earlier=(),
):
    rows = queries.shape[0]
    half = rows // 2
    pack = keys.shape[0]
    pair = GROUPS * HEAD_DIM

    def body(
        q_ref, do_ref, mix_ref, k_ref, v_ref, lse_ref, lo_ref, hi_ref, ks_ref, raw_ref, g_ref, c_ref, s_ref,
        *rest,
    ):
        dq_ref, gg_ref, bias = rest[len(earlier) :]

        @pl.when(pl.program_id(0) == 0)
        def _():
            ks = ks_ref[...]
            ok = (ks >= lo_ref[...]) & (ks <= hi_ref[...])
            bias[...] = jnp.where(ok, 0.0, MASKED)
            gg_ref[...] = jnp.zeros_like(gg_ref)

        deltas = lane_sums(do_ref[...].astype(F32) * mix_ref[...].astype(F32))
        for j in range(GROUPS):
            cols = slice(j * HEAD_DIM, (j + 1) * HEAD_DIM)
            lse_col = jnp.broadcast_to(lse_ref[j, 0:1, :], (HEAD_DIM, rows)).T[:, :1]
            grads = []
            for part in range(2):
                here = slice(part * half, (part + 1) * half)
                seen = pack // 2 if part == 0 else pack
                scores = mm_nt(q_ref[here, cols], k_ref[:seen, :]) * (SCALE * LOG2E) + bias[here, :seen]
                probs = jnp.exp2(scores - lse_col[here])
                d_probs = mm_nt(do_ref[here, cols], v_ref[:seen, :])
                d_scores = (probs * (d_probs - deltas[here, cols][:, :1])).astype(BF16)
                grads.append(mm(d_scores, k_ref[:seen, :]))
            dq = jnp.concatenate(grads, axis=0) * SCALE
            dq = dq * c_ref[...] - turn(dq) * s_ref[...]
            dq, terms = head_norm_back(raw_ref[:, cols].astype(F32), g_ref[...], dq)
            dq_ref[:, cols] = dq.astype(BF16)
            gg_ref[...] += jnp.sum(terms, axis=0, keepdims=True)

    col = pl.BlockSpec((rows, pair), lambda g: (0, first + g))
    key = pl.BlockSpec((pack, HEAD_DIM), lambda g: (0, first + g))
    return call(
        "query_back", body,
        [queries, grad_mixed, mixed, keys, values, lse, q_low, q_high, k_stream, query_raw, gain, cos, sin, *earlier],
        [
            col, col, col, key, key,
            pl.BlockSpec((GROUPS, 8, rows), lambda g: (first + g, 0, 0)),
            whole((rows, 1)), whole((rows, 1)), whole((1, pack)),
            col, whole((1, HEAD_DIM)), whole((rows, HEAD_DIM)), whole((rows, HEAD_DIM)),
        ]
        + [ANY] * len(earlier),
        [col, whole((1, HEAD_DIM))],
        [shape((rows, HEADS * HEAD_DIM), BF16), shape((1, HEAD_DIM), F32)],
        grid=(count,), vmem=room(pack),
        scratch=[pltpu.VMEM((rows, pack), F32)],
        aliases={13: 0} if earlier else None,
    )


def key_back(
    queries, grad_mixed, keys, values, far, q_low, q_high, k_stream, key_raw, gain, cos, sin,
    ctx_at, ctx_size, first, count, earlier=(),
):
    pack = queries.shape[0]
    rows = pack // ctx_size
    half = rows // 2
    pair = GROUPS * HEAD_DIM

    def body(
        at_ref, q_ref, do_ref, k_ref, v_ref, far_ref, lo_ref, hi_ref, ks_ref, raw_ref, g_ref,
        c_ref, s_ref, *rest,
    ):
        out_ref, gg_ref, bias, acc = rest[len(earlier) :]

        @pl.when(pl.program_id(0) == 0)
        def _():
            ks = ks_ref[...]
            ok = (ks >= lo_ref[...]) & (ks <= hi_ref[...])
            bias[...] = jnp.where(ok, 0.0, MASKED)
            gg_ref[...] = jnp.zeros_like(gg_ref)

        k_own = k_ref[...].reshape(rows, HEAD_DIM)
        v_own = v_ref[...].reshape(rows, HEAD_DIM)
        for j in range(GROUPS):
            cols = slice(j * HEAD_DIM, (j + 1) * HEAD_DIM)
            head = GROUPS * (first + pl.program_id(0)) + j
            lse, delta, factors = [far_ref[pl.ds(i * HEADS + head, 1), :] for i in range(3)]
            for late in range(2):
                there = slice(late * pack // 2, (late + 1) * pack // 2)
                here = slice(0, rows if late else half)
                qq, dd = q_ref[there, cols], do_ref[there, cols]
                factor = factors[:, there]
                scores = mm_nt(k_own[here], qq) * (factor * (SCALE * LOG2E)) + bias[here, there]
                probs = jnp.exp2(scores - lse[:, there])
                d_probs = mm_nt(v_own[here], dd)
                d_scores = (probs * factor * (d_probs - delta[:, there])).astype(BF16)
                dv = mm(probs.astype(BF16), dd)
                dk = mm(d_scores, qq)
                if j == 0 and late == 0:
                    acc[...] = jnp.zeros_like(acc)
                acc[0, here, :] += dk
                acc[1, here, :] += dv
        out_ref[1] = acc[1].astype(BF16)
        dk = acc[0] * SCALE
        dk = dk * c_ref[...] - turn(dk) * s_ref[...]
        dk, terms = head_norm_back(raw_ref[...].astype(F32).reshape(rows, HEAD_DIM), g_ref[...], dk)
        out_ref[0] = dk.astype(BF16)
        gg_ref[...] += jnp.sum(terms, axis=0, keepdims=True)

    col = pl.BlockSpec((pack, pair), lambda g, at: (0, first + g))
    key = pl.BlockSpec((2, 1, half, HEAD_DIM), lambda g, at: (0, at[0], 0, first + g))
    laid = (2, ctx_size, half, KV_HEADS * HEAD_DIM)
    return call(
        "key_back", body,
        [
            queries, grad_mixed, keys.reshape(laid), values.reshape(laid), far, q_low, q_high, k_stream, key_raw.reshape(laid), gain, cos, sin, *earlier,
        ],
        [
            col, col, key, key, whole(far.shape), whole((1, pack)), whole((1, pack)), whole((rows, 1)),
            key, whole((1, HEAD_DIM)), whole((rows, HEAD_DIM)), whole((rows, HEAD_DIM)),
        ]
        + [ANY] * len(earlier),
        [pl.BlockSpec((2, rows, HEAD_DIM), lambda g, at: (0, 0, first + g)), whole((1, HEAD_DIM))],
        [shape((2, rows, KV_HEADS * HEAD_DIM), BF16), shape((1, HEAD_DIM), F32)],
        grid=(count,), vmem=room(pack),
        scratch=[pltpu.VMEM((rows, pack), F32), pltpu.VMEM((2, rows, HEAD_DIM), F32)],
        prefetch=[ctx_at], aliases={12: 0} if earlier else None,
    )


def all_queries(x, weights, gain, cos, sin):
    rows, width = x.shape
    cols = HEADS * HEAD_DIM
    block = 2 * HEAD_DIM
    part = 256

    def body(x_ref, w_ref, g_ref, c_ref, s_ref, rot_ref):
        g = twice(g_ref)
        for i in range(rows // part):
            here = slice(i * part, (i + 1) * part)
            raw = mm(x_ref[here, :], w_ref[...])
            c, s = [jnp.concatenate([r[here, :]] * 2, axis=1) for r in (c_ref, s_ref)]
            rot_ref[here, :] = rotated(raw * g, c, s).astype(BF16)

    return call(
        "all_queries", body, [x, weights, gain, cos, sin],
        [IN_VMEM, pl.BlockSpec((width, block), lambda j: (0, j)), IN_VMEM, IN_VMEM, IN_VMEM],
        [pl.BlockSpec((rows, block), lambda j: (0, j))], [shape((rows, cols), BF16)],
        grid=(cols // block,), vmem=room(rows),
    )[0]


def all_grad_mixed(own, parcels, stack, places, ctx_at, rows):
    count = (len(parcels) + 1) // 2
    numbers = parcels[0].shape[0] - rows
    half = rows // 2
    inner = own.shape[1]
    _, _, width = stack.shape
    owners = stack.shape[0]
    unit = width // owners

    def body(places_ref, at_ref, own_ref, a_ref, b_ref, *refs):
        blocks, (out_ref, far_ref, turned) = refs[:-3], refs[-3:]
        step = pl.program_id(0)
        me = at_ref[0]

        def spread(ref):
            both = ref[rows:, :rows].astype(F32) + ref[rows:, rows : 2 * rows].astype(F32)
            far_ref[0, 0] = both[:, :half]
            far_ref[1, 0] = both[:, half:]

        @pl.when(step == 0)
        def _():
            spread(blocks[0])
            out_ref[...] = own_ref[...].reshape(2, 1, half, inner)
            turned[...] = jnp.concatenate([a_ref[...], b_ref[...]], axis=1).reshape(inner, width)

        def write(ref):
            spread(ref)
            for j in range(inner // 512):
                at = slice(j * 512, (j + 1) * 512)
                part = mm_nt(ref[:rows, :], turned[at, :]).astype(BF16)
                out_ref[:, :, :, at] = part.reshape(2, 1, half, 512)

        for s in range(1, count):

            @pl.when((step == s) & (me >= s))
            def _():
                write(blocks[s])

            @pl.when((step == s) & (me < s))
            def _():
                write(blocks[count - 1 + count - s])

    return call(
        "all_grad_mixed", body, [own, stack, stack, *parcels],
        [
            IN_VMEM,
            pl.BlockSpec((owners, unit, width), lambda *_: (0, 9, 0)),
            pl.BlockSpec((owners, unit, width), lambda *_: (0, 10, 0)),
        ]
        + [whole(parcel.shape) for parcel in parcels],
        [
            pl.BlockSpec((2, 1, half, inner), lambda k, at, me: (0, at[k], 0, 0)),
            pl.BlockSpec((2, 1, numbers, half), lambda k, at, me: (0, at[k], 0, 0)),
        ],
        [shape((2, count, half, inner), BF16), shape((2, count, numbers, half), F32)],
        grid=(count,), scratch=[pltpu.VMEM((inner, width), BF16)], prefetch=[places, ctx_at], vmem=32,
    )


def normed_back(d_queries, d_pair, weights):
    rows, inner = d_queries.shape
    cols = d_pair.shape[2]
    width = weights.shape[0]

    def body(dq_ref, pair_ref, wq_ref, wk_ref, wv_ref, out_ref):
        part = mm_nt(dq_ref[...], wq_ref[...])
        part += mm_nt(pair_ref[0], wk_ref[...])
        part += mm_nt(pair_ref[1], wv_ref[...])
        out_ref[...] = part

    block = 256
    return call(
        "normed_back", body, [d_queries, d_pair, weights, weights, weights],
        [
            IN_VMEM,
            IN_VMEM,
            pl.BlockSpec((block, inner), lambda j: (j, 0)),
            pl.BlockSpec((block, cols), lambda j: (j, inner // cols)),
            pl.BlockSpec((block, cols), lambda j: (j, inner // cols + 1)),
        ],
        [pl.BlockSpec((rows, block), lambda j: (0, j))],
        [shape((rows, width), F32)],
        grid=(width // block,),
    )[0]


def input_back(d_normed, tokens, gain, grad_middle):
    rows, width = tokens.shape

    def body(a_ref, t_ref, gain_ref, gm_ref, out_ref, gg_ref):
        back, terms = norm_back(t_ref[...].astype(F32), gain_ref[...], a_ref[...])
        out_ref[...] = (gm_ref[...] + back).astype(BF16)
        gg_ref[...] = jnp.sum(terms, axis=0, keepdims=True)

    return call(
        "input_back", body, [d_normed, tokens, gain, grad_middle],
        [IN_VMEM] * 4,
        [whole((rows, width)), IN_VMEM],
        [shape((rows, width), BF16), shape((1, width), F32)],
    )


def weight_grad(left, right, owners=None, cols=None, block=512, apart=False, beside=False):
    tokens, rows = left.shape
    count = 1 if owners is None else owners.shape[0]
    unit = rows // count
    deep = right.ndim == 3
    first, each = cols or (0, right.shape[-1])
    width = each * (right.shape[0] if deep else 1)
    steps = width // block
    split = owners is not None
    results = 2 * (right.shape[0] if apart else 1) if split else 1

    def body(*refs):
        if split:
            own_ref, refs = refs[0], refs[1:]
        l_ref, r_ref, refs = refs[0], refs[1], refs[2:]
        outs, scratch = refs[:results], refs[results:]

        @pl.when(pl.program_id(0) == 0)
        def _():
            scratch[0][...] = l_ref[...].T
            for k in range(count if split else 0):
                at = pl.multiple_of(own_ref[k] * unit, unit)
                scratch[1][k * unit : (k + 1) * unit, :] = scratch[0][pl.ds(at, unit), :]

        def block_at(j):
            if deep:
                per = each // block
                return r_ref[j // per, :, pl.ds(pl.multiple_of(first + (j % per) * block, block), block)]
            return r_ref[:, pl.ds(pl.multiple_of(first + j * block, block), block)]

        if not split:
            outs[0][...] = mm(scratch[0][...], block_at(pl.program_id(0))).astype(BF16)
            return
        per = each // block
        for j in range(steps):
            at = 2 * (j // per) if apart else 0
            to = slice((j % per) * block, (j % per + 1) * block) if apart else slice(j * block, (j + 1) * block)
            for side in range(2):
                here = slice(side * rows // 2, (side + 1) * rows // 2)
                part = mm(scratch[1][here, :], block_at(j)).astype(BF16)
                part = part.reshape(count // 2, unit, block)
                if beside:
                    outs[side][:, :, to] = part[:, : unit // 2]
                    outs[side][:, :, width + j * block : width + (j + 1) * block] = part[:, unit // 2 :]
                else:
                    outs[at + side][:, :, to] = part

    if split:
        out = [IN_VMEM] * results
        dims = (count // 2, unit // 2, 2 * width) if beside else (count // 2, unit, each if apart else width)
        out_shape = [shape(dims, BF16)] * results
    else:
        out = [pl.BlockSpec((rows, block), lambda j: (0, j))]
        out_shape = [shape((rows, width), BF16)]
    return call(
        "weight_grad", body, [left, right], [IN_VMEM] * 2, out, out_shape,
        grid=(1 if split else steps,),
        scratch=[pltpu.VMEM((rows, tokens), BF16)] * (1 + split),
        prefetch=[owners] if split else (),
    )


def fold(items, steps=1):
    arrays = []

    def slot(term):
        for i, known in enumerate(arrays):
            if known is term:
                return i
        arrays.append(term)
        return len(arrays) - 1

    laid = [([slot(t) for t in terms], rows, bit) for terms, rows, bit in items]
    in_specs = []
    for a in arrays:
        in_specs.append(
            IN_VMEM if steps == 1 else pl.BlockSpec(a.shape[:2] + (a.shape[2] // steps,), lambda j: (0, 0, j))
        )
    out_specs, out_shape = [], []
    for slots, (_, rows), bit in laid:
        many, _, cols = arrays[slots[0]].shape
        dims = (many, rows, cols) if bit is None else (many // 2, rows, cols)
        for _ in range(1 if bit is None else 2):
            out_specs.append(
                IN_VMEM if steps == 1 else pl.BlockSpec(dims[:2] + (cols // steps,), lambda j: (0, 0, j))
            )
            out_shape.append(shape(dims, BF16))

    def body(*refs):
        ins, outs = refs[: len(arrays)], list(refs[len(arrays) :])
        for slots, (first, rows), bit in laid:
            here = slice(first, first + rows)
            many = arrays[slots[0]].shape[0]

            def total(k):
                value = ins[slots[0]][k, here, :].astype(F32)
                for at in slots[1:]:
                    value = value + ins[at][k, here, :].astype(F32)
                return value.astype(BF16)

            if bit is None:
                out = outs.pop(0)
                for k in range(many):
                    out[k] = total(k)
                continue
            sent, kept = outs.pop(0), outs.pop(0)
            places = [0, 0]
            for k in range(many):
                with_bit = (k >> bit) & 1
                (sent if with_bit else kept)[places[with_bit]] = total(k)
                places[with_bit] += 1

    return call("fold", body, arrays, in_specs, out_specs, out_shape, grid=(steps,))


def choose(first, second, dims, odd):
    arrays = [a for a, _ in first + second]
    views = [v for _, v in first + second]

    def body(odd_ref, *refs):
        ins, (sent, kept) = refs[: len(arrays)], refs[len(arrays) :]

        def total(begin, end):
            value = ins[begin][views[begin]].astype(F32)
            for at in range(begin + 1, end):
                value = value + ins[at][views[at]].astype(F32)
            return value.astype(BF16)

        @pl.when(odd_ref[0] == 1)
        def _():
            sent[...] = total(0, len(first))
            kept[...] = total(len(first), len(arrays))

        @pl.when(odd_ref[0] == 0)
        def _():
            kept[...] = total(0, len(first))
            sent[...] = total(len(first), len(arrays))

    return call(
        "choose", body, arrays, [IN_VMEM] * len(arrays), [IN_VMEM] * 2, [shape(dims, BF16)] * 2,
        prefetch=[odd],
    )


def place(sums, odd, out_dims, cuts):
    arrays = [a for pair in sums for a in pair]

    def body(odd_ref, *refs):
        ins, outs = refs[: len(arrays)], refs[len(arrays) :]

        def write(swapped):
            for which, half, source, at, target in cuts:
                outs[at][target] = ins[2 * which + (half ^ swapped)][source].astype(F32)

        @pl.when(odd_ref[0] == 1)
        def _():
            write(1)

        @pl.when(odd_ref[0] == 0)
        def _():
            write(0)

    return call(
        "place", body, arrays, [IN_VMEM] * len(arrays), [whole(d) for d in out_dims],
        [shape(d, F32) for d in out_dims], prefetch=[odd],
    )


def swap(x, axis, bit):
    size = lax.axis_size(axis)
    return lax.ppermute(x, axis, [(i, i ^ bit) for i in range(size)])


def bits_of(size):
    return [1 << b for b in range(size.bit_length() - 1)]


def gather_pieces(own, cut):
    rest = bits_of(lax.axis_size("dp"))[1:]
    spans = [slice(0, cut), slice(cut, own.shape[1])]
    everything = slice(0, own.shape[1])
    held = {0: [(everything, own)]}
    for bit in rest:
        held[bit] = [(everything, swap(own, "dp", bit))]
    first = [held[bit][0][1] for bit in rest]
    for at in range(1 << len(rest)):
        at = 2 * at
        if at in held:
            continue
        held[at] = []
        for span, order in zip(spans, (rest, rest[::-1])):
            last = [bit for bit in order if at & bit][-1]
            before = held[at ^ last]
            source = before[0][1][:, span] if len(before) == 1 else before[spans.index(span)][1]
            held[at].append((span, swap(source, "dp", last)))
    for at in sorted(held):
        held[at | 1] = [(span, swap(piece, "dp", 1)) for span, piece in held[at]]
    return held, first


class Sum:
    def __init__(self, kept, sent, halves, odd):
        self.rest = bits_of(lax.axis_size("dp"))[1:]
        self.order = [list(range(len(self.rest))), list(range(len(self.rest)))[::-1]]
        self.left = [list(range(len(self.rest))), list(range(len(self.rest)))]
        self.odd = odd
        arrived = [swap(s, "dp", 1) for s in sent]
        if len(kept) == 1:
            kept, arrived = kept * 2, arrived * 2
        self.terms = [[k, a] for k, a in zip(kept, arrived)]
        self.rows = halves
        self.stage = 0

    def over_dp(self, steps=1):
        bits = [order[self.stage] for order in self.order]
        items = [
            (terms, rows, left.index(bit))
            for terms, rows, left, bit in zip(self.terms, self.rows, self.left, bits)
        ]
        sent0, kept0, sent1, kept1 = fold(items, steps)
        self.terms = [
            [kept, swap(sent, "dp", self.rest[bit])]
            for kept, sent, bit in zip((kept0, kept1), (sent0, sent1), bits)
        ]
        self.rows = [(0, k.shape[1]) for k in (kept0, kept1)]
        for left, bit in zip(self.left, bits):
            left.remove(bit)
        self.stage += 1

    def joined(self):
        dims = [terms[0].shape[1:] for terms in self.terms]
        arrays = [term for terms in self.terms for term in terms]
        many = len(self.terms[0])

        def body(*refs):
            at = 0
            for part, (rows, _) in enumerate(dims):
                value = refs[part * many][0].astype(F32)
                for k in range(1, many):
                    value = value + refs[part * many + k][0].astype(F32)
                refs[-1][at : at + rows, :] = value.astype(BF16)
                at += rows

        total = (sum(rows for rows, _ in dims), dims[0][1])
        return call(
            "joined", body, arrays, [IN_VMEM] * len(arrays), [IN_VMEM], [shape(total, BF16)]
        )[0]

    def to_ctx(self):
        first, second = [[(t, 0) for t in terms] for terms in self.terms]
        self.begin_ctx(first, second, first[0][0].shape[1:])

    def begin_ctx(self, first, second, dims):
        sent, kept = choose(first, second, dims, self.odd)
        self.total, self.next = [kept, swap(sent, "ctx", 1)], bits_of(lax.axis_size("ctx"))[1:]

    def over_ctx(self):
        a, b = [t[None] for t in self.total]
        total = fold([([a, b], (0, a.shape[1]), None)])[0][0]
        if self.next:
            self.total = [total, swap(total, "ctx", self.next.pop(0))]
        else:
            self.total = [total, swap(total, "ctx", 1)]


class Line:
    def __init__(self, total):
        size = lax.axis_size("ctx")
        middle = size // 2
        self.hops = [("add", [(k, k + 1), (size - 1 - k, size - 2 - k)]) for k in range(middle - 1)]
        self.hops.append(("add", [(middle - 1, middle), (middle, middle - 1)]))
        for k in reversed(range(middle - 1)):
            self.hops.append(("take", [(k + 1, k), (size - 2 - k, size - 1 - k)]))
        self.total = total
        self.send()

    def send(self):
        self.kind, pairs = self.hops.pop(0)
        self.takers = [b for _, b in pairs]
        self.came = lax.ppermute(self.total, "ctx", pairs)

    def taking(self):
        at = lax.axis_index("ctx")
        return sum((at == taker).astype(jnp.int32) for taker in self.takers)[None]

    def step(self):
        if self.kind == "add":
            rows = self.total.shape[0]
            self.total = fold([([self.total[None], self.came[None]], (0, rows), None)])[0][0]
        else:
            self.total = jnp.where(self.taking()[0] == 1, self.came, self.total)
        self.send()

    def finish(self):
        while self.hops:
            self.step()

    def place(self, out_dims, cuts):
        cuts = [(0, 0, source, at, target) for source, at, target in cuts]
        if self.kind == "add":
            self.total, self.came = fold([([self.total[None], self.came[None]], (0, self.total.shape[0]), None)])[0][0], self.total
            return place([(self.total, self.came)], jnp.zeros((1,), jnp.int32), out_dims, cuts)
        return place([(self.total, self.came)], self.taking(), out_dims, cuts)


class Relay:
    def __init__(self, block):
        self.size = lax.axis_size("ctx")
        self.from_left, self.from_right = [], []
        self.send(block, block)

    def send(self, right, left):
        step = len(self.from_left)
        self.from_left.append(lax.ppermute(right, "ctx", [(i, i + 1) for i in range(step, self.size - 1)]))
        self.from_right.append(
            lax.ppermute(left, "ctx", [(i + 1, i) for i in range(self.size - 1 - step)])
        )

    def step(self):
        came = [self.from_left[-1], self.from_right[-1]]
        self.send(
            *copies(
                "pass_on", came, lambda _, ins, outs: list(zip(ins, outs)),
                [shape(c.shape, c.dtype) for c in came],
                in_specs=[whole(c.shape) for c in came], out_specs=[whole(c.shape) for c in came],
            )
        )

    def finish(self):
        while len(self.from_left) < self.size - 1:
            self.step()


class Everywhere:
    def __init__(self, x):
        self.left = [("dp", bit) for bit in bits_of(lax.axis_size("dp"))]
        self.left += [("ctx", bit) for bit in bits_of(lax.axis_size("ctx"))]
        self.total = x
        self.came = swap(x, *self.left.pop(0))

    def step(self):
        def body(a_ref, b_ref, out_ref):
            out_ref[...] = a_ref[...] + b_ref[...]

        self.total = call(
            "add_small", body, [self.total, self.came], [IN_VMEM] * 2, [IN_VMEM],
            [shape(self.total.shape, F32)],
        )[0]
        if self.left:
            self.came = swap(self.total, *self.left.pop(0))
            return True
        return False

    def finish(self):
        while self.step():
            pass
        return self.total


def on_device(
    tokens, doc_starts, attn_gain, w_query, w_key, w_value, w_out,
    query_gain, key_gain, mlp_gain, w_gate, w_up, w_down, cotangent,
):
    ORDER.clear()
    rows, width = tokens.shape[1], tokens.shape[2]
    stretch = rows // 2
    ctx_size = lax.axis_size("ctx")
    dp_size = lax.axis_size("dp")
    ctx_at = lax.axis_index("ctx")
    dp_at = lax.axis_index("dp")
    pack_rows = rows * ctx_size
    unit = width // dp_size
    inner = HEADS * HEAD_DIM
    own_tokens = tokens[0]
    grad_out = cotangent[0]
    starts = doc_starts[0]
    odd = (ctx_at % 2).astype(jnp.int32)[None]
    dp_bits = bits_of(dp_size)

    gains = jnp.concatenate(
        [attn_gain[:, None], mlp_gain[:, None], jnp.zeros((unit, HEAD_DIM - 2), BF16)], axis=1
    )

    def packing(_, ins, outs):
        at = 0
        for ref in ins:
            yield ref.at[:, :], outs[0].at[:, pl.ds(at, ref.shape[1])]
            at += ref.shape[1]

    def stacking(_, ins, outs):
        down, gate, up, out = ins
        stack_ref = outs[0]
        yield down.at[:, :], stack_ref.at[pl.ds(0, 3 * unit)]
        for i in range(3):
            cols = pl.ds(i * width, width)
            yield gate.at[:, cols], stack_ref.at[pl.ds((3 + i) * unit, unit)]
            yield up.at[:, cols], stack_ref.at[pl.ds((6 + i) * unit, unit)]
        yield out.at[:, :], stack_ref.at[pl.ds(9 * unit, 2 * unit)]

    attn_cols = inner + 2 * width + HEAD_DIM
    own_attn = copies(
        "pack_attn", [w_query, w_key, w_value, gains], packing, [shape((unit, attn_cols), BF16)],
        in_specs=[whole(w.shape) for w in (w_query, w_key, w_value)] + [IN_VMEM],
    )[0]
    pieces, first_pieces = gather_pieces(own_attn, inner)
    gathered = Relay(own_tokens)
    stack_in = copies(
        "pack_stack", [w_down, w_gate, w_up, w_out], stacking, [shape((11 * unit, width), BF16)],
        in_specs=[whole(w.shape) for w in (w_down, w_gate, w_up, w_out)],
        out_specs=[whole((11 * unit, width))],
    )[0]
    stack = lax.all_gather(stack_in, "dp", axis=0)
    gathered.step()
    touch(first_pieces)
    gathered.finish()
    from_left, from_right = gathered.from_left, gathered.from_right

    place_at = jnp.arange(pack_rows, dtype=jnp.int32)
    in_half = place_at % (pack_rows // 2)
    part, device, row = place_at // (pack_rows // 2), in_half // stretch, place_at % stretch
    key_stream = stream_index(device * rows + part * stretch + row, stretch, ctx_size)
    query_stream = stream_index(
        ctx_at * rows + jnp.arange(rows, dtype=jnp.int32), stretch, ctx_size
    )
    key_open = opening_of(key_stream, starts)
    query_open = opening_of(query_stream, starts)
    cos_pack, sin_pack = rotary(key_stream - key_open)
    cos_own, sin_own = rotary(query_stream - query_open)

    owners = (dp_at ^ jnp.arange(dp_size, dtype=jnp.int32)).astype(jnp.int32)
    listed = [(k, span, piece) for k in range(dp_size) for span, piece in pieces[k]]

    def assembling(prefetch, ins, outs):
        for (k, span, _), ref in zip(listed, ins):
            at = pl.multiple_of(prefetch[0][k] * unit, unit)
            cols = pl.ds(span.start, span.stop - span.start)
            yield ref.at[:, :], outs[0].at[pl.ds(at, unit), cols]
            if span.stop == attn_cols:
                last = ref.shape[1] - HEAD_DIM
                yield ref.at[:, pl.ds(last, HEAD_DIM)], outs[1].at[pl.ds(at, unit), :]

    attn_w, gain_cols = copies(
        "assemble_weights", [piece for _, _, piece in listed], assembling,
        [shape((width, attn_cols), BF16), shape((width, HEAD_DIM), BF16)], prefetch=[owners],
        out_specs=[whole((width, attn_cols)), IN_VMEM],
    )
    gain_rows = gain_cols[:, :2].astype(F32).T
    gain_attn, gain_mlp = gain_rows[0:1], gain_rows[1:2]
    gain_query = query_gain.astype(F32)[None, :]
    gain_key = key_gain.astype(F32)[None, :]

    normed = norm_own(own_tokens, gain_attn)
    query_raw, queries, factors = project_queries(normed, attn_w, gain_query, cos_own, sin_own)
    places = ((ctx_at - jnp.arange(ctx_size, dtype=jnp.int32)) % ctx_size).astype(jnp.int32)
    normed_pack = norm_pack(
        own_tokens, from_left, from_right, gain_attn, places, ctx_at.astype(jnp.int32)[None]
    ).reshape(pack_rows, width)
    key_raw, keys, values = project_keys_values(normed_pack, attn_w, gain_key, cos_pack, sin_pack)
    mixed, lse = attend(
        queries, keys, values, query_open[:, None], query_stream[:, None], key_stream[None, :]
    )
    (
        output, normed_mid, hidden, d_both, grad_middle, grad_branch, mlp_part, grad_mixed, parcel,
    ) = middle_block(mixed, lse, factors, own_tokens, grad_out, gain_mlp, stack)

    order = [2 * k for k in range(dp_size // 2)] + [2 * k + 1 for k in range(dp_size // 2)]
    owners = (dp_at ^ jnp.array(order, jnp.int32)).astype(jnp.int32)
    everything = slice(None)
    ctx_steps = len(bits_of(ctx_size))
    later_dp, later_ctx = len(dp_bits) - 2, ctx_steps - 1

    def two_rows(total, half, widths=(width,)):
        cuts, at = [], 0
        for which, each in enumerate(widths):
            for k in range(2):
                to = (slice(k * half, (k + 1) * half), everything)
                cuts.append((0, k, (everything, slice(at, at + each)), which, to))
            at += each
        return place([total.total], odd, [(2 * half, each) for each in widths], cuts)

    def halves_of(pair):
        half = pair[0].shape[1] // 2
        return Sum(pair[:1], pair[1:], [(0, half), (half, half)], odd), half

    half_heads = KV_HEADS // 2
    parcels = Relay(parcel)
    wide_grad = weight_grad(normed_mid, d_both, block=1024)[0]
    wide_grad = lax.psum_scatter(wide_grad, "dp", scatter_dimension=0, tiled=True)
    query_args = (
        queries, grad_mixed, mixed, keys, values, lse, query_open[:, None], query_stream[:, None],
        key_stream[None, :], query_raw, gain_query, cos_own, sin_own,
    )
    d_query, query_part = query_back(*query_args, 0, half_heads)
    out_kept, out_sent = weight_grad(mixed, grad_branch, owners, beside=True)

    parcels.step()

    d_query, query_more = query_back(*query_args, half_heads, half_heads, (d_query,))

    parcels.finish()
    query_kept, query_sent = weight_grad(normed, d_query, owners)
    outer = Sum([out_kept, query_kept], [out_sent, query_sent], [(0, unit), (0, unit)], odd)

    every_query = all_queries(normed_pack, attn_w, gain_query, cos_pack, sin_pack)

    touch([parcels.from_left[-1], parcels.from_right[-1]])
    outer.over_dp()
    wide_grad = copies(
        "take", [wide_grad], lambda _, ins, outs: [(ins[0], outs[0])], [shape(wide_grad.shape, BF16)]
    )[0]
    wide = Line(wide_grad)

    parcels = [parcel] + parcels.from_left + parcels.from_right
    grad_mixed_pack, far = all_grad_mixed(
        grad_mixed, parcels, stack, places, ctx_at.astype(jnp.int32)[None], rows
    )
    grad_mixed_pack = grad_mixed_pack.reshape(pack_rows, inner)
    far = far.transpose(2, 0, 1, 3).reshape(3 * HEADS, pack_rows)
    key_args = (
        every_query, grad_mixed_pack, keys, values, far,
        key_open[None, :], key_stream[None, :], query_stream[:, None],
        key_raw, gain_key, cos_own, sin_own, ctx_at.astype(jnp.int32)[None], ctx_size,
    )
    d_pair, key_part = key_back(*key_args, 0, half_heads)

    for _ in range(later_dp):
        outer.over_dp()
    wide.step()
    down_grad = weight_grad(hidden, grad_out, block=256)[0]
    down_grad = lax.psum_scatter(down_grad, "dp", scatter_dimension=0, tiled=True)

    d_pair, key_more = key_back(*key_args, half_heads, half_heads, (d_pair,))
    query_part, key_part = query_part + query_more, key_part + key_more

    outer = Line(outer.joined())
    key_kept, key_sent, value_kept, value_sent = weight_grad(normed, d_pair, owners, apart=True)
    pair = Sum([key_kept, value_kept], [key_sent, value_sent], [(0, unit), (0, unit)], odd)

    d_normed = normed_back(d_query, d_pair, attn_w)
    input_grad, attn_part = input_back(d_normed, own_tokens, gain_attn, grad_middle)

    wide.finish()
    pair.over_dp()
    small = Everywhere(
        jnp.concatenate([attn_part, mlp_part, query_part, key_part], axis=1).reshape(-1, HEAD_DIM)
    )
    small.step()

    for _ in range(later_dp):
        pair.over_dp()
    outer.step()
    small.step()

    pair.to_ctx()
    down_grad = copies(
        "take", [down_grad], lambda _, ins, outs: [(ins[0], outs[0])], [shape(down_grad.shape, BF16)],
        in_specs=[whole(down_grad.shape)], out_specs=[whole(down_grad.shape)],
    )[0]
    down_sum = lax.psum(down_grad, "ctx")
    small.step()
    gate_grad, up_grad = wide.place(
        [(unit, 3 * width)] * 2,
        [((everything, slice(k * 3 * width, (k + 1) * 3 * width)), k, everything) for k in range(2)],
    )

    pair.over_ctx()
    small.step()
    outer.finish()
    touch([down_sum])

    for _ in range(later_ctx):
        pair.over_ctx()
    small = small.finish().reshape(-1)
    near, far_half = slice(0, width), slice(width, 2 * width)
    first, second = slice(0, unit), slice(unit, 2 * unit)
    w_out_grad, query_grad = outer.place(
        [(2 * unit, width), (unit, inner)],
        [
            ((first, near), 0, (first, everything)),
            ((first, far_half), 0, (second, everything)),
            ((second, everything), 1, everything),
        ],
    )
    down_grad = down_sum.astype(F32)
    key_grad, value_grad = place(
        [pair.total], odd, [(unit, width)] * 2, [(0, k, everything, k, everything) for k in range(2)]
    )

    attn_gain_grad = lax.dynamic_slice(small, (dp_at * unit,), (unit,))
    mlp_gain_grad = lax.dynamic_slice(small, (width + dp_at * unit,), (unit,))
    query_gain_grad = small[2 * width : 2 * width + HEAD_DIM]
    key_gain_grad = small[2 * width + HEAD_DIM :]
    return (
        output[None], input_grad[None], attn_gain_grad, query_grad, key_grad, value_grad, w_out_grad,
        query_gain_grad, key_gain_grad, mlp_gain_grad, gate_grad, up_grad, down_grad,
    )


def solution(mesh):
    in_specs = (
        P("dp", "ctx", None),
        P("dp", None),
        P("dp"),
        P("dp", None),
        P("dp", None),
        P("dp", None),
        P("dp", None),
        P(),
        P(),
        P("dp"),
        P("dp", None),
        P("dp", None),
        P("dp", None),
        P("dp", "ctx", None),
    )
    out_specs = (
        P("dp", "ctx", None),
        P("dp", "ctx", None),
        P("dp"),
        P("dp", None),
        P("dp", None),
        P("dp", None),
        P("dp", None),
        P(),
        P(),
        P("dp"),
        P("dp", None),
        P("dp", None),
        P("dp", None),
    )
    return jax.shard_map(
        on_device, mesh=mesh, in_specs=in_specs, out_specs=out_specs, check_vma=False
    )
```
